128 devices in a mesh: roll: 8 (over y, core), fsdp: 16 (over x, z).
Axes of the slice: x: 4, y: 4, z: 4, core: 2. Of those that a mesh axis runs over, the one named last changes fastest.
Arguments:
- latents: bfloat16 [256, 80, 2432], P(('roll', 'fsdp')), may hold values from -6 to 6
- stale_velocity: bfloat16 [256, 80, 2432], P(('roll', 'fsdp')), may hold values from -6 to 6
- noise: bfloat16 [256, 80, 2432], P(('roll', 'fsdp')), may hold values from -6 to 6
- modulation: float32 [256, 3, 2432], P(('roll', 'fsdp')), may hold values from -3 to 3
- step_ratio: float32 [256], P(('roll', 'fsdp')), may hold values from 0.003 to 0.03
- rewards: float32 [256], P(('roll', 'fsdp')), may hold values from 0 to 1
- group_ids: int32 [256], P(('roll', 'fsdp')), may hold values from 0 to 11
- step_index: int32 [256], P(('roll', 'fsdp')), may hold values from 0 to 9
- valid_steps: int32 [256], P(('roll', 'fsdp')), may hold values from 1 to 10
- patch_mask: int32 [256, 80], P(('roll', 'fsdp')), may hold values 0 or 1
- params: float32 [2, 2432, 5120], P(None, 'fsdp', 'roll'), may hold values from -0.125 to 0.125
- first_moment: float32 [2, 2432, 5120], P(None, 'fsdp', 'roll'), may hold values from -6e-05 to 6e-05
- second_moment: float32 [2, 2432, 5120], P(None, 'fsdp', 'roll'), may hold values from 1e-11 to 1e-09
Outputs:
- new_params: float32 [2, 2432, 5120], P(None, 'fsdp', 'roll')
- new_first: float32 [2, 2432, 5120], P(None, 'fsdp', 'roll')
- new_second: float32 [2, 2432, 5120], P(None, 'fsdp', 'roll')
- rollout_weights: bfloat16 [2, 2432, 5120], P(None, 'fsdp')
The draws below stay inside these ranges and needn't reach their ends.
All inputs are finite; a program needn't handle non-finite values. No bound on the sum of `patch_mask` on one device may be relied on, other than what follows from the above.
Results may differ from the reference program's by a relative error of at most 0.004.
Values may be sent and summed in bfloat16 or wider, within the bound.
A program may use at most 128 MiB of HBM per device.

```python
import math
import jax
import jax.numpy as jnp
from jax import lax

D = 2432
FFW = 5120
PATCH = 80
STEPS = 10
GROUPS = 12
SAMPLES = 256


def touch_ends(values, stream_key, least, top_value):
    extent = values.shape
    index_at = [jax.random.randint(jax.random.fold_in(stream_key, axis), (), 0, extent[axis]) for axis in range(len(extent))]
    values = values.at[tuple(index_at)].set(least)
    longest = extent.index(max(extent))
    index_at[longest] = (index_at[longest] + 1) % extent[longest]
    return values.at[tuple(index_at)].set(top_value)


def steps_of(rng, dims, shards, smallest, high):
    gain, own = 1.0, jax.random.fold_in(rng, 6)
    for axis_at, shards_of in shards:
        draws = jnp.exp(jax.random.uniform(jax.random.fold_in(own, axis_at), (shards_of,), jnp.float32, smallest / len(shards), high / len(shards)))
        gain = gain * jnp.repeat(draws, dims[axis_at] // shards_of).reshape([-1 if axis == axis_at else 1 for axis in range(len(dims))])
    return gain


def scatter_about(stream_key, dims, deviation, bound, pieces=(), kind=jnp.bfloat16):
    gain = steps_of(stream_key, dims, pieces, -0.22, 0.18) if pieces else 1.0
    result = jax.random.normal(stream_key, dims, jnp.float32) * deviation * gain
    return jnp.minimum(jnp.maximum(result, -bound), bound).astype(kind)


def setup_inputs(seed: int = 0) -> dict:
    seeds = jax.random.split(jax.random.key(seed), 14)
    return {
        "latents": scatter_about(seeds[0], (SAMPLES, PATCH, D), 1.0, 6.0, ((0, 128),)),
        "stale_velocity": scatter_about(seeds[1], (SAMPLES, PATCH, D), 1.0, 6.0, ((0, 128),)),
        "noise": scatter_about(seeds[2], (SAMPLES, PATCH, D), 1.0, 6.0, ((0, 128),)),
        "modulation": scatter_about(seeds[3], (SAMPLES, 3, D), 0.5, 3.0, ((0, 128),), jnp.float32),
        "step_ratio": jnp.clip(jnp.exp(math.log(0.03) - 2.3025851 * jax.random.uniform(seeds[4], (SAMPLES,), jnp.float32) ** steps_of(seeds[4], (SAMPLES,), ((0, 128),), -0.2, 0.2)), 0.003, 0.03),
        "rewards": jnp.clip(1.0 * jax.random.uniform(seeds[5], (SAMPLES,), jnp.float32) ** steps_of(seeds[5], (SAMPLES,), ((0, 128),), -0.2, 0.2), 0.0, 1.0),
        "group_ids": touch_ends(jax.random.randint(seeds[6], (SAMPLES,), 0, GROUPS), jax.random.fold_in(seeds[6], 1), 0, GROUPS - 1).astype(jnp.int32),
        "step_index": touch_ends(jax.random.randint(seeds[7], (SAMPLES,), 0, STEPS), jax.random.fold_in(seeds[7], 1), 0, STEPS - 1).astype(jnp.int32),
        "valid_steps": touch_ends(jax.random.randint(seeds[8], (SAMPLES,), 1, STEPS + 1), jax.random.fold_in(seeds[8], 1), 1, STEPS).astype(jnp.int32),
        "patch_mask": touch_ends((jax.random.randint(seeds[9], (SAMPLES, PATCH), 0, 4) < 3).astype(jnp.int32), jax.random.fold_in(seeds[9], 1), 0, 1),
        "params": scatter_about(seeds[10], (2, D, FFW), D ** -0.5, 0.125, ((1, 16), (2, 8)), jnp.float32),
        "first_moment": scatter_about(seeds[11], (2, D, FFW), (1e-5), 5.999999848427251e-05, ((1, 16), (2, 8)), jnp.float32),
        "second_moment": jnp.clip(jnp.exp(math.log(9.999999717180685e-10) - 4.6051702 * jax.random.uniform(seeds[12], (2, D, FFW), jnp.float32) ** steps_of(seeds[12], (2, D, FFW), ((1, 16), (2, 8)), -0.2, 0.2)), 9.999999960041972e-12, 9.999999717180685e-10),
    }


eps_norm = 1e-06
clip_low = 0.8
clip_high = 1.2
spread_floor = 0.25
beta_one = 0.9
beta_two = 0.999
learn_rate = 0.001
weight_decay = 0.01
adam_eps = 1e-08
adam_count = 100.0

def modulated(latents, modulation):
    values = latents.astype(jnp.float32)
    middle = lax.optimization_barrier(jnp.mean(values, axis=-1, keepdims=True))
    centred = values - middle
    spread = lax.optimization_barrier(jnp.mean(centred * centred, axis=-1, keepdims=True))
    normed = centred * lax.rsqrt(spread + eps_norm)
    shift = modulation[:, 0, :][:, None, :]
    scaling = modulation[:, 1, :][:, None, :]
    return (normed * (1.0 + scaling) + shift).astype(jnp.bfloat16)

def group_terms(rewards, group_ids, step_index, valid_steps):
    valid = (step_index < valid_steps).astype(jnp.float32)
    member = (group_ids[:, None] == jnp.arange(GROUPS, dtype=jnp.int32)[None, :]).astype(jnp.float32)
    weighted = member * valid[:, None]
    counts = lax.optimization_barrier(jnp.sum(weighted, axis=0))
    sums = lax.optimization_barrier(jnp.sum(weighted * rewards[:, None], axis=0))
    squares = lax.optimization_barrier(jnp.sum(weighted * (rewards * rewards)[:, None], axis=0))
    return (valid, counts, sums, squares, jnp.sum(valid))

def advantages(rewards, group_ids, counts, sums, squares):
    safe = jnp.maximum(counts, 1.0)
    middle = sums / safe
    variance = jnp.maximum(squares / safe - middle * middle, 0.0)
    spread = jnp.maximum(jnp.sqrt(variance), spread_floor)
    member = (group_ids[:, None] == jnp.arange(GROUPS, dtype=jnp.int32)[None, :]).astype(jnp.float32)
    own_mean = lax.optimization_barrier(jnp.sum(member * middle[None, :], axis=1))
    own_spread = lax.optimization_barrier(jnp.sum(member * spread[None, :], axis=1))
    return (rewards - own_mean) / own_spread

def velocity_grad(velocity, stale_velocity, noise, patch_mask, step_ratio, advantage, valid, total_valid):
    mask = patch_mask.astype(jnp.float32)
    npatch = jnp.maximum(lax.optimization_barrier(jnp.sum(mask, axis=1)), 1.0)
    factor = step_ratio[:, None, None]
    drawn = noise.astype(jnp.float32)
    err = drawn + factor * (stale_velocity.astype(jnp.float32) - velocity)
    logratio = lax.optimization_barrier(jnp.sum(mask[:, :, None] * (drawn * drawn - err * err), axis=(1, 2))) / (2.0 * npatch)
    ratio = jnp.exp(logratio)
    clipped = jnp.clip(ratio, clip_low, clip_high)
    active = (ratio * advantage <= clipped * advantage).astype(jnp.float32)
    coef = -valid * advantage * ratio * active / jnp.maximum(total_valid, 1.0)
    return (coef / npatch)[:, None, None] * mask[:, :, None] * factor * err

def adamw(params, first_moment, second_moment, grads):
    new_first = beta_one * first_moment + (1.0 - beta_one) * grads
    new_second = beta_two * second_moment + (1.0 - beta_two) * grads * grads
    first_hat = new_first / (1.0 - beta_one ** adam_count)
    second_hat = new_second / (1.0 - beta_two ** adam_count)
    update = first_hat / (jnp.sqrt(second_hat) + adam_eps) + weight_decay * params
    return (params - learn_rate * update, new_first, new_second)

def reference(latents, stale_velocity, noise, modulation, step_ratio, rewards, group_ids, step_index, valid_steps, patch_mask, params, first_moment, second_moment):
    samples, patch, width = latents.shape
    block = 16
    weights = params.astype(jnp.bfloat16)
    up_mat = weights[0]
    down_mat = weights[1]
    gate = 1.0 + modulation[:, 2, :]
    hidden_in = modulated(latents, modulation)
    blocks = hidden_in.reshape(samples // block, block * patch, width)
    contract_last = (((1,), (1,)), ((), ()))
    contract_first = (((0,), (0,)), ((), ()))

    def forward(carry, rows):
        pre = jnp.dot(rows, up_mat, preferred_element_type=jnp.float32)
        act = jax.nn.gelu(pre).astype(jnp.bfloat16)
        return (carry, lax.dot_general(act, down_mat, contract_last, preferred_element_type=jnp.float32))
    _, branch = lax.scan(forward, jnp.zeros((), jnp.float32), blocks)
    velocity = gate[:, None, :] * branch.reshape(samples, patch, width)
    valid, counts, sums, squares, total_valid = group_terms(rewards, group_ids, step_index, valid_steps)
    advantage = advantages(rewards, group_ids, counts, sums, squares)
    grad_velocity = velocity_grad(velocity, stale_velocity, noise, patch_mask, step_ratio, advantage, valid, total_valid)
    back = (gate[:, None, :] * grad_velocity).astype(jnp.bfloat16).reshape(samples // block, block * patch, width)

    def backward(total, pair):
        rows, back_rows = pair
        pre = jnp.dot(rows, up_mat, preferred_element_type=jnp.float32)
        act = jax.nn.gelu(pre).astype(jnp.bfloat16)
        grad_down = lax.dot_general(back_rows, act, contract_first, preferred_element_type=jnp.float32)
        back_act = jnp.dot(back_rows, down_mat, preferred_element_type=jnp.float32)
        _, pull = jax.vjp(jax.nn.gelu, pre)
        back_pre = pull(back_act)[0].astype(jnp.bfloat16)
        grad_up = lax.dot_general(rows, back_pre, contract_first, preferred_element_type=jnp.float32)
        return (total + jnp.stack([grad_up, grad_down], axis=0), None)
    grads, _ = lax.scan(backward, jnp.zeros(params.shape, jnp.float32), (blocks, back))
    new_params, new_first, new_second = adamw(params, first_moment, second_moment, grads)
    return (new_params, new_first, new_second, new_params.astype(jnp.bfloat16))
```

```python
import functools

import jax
import jax.numpy as jnp
from jax import lax
from jax.experimental import pallas as pl
from jax.experimental.pallas import tpu as pltpu
from jax.sharding import PartitionSpec as P

GROUPS = 12
D = 2432
BLOCK = 152
SLICE = 640
PATCH = 80
CHUNK = 16

eps_norm = 1e-06
clip_low = 0.8
clip_high = 1.2
spread_floor = 0.25
beta_one = 0.9
beta_two = 0.999
learn_rate = 0.001
weight_decay = 0.01
adam_eps = 1e-08
adam_count = 100.0

BF = jnp.bfloat16
F32 = jnp.float32
MESH = pl.DeviceIdType.MESH
TILES = ((0, 640), (640, 640), (1280, 640), (1920, 512))
COLS = (pl.ds(0, 1280), pl.ds(1280, 1152))
OUT_COLS = ((0, 384), (384, 256))
LAST = (((1,), (1,)), ((), ()))
FIRST = (((0,), (0,)), ((), ()))
N_COPIES = 180


def gelu_parts(pre):
    root = 0.7978845608028654
    square = pre * pre
    t = jnp.tanh(root * (pre + 0.044715 * (square * pre)))
    cdf = 0.5 * (1.0 + t)
    slope = cdf + pre * (0.5 * (1.0 - t * t)) * (root * (1.0 + (3.0 * 0.044715) * square))
    return pre * cdf, slope


def kernel(
    rewards,
    group_ids,
    step_index,
    valid_steps,
    step_ratio,
    mask_in,
    mod,
    lat_h,
    stale_h,
    noise_h,
    par_h,
    m1_h,
    m2_h,
    o_par,
    o_m1,
    o_m2,
    o_roll,
    hid,
    bk,
    raw0,
    raw1,
    asm_up,
    asm_down,
    pre,
    act,
    sib_recv,
    y_send,
    y_recv,
    own,
    grad,
    x_recv,
    grad_own,
    b_send,
    b_recv,
    lat,
    stale,
    noise,
    par,
    m1,
    m2,
    fresh,
    mask_col,
    stats,
    stats_recv,
    send_sem,
    recv_sem,
    local_sem,
):
    roll = lax.axis_index("roll")
    fsdp = lax.axis_index("fsdp")
    y, c = roll // 2, lax.rem(roll, 2)
    x, z = fsdp // 4, lax.rem(fsdp, 4)

    def turn(a, by):
        return lax.rem(a + by, 4)

    def at(x_, y_, z_, c_):
        return (y_ * 2 + c_, x_ * 4 + z_)

    y_ring = [at(x, turn(y, j), z, c) for j in range(4)]
    x_ring = [at(turn(x, j), y, z, c) for j in range(4)]
    z_ring = [at(x, y, turn(z, j), c) for j in range(4)]
    sibling = at(x, y, z, 1 - c)
    y_plus, y_minus = y_ring[1], y_ring[3]

    barrier = pltpu.get_barrier_semaphore()
    partners = y_ring[1:] + x_ring[1:] + z_ring[1:] + [sibling]
    for partner in partners:
        pl.semaphore_signal(barrier, inc=1, device_id=partner, device_id_type=MESH)

    count = [0]
    sent = []

    def push(src, dst, device, landed=None, keep=True):
        i = count[0]
        count[0] += 1
        copy = pltpu.make_async_remote_copy(
            src_ref=src,
            dst_ref=dst,
            send_sem=send_sem.at[i],
            recv_sem=recv_sem.at[i],
            device_id=device,
            device_id_type=MESH,
        )
        copy.start()
        if keep:
            sent.append(copy)
        if landed is None:
            return copy
        return pltpu.make_async_remote_copy(
            src_ref=landed,
            dst_ref=landed,
            send_sem=send_sem.at[i],
            recv_sem=recv_sem.at[i],
            device_id=device,
            device_id_type=MESH,
        )

    local = [0]

    def move(src, dst):
        i = local[0]
        local[0] += 1
        copy = pltpu.make_async_copy(src, dst, local_sem.at[i])
        copy.start()
        return copy

    par_in = move(par_h, par)
    lat_in = move(lat_h, lat)
    stale_in = move(stale_h, stale)
    noise_in = move(noise_h, noise)
    m1_in = move(m1_h, m1)
    m2_in = move(m2_h, m2)

    raws = (raw0, raw1)
    near = (x_ring, z_ring)
    far = (z_ring, x_ring)
    near_at = (x, z)
    far_at = (z, x)

    par_in.wait()
    for m in range(2):
        raw0[m, z, x] = par[m, 0:80, :].astype(BF)
        raw1[m, x, z, 0:72, :] = par[m, 80:BLOCK, :].astype(BF)
        raw1[m, x, z, 64:80, :] = jnp.concatenate(
            [par[m, 144:BLOCK, :], jnp.zeros((8, SLICE), F32)], axis=0
        ).astype(BF)

    def modulated(s):
        shift = mod[0, s : s + 1, :]
        scaling = 1.0 + mod[1, s : s + 1, :]

        def body(i, carry):
            rows = pl.ds(pl.multiple_of(i * CHUNK, CHUNK), CHUNK)
            values = lat[s, rows, :].astype(F32)
            middle = jnp.sum(values, axis=-1, keepdims=True) / D
            centred = values - middle
            spread = jnp.sum(centred * centred, axis=-1, keepdims=True) / D
            normed = centred * lax.rsqrt(spread + eps_norm)
            hid[s, 0, 0, rows, :] = (normed * scaling + shift).astype(BF)
            return carry

        lax.fori_loop(0, PATCH // CHUNK, body, 0)

    pl.semaphore_wait(barrier, len(partners))

    first = {}
    for m in range(2):
        for h in range(2):
            a, b = far_at[h], near_at[h]
            mine = raws[h].at[m, a, b]
            first[m, h, 0] = push(mine, mine, near[h][1], raws[h].at[m, a, turn(b, 3)])
            first[m, h, 1] = push(mine, mine, near[h][3], raws[h].at[m, a, turn(b, 1)])

    lat_in.wait()

    def gather_own(buf, s):
        mine = buf.at[s, 0, 0]
        left, right = buf.at[s, 0, 3], buf.at[s, 0, 1]
        lo, hi = COLS
        return {
            "left_lo": push(mine.at[:, lo], left.at[:, lo], y_plus),
            "right_hi": push(mine.at[:, hi], right.at[:, hi], y_minus),
            "left_hi": push(mine.at[:, hi], left.at[:, hi], y_plus),
            "right_lo": push(mine.at[:, lo], right.at[:, lo], y_minus),
            "sib0": push(mine, buf.at[s, 1, 0], sibling),
        }

    def gather_on(buf, s, d):
        left, right, across = buf.at[s, 0, 3], buf.at[s, 0, 1], buf.at[s, 0, 2]
        lo, hi = COLS
        d["left_lo"].wait_recv()
        d["across_lo"] = push(left.at[:, lo], across.at[:, lo], y_plus)
        d["right_hi"].wait_recv()
        d["across_hi"] = push(right.at[:, hi], across.at[:, hi], y_minus)

    def gather_near(buf, s, d):
        d["left_hi"].wait_recv()
        d["sib3"] = push(buf.at[s, 0, 3], buf.at[s, 1, 3], sibling)
        d["right_lo"].wait_recv()
        d["sib1"] = push(buf.at[s, 0, 1], buf.at[s, 1, 1], sibling)

    def gather_end(buf, s, d):
        d["across_lo"].wait_recv()
        d["across_hi"].wait_recv()
        d["sib2"] = push(buf.at[s, 0, 2], buf.at[s, 1, 2], sibling)

    def gather_sib(d):
        for j in range(4):
            d["sib%d" % j].wait_recv()

    modulated(0)
    rows0 = gather_own(hid, 0)
    modulated(1)

    lane = lax.broadcasted_iota(jnp.int32, (1, 128), 1)
    valid = [jnp.where(step_index[s] < valid_steps[s], 1.0, 0.0).astype(F32) for s in range(2)]
    member = [jnp.where(lane == group_ids[s], 1.0, 0.0).astype(F32) for s in range(2)]
    stats[...] = jnp.zeros((8, 128), F32)
    stats[0:1, :] = member[0] * valid[0] + member[1] * valid[1]
    stats[1:2, :] = member[0] * (valid[0] * rewards[0]) + member[1] * (valid[1] * rewards[1])
    stats[2:3, :] = member[0] * (valid[0] * (rewards[0] * rewards[0])) + member[1] * (
        valid[1] * (rewards[1] * rewards[1])
    )
    stats[3:4, :] = jnp.zeros((1, 128), F32) + (valid[0] + valid[1])

    def stats_send(step):
        ring = ([None, sibling], y_ring, x_ring, z_ring)[step]
        copies = []
        for j in range(1, len(ring)):
            slot = stats_recv.at[step, j]
            copies.append(push(stats, slot, ring[j], keep=False))
        return copies

    def stats_sum(step, copies):
        total = stats[...]
        for j, copy in enumerate(copies):
            copy.wait_recv()
            total = total + stats_recv[step, j + 1]
        for copy in copies:
            copy.wait_send()
        stats[...] = total

    stats_copies = stats_send(0)

    def pass_on(m):
        for h in range(2):
            a, b = far_at[h], near_at[h]
            got = (turn(b, 3), turn(b, 1))[m]
            step = (1, 3)[m]
            first[m, h, m].wait_recv()
            block = raws[h].at[m, a, got]
            first[m, h, 2] = push(block, block, near[h][step], raws[h].at[m, a, turn(b, 2)])

    second = {}

    def groups(m):
        for h in range(2):
            first[m, h, 1 - m].wait_recv()
            first[m, h, 2].wait_recv()
            a = far_at[h]
            lo, hi = (raws[h].at[m, a, pl.ds(k, 2)] for k in (0, 2))
            left, right = turn(a, 3), turn(a, 1)
            second[m, h, "left_lo"] = push(lo, lo, far[h][1], raws[h].at[m, left, pl.ds(0, 2)])
            second[m, h, "right_hi"] = push(hi, hi, far[h][3], raws[h].at[m, right, pl.ds(2, 2)])
            second[m, h, "left_hi"] = push(hi, hi, far[h][1], raws[h].at[m, left, pl.ds(2, 2)])
            second[m, h, "right_lo"] = push(lo, lo, far[h][3], raws[h].at[m, right, pl.ds(0, 2)])

    def groups_on(m):
        for h in range(2):
            a = far_at[h]
            left, right, across = turn(a, 3), turn(a, 1), turn(a, 2)
            second[m, h, "left_lo"].wait_recv()
            block = raws[h].at[m, left, pl.ds(0, 2)]
            second[m, h, "across_lo"] = push(
                block, block, far[h][1], raws[h].at[m, across, pl.ds(0, 2)]
            )
            second[m, h, "right_hi"].wait_recv()
            block = raws[h].at[m, right, pl.ds(2, 2)]
            second[m, h, "across_hi"] = push(
                block, block, far[h][3], raws[h].at[m, across, pl.ds(2, 2)]
            )

    def assemble(m, out):
        for h in range(2):
            for part in ("left_hi", "right_lo", "across_lo", "across_hi"):
                second[m, h, part].wait_recv()

        def body(i, carry):
            base = pl.multiple_of(i * (4 * BLOCK), CHUNK)
            parts = []
            for k in range(4):
                parts += [raw0[m, k, i], raw1[m, i, k, 0:72, :]]
            out[pl.ds(base, 4 * BLOCK), :] = jnp.concatenate(parts, axis=0)
            return carry

        lax.fori_loop(0, 4, body, 0)

    pass_on(0)
    pass_on(1)
    gather_on(hid, 0, rows0)
    groups(0)
    rows1 = gather_own(hid, 1)
    stats_sum(0, stats_copies)
    stats_copies = stats_send(1)
    gather_near(hid, 0, rows0)
    groups_on(0)
    groups(1)
    stats_sum(1, stats_copies)
    stats_copies = stats_send(2)
    gather_end(hid, 0, rows0)
    gather_on(hid, 1, rows1)
    stats_sum(2, stats_copies)
    stats_copies = stats_send(3)

    diag = lax.broadcasted_iota(jnp.int32, (PATCH, PATCH), 0) == lax.broadcasted_iota(
        jnp.int32, (PATCH, PATCH), 1
    )
    npatch = []
    for s in range(2):
        row = jnp.broadcast_to(mask_in[s : s + 1, :].astype(F32), (PATCH, PATCH))
        column = jnp.sum(jnp.where(diag, row, 0.0), axis=1, keepdims=True)
        mask_col[s] = jnp.broadcast_to(column, (PATCH, 128))
        npatch.append(jnp.maximum(jnp.sum(column, axis=0, keepdims=True), 1.0))

    stats_sum(3, stats_copies)

    def forward(s):
        def body(i, carry):
            rows = hid[s, i].reshape(4 * PATCH, D)
            value = jnp.dot(rows, asm_up[0:D, :], preferred_element_type=F32)
            pre[s, i] = value
            act[s, i] = gelu_parts(value)[0].astype(BF)
            return carry

        lax.fori_loop(0, 2, body, 0)

    assemble(0, asm_up)
    gather_sib(rows0)
    forward(0)
    gather_near(hid, 1, rows1)
    groups_on(1)
    gather_end(hid, 1, rows1)
    gather_sib(rows1)
    forward(1)
    assemble(1, asm_down)

    def branch_tile(s, i, n):
        start, width = TILES[n]
        return lax.dot_general(
            act[s, i], asm_down[start : start + width, :], LAST, preferred_element_type=F32
        )

    pair = {}

    def branch_away(s):
        for n, (start, width) in enumerate(TILES):
            slot = asm_up.at[pl.ds((s * 4 + n) * 320, 320)]
            slot[:, 0:width] = branch_tile(s, 1, n).astype(BF)
            pair[s, n] = push(slot, sib_recv.at[s, n], sibling)

    def branch_mine(s):
        for n, (start, width) in enumerate(TILES):
            value = branch_tile(s, 0, n)
            pair[s, n].wait_recv()
            value = value + sib_recv[s, n, :, 0:width].astype(F32)
            cols = slice(start, start + width)
            own[s, :, cols] = value[0:80]
            for j, k in ((2, 0), (1, 1), (3, 2)):
                y_send[s, k, :, cols] = value[j * 80 : j * 80 + 80].astype(BF)

    def ring_start(send, recv, parts, plus, minus):
        lo, hi = parts
        return {
            "across_hi": push(hi(send, 0), hi(recv, 0), plus),
            "across_lo": push(lo(send, 0), lo(recv, 0), minus),
            "plus_lo": push(lo(send, 1), lo(recv, 1), plus),
            "minus_hi": push(hi(send, 2), hi(recv, 2), minus),
        }

    def ring_add(send, recv, parts, plus, minus, add, d):
        lo, hi = parts
        d["across_hi"].wait_recv()
        add(hi(send, 1), hi(recv, 0))
        d["plus_hi"] = push(hi(send, 1), hi(recv, 1), plus)
        d["across_lo"].wait_recv()
        add(lo(send, 2), lo(recv, 0))
        d["minus_lo"] = push(lo(send, 2), lo(recv, 2), minus)

    def ring_wait(d):
        for part in ("plus_lo", "minus_hi", "plus_hi", "minus_lo"):
            d[part].wait_recv()

    def add_rows(dst, src):
        def body(i, carry):
            rows = pl.ds(pl.multiple_of(i * CHUNK, CHUNK), CHUNK)
            dst[rows, :] = (dst[rows, :].astype(F32) + src[rows, :].astype(F32)).astype(BF)
            return carry

        lax.fori_loop(0, dst.shape[0] // CHUNK, body, 0)

    def add_blocks(dst, src):
        for k in range(2):
            dst[k] = (dst[k].astype(F32) + src[k].astype(F32)).astype(BF)

    col_parts = tuple((lambda ref, k, cols=cols: ref.at[k, :, cols]) for cols in COLS)
    block_parts = tuple((lambda ref, k, i=i: ref.at[k, pl.ds(i, 2)]) for i in (0, 2))
    row_parts = tuple((lambda ref, k, r=r: ref.at[k, pl.ds(*r)]) for r in ((0, 48), (48, 32)))

    def branch_ring(s):
        return ring_start(y_send.at[s], y_recv.at[s], col_parts, y_plus, y_minus)

    def branch_add(s, d):
        ring_add(y_send.at[s], y_recv.at[s], col_parts, y_plus, y_minus, add_rows, d)

    def back_rows(s, d):
        ring_wait(d)
        gate = 1.0 + mod[2, s : s + 1, :]
        factor = step_ratio[s]

        def err_body(i, total):
            rows = pl.ds(pl.multiple_of(i * CHUNK, CHUNK), CHUNK)
            branch = (
                own[s, rows, :] + y_recv[s, 1, rows, :].astype(F32) + y_recv[s, 2, rows, :].astype(F32)
            )
            velocity = gate * branch
            drawn = noise[s, rows, :].astype(F32)
            err = drawn + factor * (stale[s, rows, :].astype(F32) - velocity)
            own[s, rows, :] = err
            gap = jnp.sum(drawn * drawn - err * err, axis=1, keepdims=True)
            return total + mask_col[s, rows, 0:1] * gap

        gaps = lax.fori_loop(0, PATCH // CHUNK, err_body, jnp.zeros((CHUNK, 1), F32))
        logratio = jnp.sum(gaps, axis=0, keepdims=True) / (2.0 * npatch[s])
        safe = jnp.maximum(stats[0:1, :], 1.0)
        middle = stats[1:2, :] / safe
        variance = jnp.maximum(stats[2:3, :] / safe - middle * middle, 0.0)
        spread = jnp.maximum(jnp.sqrt(variance), spread_floor)
        own_mean = jnp.sum(member[s] * middle, axis=1, keepdims=True)
        own_spread = jnp.sum(member[s] * spread, axis=1, keepdims=True)
        advantage = (rewards[s] - own_mean) / own_spread
        ratio = jnp.exp(logratio)
        clipped = jnp.clip(ratio, clip_low, clip_high)
        active = jnp.where(ratio * advantage <= clipped * advantage, 1.0, 0.0).astype(F32)
        coef = -valid[s] * advantage * ratio * active / jnp.maximum(stats[3:4, 0:1], 1.0)
        per_patch = coef / npatch[s]

        def back_body(i, carry):
            rows = pl.ds(pl.multiple_of(i * CHUNK, CHUNK), CHUNK)
            scale = per_patch * mask_col[s, rows, 0:1] * factor
            bk[s, 0, 0, rows, :] = (gate * (scale * own[s, rows, :])).astype(BF)
            return carry

        lax.fori_loop(0, PATCH // CHUNK, back_body, 0)

    branch_away(0)
    branch_mine(0)
    ring0 = branch_ring(0)
    branch_away(1)
    branch_mine(1)
    branch_add(0, ring0)
    ring1 = branch_ring(1)
    stale_in.wait()
    noise_in.wait()
    back_rows(0, ring0)
    branch_add(1, ring1)
    back0 = gather_own(bk, 0)
    back_rows(1, ring1)
    gather_on(bk, 0, back0)
    back1 = gather_own(bk, 1)
    gather_near(bk, 0, back0)
    gather_end(bk, 0, back0)
    gather_sib(back0)

    def back_pre(s):
        def body(i, carry):
            rows = bk[s, i].reshape(4 * PATCH, D)
            value = jnp.dot(rows, asm_down[...], preferred_element_type=F32)
            act[s, i] = (value * gelu_parts(pre[s, i])[1]).astype(BF)
            return carry

        lax.fori_loop(0, 2, body, 0)

    def grad_tile(rows, s, n):
        start, width = TILES[n]
        left = rows[s, :, :, :, start : start + width].reshape(8 * PATCH, width)
        right = act[s].reshape(8 * PATCH, SLICE)
        return lax.dot_general(left, right, FIRST, preferred_element_type=F32)

    def grad_rows(h, j, k):
        a, b = turn(far_at[h], j), turn(near_at[h], k)
        block = (b * 4 + a) if h == 0 else (a * 4 + b)
        return grad[pl.ds(pl.multiple_of(block * BLOCK + 80 * h, 8), 80), :]

    def far_start(m):
        for j, slot in ((2, 0), (1, 1), (3, 2)):
            for h in range(2):
                for k in range(4):
                    raws[h][m, slot, k] = grad_rows(h, j, k).astype(BF)
        out = [
            ring_start(raws[h].at[m], x_recv.at[m, h], block_parts, far[h][1], far[h][3])
            for h in range(2)
        ]
        for h in range(2):
            for k in range(4):
                grad_own[m, h, k] = grad_rows(h, 0, k)
        return out

    def far_add(m, d):
        for h in range(2):
            ring_add(
                raws[h].at[m],
                x_recv.at[m, h],
                block_parts,
                far[h][1],
                far[h][3],
                add_blocks,
                d[h],
            )

    def near_start(m, d):
        out = []
        for h in range(2):
            ring_wait(d[h])
            for k in (2, 1, 3, 0):
                total = (
                    grad_own[m, h, k] + x_recv[m, h, 1, k].astype(F32) + x_recv[m, h, 2, k].astype(F32)
                )
                if k == 0:
                    grad_own[m, h, 0] = total
                else:
                    b_send[m, h, {2: 0, 1: 1, 3: 2}[k]] = total.astype(BF)
            out.append(
                ring_start(b_send.at[m, h], b_recv.at[m, h], row_parts, near[h][1], near[h][3])
            )
        return out

    def near_add(m, d):
        for h in range(2):
            ring_add(
                b_send.at[m, h],
                b_recv.at[m, h],
                row_parts,
                near[h][1],
                near[h][3],
                add_rows,
                d[h],
            )

    def out_cols(owner, start, width):
        return pl.ds(pl.multiple_of(owner * SLICE + start, 128), width)

    out_copies = []

    def update(m, d):
        for h in range(2):
            ring_wait(d[h])
            rows = slice(0, 80) if h == 0 else slice(80, BLOCK)
            high = 80 if h == 0 else 72
            grads = (
                grad_own[m, h, 0, 0:high, :]
                + b_recv[m, h, 1, 0:high, :].astype(F32)
                + b_recv[m, h, 2, 0:high, :].astype(F32)
            )
            weights = par[m, rows, :]
            new_first = beta_one * m1[m, rows, :] + (1.0 - beta_one) * grads
            new_second = beta_two * m2[m, rows, :] + (1.0 - beta_two) * grads * grads
            first_hat = new_first / (1.0 - beta_one**adam_count)
            second_hat = new_second / (1.0 - beta_two**adam_count)
            step = first_hat / (jnp.sqrt(second_hat) + adam_eps) + weight_decay * weights
            new_weights = weights - learn_rate * step
            m1[m, rows, :] = new_first
            m2[m, rows, :] = new_second
            par[m, rows, :] = new_weights
            fresh[m, rows, :] = new_weights.astype(BF)
        d = {}
        place = o_roll.at[m, :, out_cols(roll, 0, SLICE)]
        left = o_roll.at[m, :, out_cols(turn(y, 3) * 2 + c, 0, SLICE)]
        right = o_roll.at[m, :, out_cols(turn(y, 1) * 2 + c, 0, SLICE)]
        d["left"] = push(fresh.at[m], place, y_plus, left)
        d["right"] = push(fresh.at[m], place, y_minus, right)
        other = o_roll.at[m, :, out_cols(y * 2 + 1 - c, 0, SLICE)]
        d["sib0"] = push(fresh.at[m], place, sibling, other)
        out_copies.append(move(fresh.at[m], place))
        out_copies.append(move(m1.at[m], o_m1.at[m]))
        out_copies.append(move(m2.at[m], o_m2.at[m]))
        out_copies.append(move(par.at[m], o_par.at[m]))
        return d

    def out_on(m, d):
        across = turn(y, 2)
        for key, by, to, half in (("left", 3, y_plus, 0), ("right", 1, y_minus, 1)):
            owner = turn(y, by)
            d[key].wait_recv()
            start, width = OUT_COLS[half]
            block = o_roll.at[m, :, out_cols(owner * 2 + c, start, width)]
            landed = o_roll.at[m, :, out_cols(across * 2 + c, start, width)]
            d[key, "across"] = push(block, block, to, landed)
            whole = o_roll.at[m, :, out_cols(owner * 2 + c, 0, SLICE)]
            twin = o_roll.at[m, :, out_cols(owner * 2 + 1 - c, 0, SLICE)]
            d[key, "sib"] = push(whole, whole, sibling, twin)

    def out_end(m, d):
        across = turn(y, 2)
        d["left", "across"].wait_recv()
        d["right", "across"].wait_recv()
        whole = o_roll.at[m, :, out_cols(across * 2 + c, 0, SLICE)]
        twin = o_roll.at[m, :, out_cols(across * 2 + 1 - c, 0, SLICE)]
        d["sib2"] = push(whole, whole, sibling, twin)

    def out_sib(d):
        d["sib0"].wait_recv()
        d["left", "sib"].wait_recv()
        d["right", "sib"].wait_recv()
        d["sib2"].wait_recv()

    for copy in sent:
        copy.wait_send()
    sent.clear()
    grad[pl.ds(D, 8), :] = jnp.zeros((8, SLICE), F32)

    for n, (start, width) in enumerate(TILES):
        grad[start : start + width, :] = grad_tile(bk, 0, n)
    gather_on(bk, 1, back1)
    back_pre(0)
    gather_near(bk, 1, back1)
    gather_end(bk, 1, back1)
    gather_sib(back1)
    for n, (start, width) in enumerate(TILES):
        grad[start : start + width, :] += grad_tile(bk, 1, n)
    down_far = far_start(1)
    back_pre(1)
    far_add(1, down_far)
    for n, (start, width) in enumerate(TILES):
        grad[start : start + width, :] = grad_tile(hid, 0, n) + grad_tile(hid, 1, n)
    up_far = far_start(0)
    m1_in.wait()
    m2_in.wait()
    down_near = near_start(1, down_far)
    far_add(0, up_far)
    near_add(1, down_near)
    down_out = update(1, down_near)
    out_on(1, down_out)
    up_near = near_start(0, up_far)
    near_add(0, up_near)
    out_end(1, down_out)
    up_out = update(0, up_near)
    out_on(0, up_out)
    out_sib(down_out)
    out_end(0, up_out)
    out_sib(up_out)
    for copy in out_copies:
        copy.wait()
    for copy in sent:
        copy.wait_send()


def per_device(
    latents,
    stale_velocity,
    noise,
    modulation,
    step_ratio,
    rewards,
    group_ids,
    step_index,
    valid_steps,
    patch_mask,
    params,
    first_moment,
    second_moment,
):
    any_ = pl.BlockSpec(memory_space=pl.ANY)
    smem = pl.BlockSpec(memory_space=pltpu.SMEM)
    vmem = pl.BlockSpec(memory_space=pltpu.VMEM)
    shard = jax.ShapeDtypeStruct(params.shape, F32)
    outs = pl.pallas_call(
        kernel,
        out_shape=(shard, shard, shard, jax.ShapeDtypeStruct((2, BLOCK, 8 * SLICE), BF)),
        in_specs=[smem] * 5 + [vmem] * 2 + [any_] * 6,
        out_specs=(any_,) * 4,
        scratch_shapes=[
            pltpu.VMEM((2, 2, 4, PATCH, D), BF),
            pltpu.VMEM((2, 2, 4, PATCH, D), BF),
            pltpu.VMEM((2, 4, 4, 80, SLICE), BF),
            pltpu.VMEM((2, 4, 4, 80, SLICE), BF),
            pltpu.VMEM((2560, SLICE), BF),
            pltpu.VMEM((D, SLICE), BF),
            pltpu.VMEM((2, 2, 4 * PATCH, SLICE), F32),
            pltpu.VMEM((2, 2, 4 * PATCH, SLICE), BF),
            pltpu.VMEM((2, 4, 4 * PATCH, SLICE), BF),
            pltpu.VMEM((2, 3, PATCH, D), BF),
            pltpu.VMEM((2, 3, PATCH, D), BF),
            pltpu.VMEM((2, PATCH, D), F32),
            pltpu.VMEM((D + 8, SLICE), F32),
            pltpu.VMEM((2, 2, 3, 4, 80, SLICE), BF),
            pltpu.VMEM((2, 2, 4, 80, SLICE), F32),
            pltpu.VMEM((2, 2, 3, 80, SLICE), BF),
            pltpu.VMEM((2, 2, 3, 80, SLICE), BF),
            pltpu.VMEM((2, PATCH, D), BF),
            pltpu.VMEM((2, PATCH, D), BF),
            pltpu.VMEM((2, PATCH, D), BF),
            pltpu.VMEM((2, BLOCK, SLICE), F32),
            pltpu.VMEM((2, BLOCK, SLICE), F32),
            pltpu.VMEM((2, BLOCK, SLICE), F32),
            pltpu.VMEM((2, BLOCK, SLICE), BF),
            pltpu.VMEM((2, PATCH, 128), F32),
            pltpu.VMEM((8, 128), F32),
            pltpu.VMEM((4, 4, 8, 128), F32),
            pltpu.SemaphoreType.DMA((N_COPIES,)),
            pltpu.SemaphoreType.DMA((N_COPIES,)),
            pltpu.SemaphoreType.DMA((16,)),
        ],
        compiler_params=pltpu.CompilerParams(
            collective_id=0, has_side_effects=True, vmem_limit_bytes=63 << 20
        ),
    )(
        rewards,
        group_ids,
        step_index,
        valid_steps,
        step_ratio,
        patch_mask,
        modulation.transpose(1, 0, 2),
        latents,
        stale_velocity,
        noise,
        params,
        first_moment,
        second_moment,
    )
    return tuple(outs)


def solution(mesh):
    rows = ("roll", "fsdp")
    weights = P(None, "fsdp", "roll")
    return jax.shard_map(
        per_device,
        mesh=mesh,
        in_specs=(
            P(rows, None, None),
            P(rows, None, None),
            P(rows, None, None),
            P(rows, None, None),
            P(rows),
            P(rows),
            P(rows),
            P(rows),
            P(rows),
            P(rows, None),
            weights,
            weights,
            weights,
        ),
        out_specs=(weights, weights, weights, P(None, "fsdp", None)),
        check_vma=False,
    )
```

```python
import functools

import jax
import jax.numpy as jnp
from jax import lax
from jax.experimental import pallas as pl
from jax.experimental.pallas import tpu as pltpu
from jax.sharding import PartitionSpec as P

GROUPS = 12
D = 2432
BLOCK = 152
SLICE = 640
PATCH = 80
CHUNK = 16

eps_norm = 1e-06
clip_low = 0.8
clip_high = 1.2
spread_floor = 0.25
beta_one = 0.9
beta_two = 0.999
learn_rate = 0.001
weight_decay = 0.01
adam_eps = 1e-08
adam_count = 100.0

BF = jnp.bfloat16
F32 = jnp.float32
MESH = pl.DeviceIdType.MESH
TILES = ((0, 640), (640, 640), (1280, 640), (1920, 512))
COLS = (pl.ds(0, 1280), pl.ds(1280, 1152))
OUT_COLS = ((0, 384), (384, 256))
LAST = (((1,), (1,)), ((), ()))
FIRST = (((0,), (0,)), ((), ()))
N_COPIES = 264


def gelu_parts(pre):
    root = 0.7978845608028654
    square = pre * pre
    t = jnp.tanh(root * (pre + 0.044715 * (square * pre)))
    cdf = 0.5 * (1.0 + t)
    slope = cdf + pre * (0.5 * (1.0 - t * t)) * (root * (1.0 + (3.0 * 0.044715) * square))
    return pre * cdf, slope


def kernel(
    rewards_h,
    group_ids_h,
    step_index_h,
    valid_steps_h,
    step_ratio_h,
    mask_h,
    mod_h,
    lat_h,
    stale_h,
    noise_h,
    par_h,
    m1_h,
    m2_h,
    o_par,
    o_m1,
    o_m2,
    o_roll,
    hid,
    bk,
    raw0,
    raw1,
    asm_up,
    asm_down,
    pre,
    act,
    sib_recv,
    y_send,
    y_recv,
    own,
    grad,
    x_recv,
    grad_own,
    b_send,
    b_recv,
    stale,
    noise,
    par,
    m1,
    m2,
    land,
    mask_col,
    stats,
    stats_recv,
    rewards,
    group_ids,
    step_index,
    valid_steps,
    step_ratio,
    mask_in,
    mod,
    send_sem,
    recv_sem,
    local_sem,
):
    roll = lax.axis_index("roll")
    fsdp = lax.axis_index("fsdp")
    y, c = roll // 2, lax.rem(roll, 2)
    x, z = fsdp // 4, lax.rem(fsdp, 4)

    def turn(a, by):
        return lax.rem(a + by, 4)

    def at(x_, y_, z_, c_):
        return (y_ * 2 + c_, x_ * 4 + z_)

    y_ring = [at(x, turn(y, j), z, c) for j in range(4)]
    x_ring = [at(turn(x, j), y, z, c) for j in range(4)]
    z_ring = [at(x, y, turn(z, j), c) for j in range(4)]
    sibling = at(x, y, z, 1 - c)
    y_plus, y_minus = y_ring[1], y_ring[3]

    barrier = pltpu.get_barrier_semaphore()
    partners = y_ring[1:] + x_ring[1:] + z_ring[1:] + [sibling]
    for partner in partners:
        pl.semaphore_signal(barrier, inc=1, device_id=partner, device_id_type=MESH)

    count = [0]
    sent = []

    def push(src, dst, device, landed=None, log=sent):
        i = count[0]
        count[0] += 1
        copy = pltpu.make_async_remote_copy(
            src_ref=src,
            dst_ref=dst,
            send_sem=send_sem.at[i],
            recv_sem=recv_sem.at[i],
            device_id=device,
            device_id_type=MESH,
        )
        copy.start()
        log.append(copy)
        if landed is None:
            return copy
        return pltpu.make_async_remote_copy(
            src_ref=landed,
            dst_ref=landed,
            send_sem=send_sem.at[i],
            recv_sem=recv_sem.at[i],
            device_id=device,
            device_id_type=MESH,
        )

    local = [0]

    def move(src, dst):
        i = local[0]
        local[0] += 1
        copy = pltpu.make_async_copy(src, dst, local_sem.at[i])
        copy.start()
        return copy

    par_in = move(par_h, par)
    lat_in = [move(lat_h.at[s], y_send.at[s, 0]) for s in range(2)] + [move(mod_h, mod)]
    small_in = [
        move(rewards_h, rewards),
        move(group_ids_h, group_ids),
        move(step_index_h, step_index),
        move(valid_steps_h, valid_steps),
        move(step_ratio_h, step_ratio),
        move(mask_h, mask_in),
    ]
    stale_in = move(stale_h, stale)
    noise_in = move(noise_h, noise)
    m1_in = move(m1_h, m1)
    m2_in = move(m2_h, m2)

    raws = (raw0, raw1)
    near = (x_ring, z_ring)
    far = (z_ring, x_ring)
    near_at = (x, z)
    far_at = (z, x)

    par_in.wait()
    for m in range(2):
        raw0[m, z, x] = par[m, 0:80, :].astype(BF)
        raw1[m, x, z, 0:72, :] = par[m, 80:BLOCK, :].astype(BF)
        raw1[m, x, z, 64:80, :] = jnp.concatenate(
            [par[m, 144:BLOCK, :], jnp.zeros((8, SLICE), F32)], axis=0
        ).astype(BF)

    def modulated(s):
        shift = mod[0, s : s + 1, :]
        scaling = 1.0 + mod[1, s : s + 1, :]

        def body(i, carry):
            rows = pl.ds(pl.multiple_of(i * CHUNK, CHUNK), CHUNK)
            values = y_send[s, 0, rows, :].astype(F32)
            middle = jnp.sum(values, axis=-1, keepdims=True) / D
            centred = values - middle
            spread = jnp.sum(centred * centred, axis=-1, keepdims=True) / D
            normed = centred * lax.rsqrt(spread + eps_norm)
            hid[s, 0, 0, rows, :] = (normed * scaling + shift).astype(BF)
            return carry

        lax.fori_loop(0, PATCH // CHUNK, body, 0)

    pl.semaphore_wait(barrier, len(partners))

    first, second, weights_sent = {}, {}, []

    def near_own(m):
        for h in range(2):
            a, b = far_at[h], near_at[h]
            mine = raws[h].at[m, a, b]
            for k in (3, 1):
                first[m, h, k] = push(
                    mine, mine, near[h][4 - k], raws[h].at[m, a, turn(b, k)], weights_sent
                )

    def near_on(m):
        k = (3, 1)[m]
        for h in range(2):
            a, b = far_at[h], near_at[h]
            first[m, h, k].wait_recv()
            block = raws[h].at[m, a, turn(b, k)]
            first[m, h, 2] = push(
                block, block, near[h][4 - k], raws[h].at[m, a, turn(b, 2)], weights_sent
            )
        for h in range(2):
            first[m, h, 4 - k].wait_recv()

    def far_own(m, k):
        for h in range(2):
            a, b = far_at[h], turn(near_at[h], k)
            if k == 2:
                first[m, h, 2].wait_recv()
            block = raws[h].at[m, a, b]
            for side in (3, 1):
                second[m, h, k, side] = push(
                    block, block, far[h][4 - side], raws[h].at[m, turn(a, side), b], weights_sent
                )

    def far_on(m, k):
        side = 3 if k < 2 else 1
        for h in range(2):
            a, b = far_at[h], turn(near_at[h], k)
            second[m, h, k, side].wait_recv()
            block = raws[h].at[m, turn(a, side), b]
            second[m, h, k, 2] = push(
                block, block, far[h][4 - side], raws[h].at[m, turn(a, 2), b], weights_sent
            )

    near_own(0)
    far_own(0, 0)
    near_own(1)
    far_own(1, 0)
    for copy in lat_in:
        copy.wait()

    def gather_own(buf, s):
        mine = buf.at[s, 0, 0]
        left, right = buf.at[s, 0, 3], buf.at[s, 0, 1]
        lo, hi = COLS
        return {
            "left_lo": push(mine.at[:, lo], left.at[:, lo], y_plus),
            "right_hi": push(mine.at[:, hi], right.at[:, hi], y_minus),
            "left_hi": push(mine.at[:, hi], left.at[:, hi], y_plus),
            "right_lo": push(mine.at[:, lo], right.at[:, lo], y_minus),
            "sib0": push(mine, buf.at[s, 1, 0], sibling),
        }

    def gather_on(buf, s, d):
        left, right, across = buf.at[s, 0, 3], buf.at[s, 0, 1], buf.at[s, 0, 2]
        lo, hi = COLS
        d["left_lo"].wait_recv()
        d["across_lo"] = push(left.at[:, lo], across.at[:, lo], y_plus)
        d["right_hi"].wait_recv()
        d["across_hi"] = push(right.at[:, hi], across.at[:, hi], y_minus)

    def gather_near(buf, s, d):
        d["left_hi"].wait_recv()
        d["sib3"] = push(buf.at[s, 0, 3], buf.at[s, 1, 3], sibling)
        d["right_lo"].wait_recv()
        d["sib1"] = push(buf.at[s, 0, 1], buf.at[s, 1, 1], sibling)

    def gather_end(buf, s, d):
        d["across_lo"].wait_recv()
        d["across_hi"].wait_recv()
        d["sib2"] = push(buf.at[s, 0, 2], buf.at[s, 1, 2], sibling)

    def gather_sib(d):
        for j in range(4):
            d["sib%d" % j].wait_recv()

    for copy in small_in:
        copy.wait()
    lane = lax.broadcasted_iota(jnp.int32, (1, 128), 1)
    valid = [jnp.where(step_index[s] < valid_steps[s], 1.0, 0.0).astype(F32) for s in range(2)]
    member = [jnp.where(lane == group_ids[s], 1.0, 0.0).astype(F32) for s in range(2)]
    stats[...] = jnp.zeros((8, 128), F32)
    stats[0:1, :] = member[0] * valid[0] + member[1] * valid[1]
    stats[1:2, :] = member[0] * (valid[0] * rewards[0]) + member[1] * (valid[1] * rewards[1])
    stats[2:3, :] = member[0] * (valid[0] * (rewards[0] * rewards[0])) + member[1] * (
        valid[1] * (rewards[1] * rewards[1])
    )
    stats[3:4, :] = jnp.zeros((1, 128), F32) + (valid[0] + valid[1])

    def stats_send(step):
        ring = ([None, sibling], y_ring, x_ring, z_ring)[step]
        copies = []
        for j in range(1, len(ring)):
            slot = stats_recv.at[step, j]
            copies.append(push(stats, slot, ring[j], log=[]))
        return copies

    def stats_sum(step, copies):
        total = stats[...]
        for j, copy in enumerate(copies):
            copy.wait_recv()
            total = total + stats_recv[step, j + 1]
        for copy in copies:
            copy.wait_send()
        stats[...] = total

    def assemble(m, out):
        for h in range(2):
            for k in range(4):
                second[m, h, k, 1 if k < 2 else 3].wait_recv()
                second[m, h, k, 2].wait_recv()

        def body(i, carry):
            base = pl.multiple_of(i * (4 * BLOCK), CHUNK)
            parts = []
            for k in range(4):
                parts += [raw0[m, k, i], raw1[m, i, k, 0:72, :]]
            out[pl.ds(base, 4 * BLOCK), :] = jnp.concatenate(parts, axis=0)
            return carry

        lax.fori_loop(0, 4, body, 0)

    diag = lax.broadcasted_iota(jnp.int32, (PATCH, PATCH), 0) == lax.broadcasted_iota(
        jnp.int32, (PATCH, PATCH), 1
    )
    npatch = []
    for s in range(2):
        row = jnp.broadcast_to(mask_in[s : s + 1, :].astype(F32), (PATCH, PATCH))
        column = jnp.sum(jnp.where(diag, row, 0.0), axis=1, keepdims=True)
        mask_col[s] = jnp.broadcast_to(column, (PATCH, 128))
        npatch.append(jnp.maximum(jnp.sum(column, axis=0, keepdims=True), 1.0))

    def forward(s):
        def body(i, carry):
            rows = hid[s, i].reshape(4 * PATCH, D)
            value = jnp.dot(rows, asm_up[0:D, :], preferred_element_type=F32)
            pre[s, i] = value
            act[s, i] = gelu_parts(value)[0].astype(BF)
            return carry

        lax.fori_loop(0, 2, body, 0)

    stats_copies = stats_send(0)
    modulated(0)
    stats_sum(0, stats_copies)
    stats_copies = stats_send(1)
    rows0 = gather_own(hid, 0)
    near_on(0)
    far_own(0, 3)
    far_own(0, 1)
    modulated(1)
    rows1 = gather_own(hid, 1)
    far_on(0, 0)
    near_on(1)
    gather_on(hid, 0, rows0)
    far_on(1, 0)
    far_own(0, 2)
    far_own(1, 3)
    far_own(1, 1)
    far_on(0, 1)
    far_on(0, 3)
    stats_sum(1, stats_copies)
    stats_copies = stats_send(2)
    gather_near(hid, 0, rows0)
    gather_on(hid, 1, rows1)
    far_on(0, 2)
    far_own(1, 2)
    gather_end(hid, 0, rows0)
    far_on(1, 1)
    far_on(1, 3)
    gather_near(hid, 1, rows1)
    gather_sib(rows0)
    assemble(0, asm_up)
    forward(0)
    far_on(1, 2)
    gather_end(hid, 1, rows1)
    gather_sib(rows1)
    forward(1)
    stats_sum(2, stats_copies)
    stats_copies = stats_send(3)
    assemble(1, asm_down)

    def branch_tile(s, i, n):
        start, width = TILES[n]
        return lax.dot_general(
            act[s, i], asm_down[start : start + width, :], LAST, preferred_element_type=F32
        )

    pair = {}

    def branch_away(s):
        for n, (start, width) in enumerate(TILES):
            slot = asm_up.at[pl.ds((s * 4 + n) * 320, 320)]
            slot[:, 0:width] = branch_tile(s, 1, n).astype(BF)
            pair[s, n] = push(slot, sib_recv.at[s, n], sibling)

    def branch_mine(s):
        for n, (start, width) in enumerate(TILES):
            value = branch_tile(s, 0, n)
            pair[s, n].wait_recv()
            value = value + sib_recv[s, n, :, 0:width].astype(F32)
            cols = slice(start, start + width)
            own[s, :, cols] = value[0:80]
            for j, k in ((2, 0), (1, 1), (3, 2)):
                y_send[s, k, :, cols] = value[j * 80 : j * 80 + 80].astype(BF)

    def ring_start(send, recv, parts, plus, minus):
        lo, hi = parts
        return {
            "across_hi": push(hi(send, 0), hi(recv, 0), plus),
            "across_lo": push(lo(send, 0), lo(recv, 0), minus),
            "plus_lo": push(lo(send, 1), lo(recv, 1), plus),
            "minus_hi": push(hi(send, 2), hi(recv, 2), minus),
        }

    def ring_add(send, recv, parts, plus, minus, add, d):
        lo, hi = parts
        d["across_hi"].wait_recv()
        add(hi(send, 1), hi(recv, 0))
        d["plus_hi"] = push(hi(send, 1), hi(recv, 1), plus)
        d["across_lo"].wait_recv()
        add(lo(send, 2), lo(recv, 0))
        d["minus_lo"] = push(lo(send, 2), lo(recv, 2), minus)

    def ring_wait(d):
        for part in ("plus_lo", "minus_hi", "plus_hi", "minus_lo"):
            d[part].wait_recv()

    def add_rows(dst, src):
        def body(i, carry):
            rows = pl.ds(pl.multiple_of(i * CHUNK, CHUNK), CHUNK)
            dst[rows, :] = (dst[rows, :].astype(F32) + src[rows, :].astype(F32)).astype(BF)
            return carry

        lax.fori_loop(0, dst.shape[0] // CHUNK, body, 0)

    def add_blocks(dst, src):
        for k in range(2):
            dst[k] = (dst[k].astype(F32) + src[k].astype(F32)).astype(BF)

    col_parts = tuple((lambda ref, k, cols=cols: ref.at[k, :, cols]) for cols in COLS)

    def branch_ring(s):
        return ring_start(y_send.at[s], y_recv.at[s], col_parts, y_plus, y_minus)

    def branch_add(s, d):
        ring_add(y_send.at[s], y_recv.at[s], col_parts, y_plus, y_minus, add_rows, d)

    def back_rows(s, d):
        ring_wait(d)
        gate = 1.0 + mod[2, s : s + 1, :]
        factor = step_ratio[s]

        def err_body(i, total):
            rows = pl.ds(pl.multiple_of(i * CHUNK, CHUNK), CHUNK)
            branch = (
                own[s, rows, :] + y_recv[s, 1, rows, :].astype(F32) + y_recv[s, 2, rows, :].astype(F32)
            )
            velocity = gate * branch
            drawn = noise[s, rows, :].astype(F32)
            err = drawn + factor * (stale[s, rows, :].astype(F32) - velocity)
            own[s, rows, :] = err
            gap = jnp.sum(drawn * drawn - err * err, axis=1, keepdims=True)
            return total + mask_col[s, rows, 0:1] * gap

        gaps = lax.fori_loop(0, PATCH // CHUNK, err_body, jnp.zeros((CHUNK, 1), F32))
        logratio = jnp.sum(gaps, axis=0, keepdims=True) / (2.0 * npatch[s])
        safe = jnp.maximum(stats[0:1, :], 1.0)
        middle = stats[1:2, :] / safe
        variance = jnp.maximum(stats[2:3, :] / safe - middle * middle, 0.0)
        spread = jnp.maximum(jnp.sqrt(variance), spread_floor)
        own_mean = jnp.sum(member[s] * middle, axis=1, keepdims=True)
        own_spread = jnp.sum(member[s] * spread, axis=1, keepdims=True)
        advantage = (rewards[s] - own_mean) / own_spread
        ratio = jnp.exp(logratio)
        clipped = jnp.clip(ratio, clip_low, clip_high)
        active = jnp.where(ratio * advantage <= clipped * advantage, 1.0, 0.0).astype(F32)
        coef = -valid[s] * advantage * ratio * active / jnp.maximum(stats[3:4, 0:1], 1.0)
        per_patch = coef / npatch[s]

        def back_body(i, carry):
            rows = pl.ds(pl.multiple_of(i * CHUNK, CHUNK), CHUNK)
            scale = per_patch * mask_col[s, rows, 0:1] * factor
            bk[s, 0, 0, rows, :] = (gate * (scale * own[s, rows, :])).astype(BF)
            return carry

        lax.fori_loop(0, PATCH // CHUNK, back_body, 0)

    branch_away(0)
    branch_mine(0)
    ring0 = branch_ring(0)
    branch_away(1)
    branch_mine(1)
    branch_add(0, ring0)
    ring1 = branch_ring(1)
    stats_sum(3, stats_copies)
    stale_in.wait()
    noise_in.wait()
    back_rows(0, ring0)
    branch_add(1, ring1)
    back0 = gather_own(bk, 0)
    back_rows(1, ring1)
    gather_on(bk, 0, back0)
    back1 = gather_own(bk, 1)
    gather_near(bk, 0, back0)
    gather_end(bk, 0, back0)
    gather_sib(back0)

    def back_pre(s):
        def body(i, carry):
            rows = bk[s, i].reshape(4 * PATCH, D)
            value = jnp.dot(rows, asm_down[...], preferred_element_type=F32)
            act[s, i] = (value * gelu_parts(pre[s, i])[1]).astype(BF)
            return carry

        lax.fori_loop(0, 2, body, 0)

    PARTS = ((1, 0, 256), (1, 256, 384), (0, 0, 384), (0, 384, 256))

    def grad_part(p, rows, s, n):
        start, width = TILES[n]
        left = rows[s, :, :, :, start : start + width].reshape(8 * PATCH, width)
        right = act[s, :, :, PARTS[p][1] : PARTS[p][1] + PARTS[p][2]].reshape(8 * PATCH, PARTS[p][2])
        return lax.dot_general(left, right, FIRST, preferred_element_type=F32)

    def grad_rows(p, h, j, k):
        a, b = turn(far_at[h], j), turn(near_at[h], k)
        block = (b * 4 + a) if h == 0 else (a * 4 + b)
        rows = pl.ds(pl.multiple_of(block * BLOCK + 80 * h, 8), 80)
        return grad[rows, PARTS[p][1] : PARTS[p][1] + PARTS[p][2]]

    def part_parts(p, lead):
        cols = pl.ds(PARTS[p][1], PARTS[p][2])
        if lead:
            return tuple((lambda ref, k, i=i: ref.at[k, pl.ds(i, 2), :, cols]) for i in (0, 2))
        return tuple((lambda ref, k, r=r: ref.at[k, pl.ds(*r), cols]) for r in ((0, 48), (48, 32)))

    def far_ring(p, h):
        m = PARTS[p][0]
        return raws[h].at[m], x_recv.at[m, h], part_parts(p, True), far[h][1], far[h][3]

    def near_ring(p, h):
        m = PARTS[p][0]
        return b_send.at[m, h], b_recv.at[m, h], part_parts(p, False), near[h][1], near[h][3]

    def far_start(p):
        m, start, width = PARTS[p]
        cols = slice(start, start + width)
        for j, slot in ((2, 0), (1, 1), (3, 2)):
            for h in range(2):
                for k in range(4):
                    raws[h][m, slot, k, :, cols] = grad_rows(p, h, j, k).astype(BF)
        out = [ring_start(*far_ring(p, h)) for h in range(2)]
        for h in range(2):
            for k in range(4):
                grad_own[m, h, k, :, cols] = grad_rows(p, h, 0, k)
        return out

    def far_add(p, d):
        for h in range(2):
            ring_add(*far_ring(p, h), add_blocks, d[h])

    def near_start(p, d):
        m, start, width = PARTS[p]
        cols = slice(start, start + width)
        out = []
        for h in range(2):
            ring_wait(d[h])
            for k in (2, 1, 3, 0):
                total = (
                    grad_own[m, h, k, :, cols]
                    + x_recv[m, h, 1, k, :, cols].astype(F32)
                    + x_recv[m, h, 2, k, :, cols].astype(F32)
                )
                if k == 0:
                    grad_own[m, h, 0, :, cols] = total
                else:
                    b_send[m, h, {2: 0, 1: 1, 3: 2}[k], :, cols] = total.astype(BF)
            out.append(ring_start(*near_ring(p, h)))
        return out

    def near_add(p, d):
        for h in range(2):
            ring_add(*near_ring(p, h), add_rows, d[h])

    def out_cols(owner, start, width):
        return pl.ds(pl.multiple_of(owner * SLICE + start, 128), width)

    out_copies = []

    def update(p, d):
        m, start, width = PARTS[p]
        cols = slice(start, start + width)
        for h in range(2):
            ring_wait(d[h])
            rows = slice(0, 80) if h == 0 else slice(80, BLOCK)
            high = 80 if h == 0 else 72
            grads = (
                grad_own[m, h, 0, 0:high, cols]
                + b_recv[m, h, 1, 0:high, cols].astype(F32)
                + b_recv[m, h, 2, 0:high, cols].astype(F32)
            )
            weights = par[m, rows, cols]
            new_first = beta_one * m1[m, rows, cols] + (1.0 - beta_one) * grads
            new_second = beta_two * m2[m, rows, cols] + (1.0 - beta_two) * grads * grads
            first_hat = new_first / (1.0 - beta_one**adam_count)
            second_hat = new_second / (1.0 - beta_two**adam_count)
            step = first_hat / (jnp.sqrt(second_hat) + adam_eps) + weight_decay * weights
            new_weights = weights - learn_rate * step
            m1[m, rows, cols] = new_first
            m2[m, rows, cols] = new_second
            par[m, rows, cols] = new_weights
            land[m, 0, rows, cols] = new_weights.astype(BF)
        mine = land.at[m, 0, :, pl.ds(start, width)]

        def slot(j, k):
            return land.at[m, 2 * j + k, :, pl.ds(start, width)]

        d = {
            "left": push(mine, slot(3, 0), y_plus),
            "right": push(mine, slot(1, 0), y_minus),
            "sib0": push(mine, slot(0, 1), sibling),
        }
        out_store(p, 0, 0)
        if p in (1, 3):
            out_copies.append(move(m1.at[m], o_m1.at[m]))
            out_copies.append(move(m2.at[m], o_m2.at[m]))
            out_copies.append(move(par.at[m], o_par.at[m]))
        return d

    def out_store(p, j, k):
        m, start, width = PARTS[p]
        owner = turn(y, j) * 2 + (c if k == 0 else 1 - c)
        block = land.at[m, 2 * j + k, :, pl.ds(start, width)]
        out_copies.append(move(block, o_roll.at[m, :, out_cols(owner, start, width)]))

    def out_on(p, d):
        m, start, width = PARTS[p]
        half = 128 * ((width // 128 + 1) // 2)
        for key, j, to, at_, wide in (
            ("left", 3, y_plus, start, half),
            ("right", 1, y_minus, start + half, width - half),
        ):
            d[key].wait_recv()
            cols = pl.ds(at_, wide)
            d[key, "across"] = push(land.at[m, 2 * j, :, cols], land.at[m, 4, :, cols], to)
            cols = pl.ds(start, width)
            d[key, "sib"] = push(
                land.at[m, 2 * j, :, cols], land.at[m, 2 * j + 1, :, cols], sibling
            )
            out_store(p, j, 0)

    def out_end(p, d):
        m, start, width = PARTS[p]
        d["left", "across"].wait_recv()
        d["right", "across"].wait_recv()
        cols = pl.ds(start, width)
        d["sib2"] = push(land.at[m, 4, :, cols], land.at[m, 5, :, cols], sibling)
        out_store(p, 2, 0)

    def out_sib(p, d):
        d["sib0"].wait_recv()
        out_store(p, 0, 1)
        d["left", "sib"].wait_recv()
        out_store(p, 3, 1)
        d["right", "sib"].wait_recv()
        out_store(p, 1, 1)
        d["sib2"].wait_recv()
        out_store(p, 2, 1)

    for copy in weights_sent:
        copy.wait_send()
    grad[pl.ds(D, 8), :] = jnp.zeros((8, SLICE), F32)

    for n, (start, width) in enumerate(TILES):
        for p in (0, 1):
            cols = slice(PARTS[p][1], PARTS[p][1] + PARTS[p][2])
            grad[start : start + width, cols] = grad_part(p, bk, 0, n)
    gather_on(bk, 1, back1)
    back_pre(0)
    gather_near(bk, 1, back1)
    gather_end(bk, 1, back1)
    gather_sib(back1)

    def down_part(p):
        cols = slice(PARTS[p][1], PARTS[p][1] + PARTS[p][2])
        for n, (start, width) in enumerate(TILES):
            grad[start : start + width, cols] += grad_part(p, bk, 1, n)

    def up_part(p):
        cols = slice(PARTS[p][1], PARTS[p][1] + PARTS[p][2])
        for n, (start, width) in enumerate(TILES):
            grad[start : start + width, cols] = grad_part(p, hid, 0, n) + grad_part(p, hid, 1, n)

    down_part(0)
    far0 = far_start(0)
    down_part(1)
    far1 = far_start(1)
    back_pre(1)
    far_add(0, far0)
    up_part(2)
    far_add(1, far1)
    far2 = far_start(2)
    up_part(3)
    m1_in.wait()
    m2_in.wait()
    near0 = near_start(0, far0)
    near1 = near_start(1, far1)
    far3 = far_start(3)
    far_add(2, far2)
    near_add(0, near0)
    near_add(1, near1)
    far_add(3, far3)
    out0 = update(0, near0)
    near2 = near_start(2, far2)
    out1 = update(1, near1)
    near3 = near_start(3, far3)
    near_add(2, near2)
    near_add(3, near3)
    out_on(0, out0)
    out2 = update(2, near2)
    out3 = update(3, near3)
    out_on(1, out1)
    out_end(0, out0)
    out_on(2, out2)
    out_end(1, out1)
    out_on(3, out3)
    out_end(2, out2)
    out_end(3, out3)
    for p, out in enumerate((out0, out1, out2, out3)):
        out_sib(p, out)
    for copy in out_copies:
        copy.wait()
    for copy in sent:
        copy.wait_send()


def settle(*refs):
    sources, targets, held, sem = refs[:4], refs[4:8], refs[8:12], refs[12]
    pieces = [(i, m) for i in range(4) for m in range(2)]
    reads = []
    for n, (i, m) in enumerate(pieces):
        reads.append(pltpu.make_async_copy(sources[i].at[m], held[i].at[m], sem.at[n]))
        reads[-1].start()
    writes = []
    for n, (i, m) in enumerate(pieces):
        reads[n].wait()
        writes.append(pltpu.make_async_copy(held[i].at[m], targets[i].at[m], sem.at[8 + n]))
        writes[-1].start()
    for write in writes:
        write.wait()


def per_device(
    latents,
    stale_velocity,
    noise,
    modulation,
    step_ratio,
    rewards,
    group_ids,
    step_index,
    valid_steps,
    patch_mask,
    params,
    first_moment,
    second_moment,
):
    any_ = pl.BlockSpec(memory_space=pl.ANY)
    shard = jax.ShapeDtypeStruct(params.shape, F32)
    outs = pl.pallas_call(
        kernel,
        out_shape=(shard, shard, shard, jax.ShapeDtypeStruct((2, BLOCK, 8 * SLICE), BF)),
        in_specs=[any_] * 13,
        out_specs=(any_,) * 4,
        scratch_shapes=[
            pltpu.VMEM((2, 2, 4, PATCH, D), BF),
            pltpu.VMEM((2, 2, 4, PATCH, D), BF),
            pltpu.VMEM((2, 4, 4, 80, SLICE), BF),
            pltpu.VMEM((2, 4, 4, 80, SLICE), BF),
            pltpu.VMEM((2560, SLICE), BF),
            pltpu.VMEM((D, SLICE), BF),
            pltpu.VMEM((2, 2, 4 * PATCH, SLICE), F32),
            pltpu.VMEM((2, 2, 4 * PATCH, SLICE), BF),
            pltpu.VMEM((2, 4, 4 * PATCH, SLICE), BF),
            pltpu.VMEM((2, 3, PATCH, D), BF),
            pltpu.VMEM((2, 3, PATCH, D), BF),
            pltpu.VMEM((2, PATCH, D), F32),
            pltpu.VMEM((D + 8, SLICE), F32),
            pltpu.VMEM((2, 2, 3, 4, 80, SLICE), BF),
            pltpu.VMEM((2, 2, 4, 80, SLICE), F32),
            pltpu.VMEM((2, 2, 3, 80, SLICE), BF),
            pltpu.VMEM((2, 2, 3, 80, SLICE), BF),
            pltpu.VMEM((2, PATCH, D), BF),
            pltpu.VMEM((2, PATCH, D), BF),
            pltpu.VMEM((2, BLOCK, SLICE), F32),
            pltpu.VMEM((2, BLOCK, SLICE), F32),
            pltpu.VMEM((2, BLOCK, SLICE), F32),
            pltpu.VMEM((2, 8, BLOCK, SLICE), BF),
            pltpu.VMEM((2, PATCH, 128), F32),
            pltpu.VMEM((8, 128), F32),
            pltpu.VMEM((4, 4, 8, 128), F32),
            pltpu.SMEM((2,), F32),
            pltpu.SMEM((2,), jnp.int32),
            pltpu.SMEM((2,), jnp.int32),
            pltpu.SMEM((2,), jnp.int32),
            pltpu.SMEM((2,), F32),
            pltpu.VMEM((2, PATCH), jnp.int32),
            pltpu.VMEM((3, 2, D), F32),
            pltpu.SemaphoreType.DMA((N_COPIES,)),
            pltpu.SemaphoreType.DMA((N_COPIES,)),
            pltpu.SemaphoreType.DMA((56,)),
        ],
        compiler_params=pltpu.CompilerParams(
            collective_id=0, has_side_effects=True, vmem_limit_bytes=63 << 20
        ),
    )(
        rewards,
        group_ids,
        step_index,
        valid_steps,
        step_ratio,
        patch_mask,
        modulation.transpose(1, 0, 2),
        latents,
        stale_velocity,
        noise,
        params,
        first_moment,
        second_moment,
    )
    return tuple(
        pl.pallas_call(
            settle,
            out_shape=tuple(jax.ShapeDtypeStruct(o.shape, o.dtype) for o in outs),
            in_specs=[any_] * 4,
            out_specs=(any_,) * 4,
            scratch_shapes=[pltpu.VMEM(o.shape, o.dtype) for o in outs]
            + [pltpu.SemaphoreType.DMA((16,))],
        )(*outs)
    )


def solution(mesh):
    rows = ("roll", "fsdp")
    weights = P(None, "fsdp", "roll")
    return jax.shard_map(
        per_device,
        mesh=mesh,
        in_specs=(
            P(rows, None, None),
            P(rows, None, None),
            P(rows, None, None),
            P(rows, None, None),
            P(rows),
            P(rows),
            P(rows),
            P(rows),
            P(rows),
            P(rows, None),
            weights,
            weights,
            weights,
        ),
        out_specs=(weights, weights, weights, P(None, "fsdp", None)),
        check_vma=False,
    )
```

```python
import functools

import jax
import jax.numpy as jnp
from jax import lax
from jax.experimental import pallas as pl
from jax.experimental.pallas import tpu as pltpu
from jax.sharding import PartitionSpec as P

GROUPS = 12
D = 2432
BLOCK = 152
SLICE = 640
PATCH = 80
CHUNK = 16

eps_norm = 1e-06
clip_low = 0.8
clip_high = 1.2
spread_floor = 0.25
beta_one = 0.9
beta_two = 0.999
learn_rate = 0.001
weight_decay = 0.01
adam_eps = 1e-08
adam_count = 100.0

BF = jnp.bfloat16
F32 = jnp.float32
MESH = pl.DeviceIdType.MESH
COLS = (pl.ds(0, 1280), pl.ds(1280, 1152))
OUT_COLS = ((0, 384), (384, 256))
LAST = (((1,), (1,)), ((), ()))
FIRST = (((0,), (0,)), ((), ()))
N_SEND = 48
N_PAIR = 8
N_RECV = 141
N_LOCAL = 20


def gelu_parts(pre):
    root = 0.7978845608028654
    square = pre * pre
    t = jnp.tanh(root * (pre + 0.044715 * (square * pre)))
    cdf = 0.5 * (1.0 + t)
    slope = cdf + pre * (0.5 * (1.0 - t * t)) * (root * (1.0 + (3.0 * 0.044715) * square))
    return pre * cdf, slope


class Once:
    def __init__(self, wait):
        self.todo = wait

    def wait(self):
        if self.todo is not None:
            self.todo()
        self.todo = None


def kernel(
    rewards_h,
    group_ids_h,
    step_index_h,
    valid_steps_h,
    step_ratio_h,
    mask_h,
    mod_h,
    lat_h,
    stale_h,
    noise_h,
    par_h,
    m1_h,
    m2_h,
    o_par,
    o_m1,
    o_m2,
    o_roll,
    hid,
    bk,
    raw0,
    raw1,
    asm_up,
    asm_down,
    pre,
    act,
    sib_recv,
    y_send,
    y_recv,
    own,
    grad,
    x_recv,
    grad_own,
    b_send,
    b_recv,
    stale,
    noise,
    par,
    m1,
    m2,
    land,
    mask_col,
    stats,
    stats_recv,
    rewards,
    group_ids,
    step_index,
    valid_steps,
    step_ratio,
    mask_in,
    mod,
    send_sem,
    recv_sem,
    local_sem,
):
    roll = lax.axis_index("roll")
    fsdp = lax.axis_index("fsdp")
    y, c = roll // 2, lax.rem(roll, 2)
    x, z = fsdp // 4, lax.rem(fsdp, 4)

    def turn(a, by):
        return lax.rem(a + by, 4)

    def at(x_, y_, z_, c_):
        return (y_ * 2 + c_, x_ * 4 + z_)

    y_ring = [at(x, turn(y, j), z, c) for j in range(4)]
    x_ring = [at(turn(x, j), y, z, c) for j in range(4)]
    z_ring = [at(x, y, turn(z, j), c) for j in range(4)]
    sibling = at(x, y, z, 1 - c)
    y_plus, y_minus = y_ring[1], y_ring[3]

    barrier = pltpu.get_barrier_semaphore()
    partners = y_ring[1:] + x_ring[1:] + z_ring[1:] + [sibling]
    for partner in partners:
        pl.semaphore_signal(barrier, inc=1, device_id=partner, device_id_type=MESH)

    stage, fresh_id, spare, sends, moves = [0], [0], [], [], []

    def recv_id():
        if stage[0] == 2 and spare:
            return spare.pop(0)
        fresh_id[0] += 1
        if stage[0] == 0:
            spare.append(fresh_id[0] - 1)
        return fresh_id[0] - 1

    def push(src, dst, device, landed=None, log=None):
        i, n = recv_id(), len(sends)
        if n >= N_SEND:
            sends[n - N_SEND].wait()

        def describe(src, dst):
            return pltpu.make_async_remote_copy(
                src_ref=src,
                dst_ref=dst,
                send_sem=send_sem.at[n % N_SEND],
                recv_sem=recv_sem.at[i],
                device_id=device,
                device_id_type=MESH,
            )

        copy = describe(src, dst)
        copy.start()
        sends.append(Once(copy.wait_send))
        if log is not None:
            log.append(sends[-1])
        return copy if landed is None else describe(landed, landed)

    def move(src, dst):
        n = len(moves)
        if n >= N_LOCAL:
            moves[n - N_LOCAL].wait()
        copy = pltpu.make_async_copy(src, dst, local_sem.at[n % N_LOCAL])
        copy.start()
        moves.append(Once(copy.wait))
        return moves[-1]

    par_in = move(par_h, par)
    lat_in = [move(lat_h.at[s], y_send.at[s, 0]) for s in range(2)] + [move(mod_h, mod)]
    small_in = [
        move(rewards_h, rewards),
        move(group_ids_h, group_ids),
        move(step_index_h, step_index),
        move(valid_steps_h, valid_steps),
        move(step_ratio_h, step_ratio),
        move(mask_h, mask_in),
    ]

    raws = (raw0, raw1)
    near = (x_ring, z_ring)
    far = (z_ring, x_ring)
    near_at = (x, z)
    far_at = (z, x)

    par_in.wait()
    for m in range(2):
        raw0[m, z, x] = par[m, 0:80, :].astype(BF)
        raw1[m, x, z, 0:72, :] = par[m, 80:BLOCK, :].astype(BF)
        raw1[m, x, z, 64:80, :] = jnp.concatenate(
            [par[m, 144:BLOCK, :], jnp.zeros((8, SLICE), F32)], axis=0
        ).astype(BF)

    def each(n, body):
        def step(i, carry):
            body(i)
            return carry

        lax.fori_loop(0, n, step, 0)

    def modulated(s):
        shift = mod[0, s : s + 1, :]
        scaling = 1.0 + mod[1, s : s + 1, :]

        def body(i, carry):
            rows = pl.ds(pl.multiple_of(i * CHUNK, CHUNK), CHUNK)
            values = y_send[s, 0, rows, :].astype(F32)
            middle = jnp.sum(values, axis=-1, keepdims=True) / D
            centred = values - middle
            spread = jnp.sum(centred * centred, axis=-1, keepdims=True) / D
            normed = centred * lax.rsqrt(spread + eps_norm)
            hid[s, 0, 0, rows, :] = (normed * scaling + shift).astype(BF)
            return carry

        lax.fori_loop(0, PATCH // CHUNK, body, 0)

    pl.semaphore_wait(barrier, len(partners))

    first, second, weights_sent = {}, {}, []

    def near_own(m):
        for h in range(2):
            a, b = far_at[h], near_at[h]
            mine = raws[h].at[m, a, b]
            for k in (3, 1):
                first[m, h, k] = push(
                    mine, mine, near[h][4 - k], raws[h].at[m, a, turn(b, k)], log=weights_sent
                )

    def near_on(m):
        k = (3, 1)[m]
        for h in range(2):
            a, b = far_at[h], near_at[h]
            first[m, h, k].wait_recv()
            block = raws[h].at[m, a, turn(b, k)]
            first[m, h, 2] = push(
                block, block, near[h][4 - k], raws[h].at[m, a, turn(b, 2)], log=weights_sent
            )
        for h in range(2):
            first[m, h, 4 - k].wait_recv()

    def far_own(m, k):
        for h in range(2):
            a, b = far_at[h], turn(near_at[h], k)
            if k == 2:
                first[m, h, 2].wait_recv()
            block = raws[h].at[m, a, b]
            for side in (3, 1):
                second[m, h, k, side] = push(
                    block, block, far[h][4 - side], raws[h].at[m, turn(a, side), b], log=weights_sent
                )

    def far_on(m, k):
        side = 3 if k < 2 else 1
        for h in range(2):
            a, b = far_at[h], turn(near_at[h], k)
            second[m, h, k, side].wait_recv()
            block = raws[h].at[m, turn(a, side), b]
            second[m, h, k, 2] = push(
                block, block, far[h][4 - side], raws[h].at[m, turn(a, 2), b], log=weights_sent
            )

    near_own(0)
    stale_in = move(stale_h, stale)
    noise_in = move(noise_h, noise)
    m1_in = move(m1_h, m1)
    m2_in = move(m2_h, m2)
    for copy in lat_in:
        copy.wait()

    def gather_own(buf, s):
        mine = buf.at[s, 0, 0]
        left, right = buf.at[s, 0, 3], buf.at[s, 0, 1]
        lo, hi = COLS
        return {
            "left_lo": push(mine.at[:, lo], left.at[:, lo], y_plus),
            "right_hi": push(mine.at[:, hi], right.at[:, hi], y_minus),
            "left_hi": push(mine.at[:, hi], left.at[:, hi], y_plus),
            "right_lo": push(mine.at[:, lo], right.at[:, lo], y_minus),
            "sib0": push(mine, buf.at[s, 1, 0], sibling),
        }

    def gather_on(buf, s, d):
        left, right, across = buf.at[s, 0, 3], buf.at[s, 0, 1], buf.at[s, 0, 2]
        lo, hi = COLS
        d["left_lo"].wait_recv()
        d["across_lo"] = push(left.at[:, lo], across.at[:, lo], y_plus)
        d["right_hi"].wait_recv()
        d["across_hi"] = push(right.at[:, hi], across.at[:, hi], y_minus)

    def gather_near(buf, s, d):
        d["left_hi"].wait_recv()
        d["sib3"] = push(buf.at[s, 0, 3], buf.at[s, 1, 3], sibling)
        d["right_lo"].wait_recv()
        d["sib1"] = push(buf.at[s, 0, 1], buf.at[s, 1, 1], sibling)

    def gather_end(buf, s, d):
        d["across_lo"].wait_recv()
        d["across_hi"].wait_recv()
        d["sib2"] = push(buf.at[s, 0, 2], buf.at[s, 1, 2], sibling)

    def gather_sib(d):
        for j in range(4):
            d["sib%d" % j].wait_recv()

    def stats_send(step):
        ring = ([None, sibling], y_ring, x_ring, z_ring)[step]
        log = []
        return [
            push(stats, stats_recv.at[step, j], ring[j], log=log) for j in range(1, len(ring))
        ], log

    def stats_sum(step, copies):
        total = stats[...]
        for j, copy in enumerate(copies[0]):
            copy.wait_recv()
            total = total + stats_recv[step, j + 1]
        for copy in copies[1]:
            copy.wait()
        stats[...] = total

    def assemble(m, out):
        for h in range(2):
            for k in range(4):
                second[m, h, k, 1 if k < 2 else 3].wait_recv()
                second[m, h, k, 2].wait_recv()

        def body(i, carry):
            base = pl.multiple_of(i * (4 * BLOCK), CHUNK)
            parts = []
            for k in range(4):
                parts += [raw0[m, k, i], raw1[m, i, k, 0:72, :]]
            out[pl.ds(base, 4 * BLOCK), :] = jnp.concatenate(parts, axis=0)
            return carry

        lax.fori_loop(0, 4, body, 0)

    def forward(s, i):
        rows = hid[s, i].reshape(4 * PATCH, D)
        value = jnp.dot(rows, asm_up[0:D, :], preferred_element_type=F32)
        pre[s, i] = value
        act[s, i] = gelu_parts(value)[0].astype(BF)

    modulated(0)
    rows0 = gather_own(hid, 0)
    near_own(1)
    near_on(0)
    far_own(0, 1)
    far_own(0, 0)
    modulated(1)

    for copy in small_in:
        copy.wait()
    lane = lax.broadcasted_iota(jnp.int32, (1, 128), 1)
    valid = [jnp.where(step_index[s] < valid_steps[s], 1.0, 0.0).astype(F32) for s in range(2)]
    member = [jnp.where(lane == group_ids[s], 1.0, 0.0).astype(F32) for s in range(2)]
    stats[...] = jnp.zeros((8, 128), F32)
    stats[0:1, :] = member[0] * valid[0] + member[1] * valid[1]
    stats[1:2, :] = member[0] * (valid[0] * rewards[0]) + member[1] * (valid[1] * rewards[1])
    stats[2:3, :] = member[0] * (valid[0] * (rewards[0] * rewards[0])) + member[1] * (
        valid[1] * (rewards[1] * rewards[1])
    )
    stats[3:4, :] = jnp.zeros((1, 128), F32) + (valid[0] + valid[1])

    stats_copies = stats_send(0)
    gather_on(hid, 0, rows0)
    near_on(1)
    rows1 = gather_own(hid, 1)
    stats_sum(0, stats_copies)
    far_own(0, 3)
    far_own(0, 2)
    far_on(0, 1)
    far_own(1, 2)
    far_on(0, 2)
    far_on(0, 0)
    far_on(0, 3)
    far_own(1, 0)
    far_own(1, 3)
    gather_on(hid, 1, rows1)
    stats_copies = stats_send(1)
    gather_near(hid, 0, rows0)
    gather_end(hid, 0, rows0)
    far_on(1, 2)
    far_own(1, 1)
    assemble(0, asm_up)
    gather_sib(rows0)
    forward(0, 0)
    gather_near(hid, 1, rows1)
    far_on(1, 0)
    forward(0, 1)
    gather_end(hid, 1, rows1)
    far_on(1, 3)
    far_on(1, 1)
    gather_sib(rows1)
    each(2, lambda i: forward(1, i))
    assemble(1, asm_down)
    stage[0] = 1
    stats_sum(1, stats_copies)
    stats_copies = stats_send(2)

    def pair_copy(s, n):
        i = s * 4 + n
        return pltpu.make_async_remote_copy(
            src_ref=asm_up.at[pl.ds(pl.multiple_of((s * 4 + n) * 320, CHUNK), 320)],
            dst_ref=sib_recv.at[s, n],
            send_sem=send_sem.at[N_SEND + i],
            recv_sem=recv_sem.at[N_RECV + i],
            device_id=sibling,
            device_id_type=MESH,
        )

    def branch_tile(s, i, n):
        cols = pl.ds(pl.multiple_of(jnp.minimum(n * SLICE, D - SLICE), 128), SLICE)
        value = lax.dot_general(act[s, i], asm_down[cols, :], LAST, preferred_element_type=F32)
        return cols, value

    def branch_away(s):
        def body(n):
            value = branch_tile(s, 1, n)[1]
            asm_up[pl.ds(pl.multiple_of((s * 4 + n) * 320, CHUNK), 320), :] = value.astype(BF)
            pair_copy(s, n).start()

        each(4, body)

    def branch_mine(s):
        def body(n):
            cols, value = branch_tile(s, 0, n)
            pair_copy(s, n).wait()
            value = value + sib_recv[s, n].astype(F32)
            own[s, :, cols] = value[0:80]
            for j, k in ((2, 0), (1, 1), (3, 2)):
                y_send[s, k, :, cols] = value[j * 80 : j * 80 + 80].astype(BF)

        each(4, body)

    def ring_start(send, recv, parts, plus, minus):
        lo, hi = parts
        return {
            "across_hi": push(hi(send, 0), hi(recv, 0), plus),
            "across_lo": push(lo(send, 0), lo(recv, 0), minus),
            "plus_lo": push(lo(send, 1), lo(recv, 1), plus),
            "minus_hi": push(hi(send, 2), hi(recv, 2), minus),
        }

    def ring_add(send, recv, parts, plus, minus, add, d):
        lo, hi = parts
        d["across_hi"].wait_recv()
        add(hi(send, 1), hi(recv, 0))
        d["plus_hi"] = push(hi(send, 1), hi(recv, 1), plus)
        d["across_lo"].wait_recv()
        add(lo(send, 2), lo(recv, 0))
        d["minus_lo"] = push(lo(send, 2), lo(recv, 2), minus)

    def ring_wait(d):
        for part in ("plus_lo", "minus_hi", "plus_hi", "minus_lo"):
            d[part].wait_recv()

    def add_rows(dst, src):
        def body(i, carry):
            rows = pl.ds(pl.multiple_of(i * CHUNK, CHUNK), CHUNK)
            dst[rows, :] = (dst[rows, :].astype(F32) + src[rows, :].astype(F32)).astype(BF)
            return carry

        lax.fori_loop(0, dst.shape[0] // CHUNK, body, 0)

    def add_blocks(dst, src):
        for k in range(2):
            dst[k] = (dst[k].astype(F32) + src[k].astype(F32)).astype(BF)

    col_parts = tuple((lambda ref, k, cols=cols: ref.at[k, :, cols]) for cols in COLS)

    def branch_ring(s):
        return ring_start(y_send.at[s], y_recv.at[s], col_parts, y_plus, y_minus)

    def branch_add(s, d):
        ring_add(y_send.at[s], y_recv.at[s], col_parts, y_plus, y_minus, add_rows, d)

    def back_rows(s, d):
        ring_wait(d)
        gate = 1.0 + mod[2, s : s + 1, :]
        factor = step_ratio[s]

        def err_body(i, total):
            rows = pl.ds(pl.multiple_of(i * CHUNK, CHUNK), CHUNK)
            branch = (
                own[s, rows, :] + y_recv[s, 1, rows, :].astype(F32) + y_recv[s, 2, rows, :].astype(F32)
            )
            velocity = gate * branch
            drawn = noise[s, rows, :].astype(F32)
            err = drawn + factor * (stale[s, rows, :].astype(F32) - velocity)
            own[s, rows, :] = err
            gap = jnp.sum(drawn * drawn - err * err, axis=1, keepdims=True)
            return total + mask_col[s, rows, 0:1] * gap

        gaps = lax.fori_loop(0, PATCH // CHUNK, err_body, jnp.zeros((CHUNK, 1), F32))
        logratio = jnp.sum(gaps, axis=0, keepdims=True) / (2.0 * npatch[s])
        safe = jnp.maximum(stats[0:1, :], 1.0)
        middle = stats[1:2, :] / safe
        variance = jnp.maximum(stats[2:3, :] / safe - middle * middle, 0.0)
        spread = jnp.maximum(jnp.sqrt(variance), spread_floor)
        own_mean = jnp.sum(member[s] * middle, axis=1, keepdims=True)
        own_spread = jnp.sum(member[s] * spread, axis=1, keepdims=True)
        advantage = (rewards[s] - own_mean) / own_spread
        ratio = jnp.exp(logratio)
        clipped = jnp.clip(ratio, clip_low, clip_high)
        active = jnp.where(ratio * advantage <= clipped * advantage, 1.0, 0.0).astype(F32)
        coef = -valid[s] * advantage * ratio * active / jnp.maximum(stats[3:4, 0:1], 1.0)
        per_patch = coef / npatch[s]

        def back_body(i, carry):
            rows = pl.ds(pl.multiple_of(i * CHUNK, CHUNK), CHUNK)
            scale = per_patch * mask_col[s, rows, 0:1] * factor
            bk[s, 0, 0, rows, :] = (gate * (scale * own[s, rows, :])).astype(BF)
            return carry

        lax.fori_loop(0, PATCH // CHUNK, back_body, 0)

    branch_away(0)
    branch_mine(0)
    ring0 = branch_ring(0)
    stats_sum(2, stats_copies)
    stats_copies = stats_send(3)

    diag = lax.broadcasted_iota(jnp.int32, (PATCH, PATCH), 0) == lax.broadcasted_iota(
        jnp.int32, (PATCH, PATCH), 1
    )
    npatch = []
    for s in range(2):
        row = jnp.broadcast_to(mask_in[s : s + 1, :].astype(F32), (PATCH, PATCH))
        column = jnp.sum(jnp.where(diag, row, 0.0), axis=1, keepdims=True)
        mask_col[s] = jnp.broadcast_to(column, (PATCH, 128))
        npatch.append(jnp.maximum(jnp.sum(column, axis=0, keepdims=True), 1.0))

    branch_away(1)
    branch_mine(1)
    branch_add(0, ring0)
    ring1 = branch_ring(1)
    stats_sum(3, stats_copies)
    stale_in.wait()
    noise_in.wait()
    back_rows(0, ring0)
    branch_add(1, ring1)
    stage[0] = 2
    back0 = gather_own(bk, 0)
    back_rows(1, ring1)
    gather_on(bk, 0, back0)
    back1 = gather_own(bk, 1)
    gather_near(bk, 0, back0)
    gather_end(bk, 0, back0)
    gather_sib(back0)

    def back_pre(s):
        def body(i, carry):
            rows = bk[s, i].reshape(4 * PATCH, D)
            value = jnp.dot(rows, asm_down[...], preferred_element_type=F32)
            act[s, i] = (value * gelu_parts(pre[s, i])[1]).astype(BF)
            return carry

        lax.fori_loop(0, 2, body, 0)

    PARTS = ((1, 0, 256), (1, 256, 384), (0, 0, 384), (0, 384, 256))

    def over_width(body):
        each(3, lambda n: body(pl.multiple_of(n * SLICE, 128), SLICE))
        body(3 * SLICE, D - 3 * SLICE)

    def grad_part(rows, s, at_, wide, start, width):
        left = rows[s, :, :, :, pl.ds(at_, wide)].reshape(8 * PATCH, wide)
        right = act[s, :, :, start : start + width].reshape(8 * PATCH, width)
        return lax.dot_general(left, right, FIRST, preferred_element_type=F32)

    def grad_rows(p, h, j, k):
        a, b = turn(far_at[h], j), turn(near_at[h], k)
        block = (b * 4 + a) if h == 0 else (a * 4 + b)
        rows = pl.ds(pl.multiple_of(block * BLOCK + 80 * h, 8), 80)
        return grad[rows, PARTS[p][1] : PARTS[p][1] + PARTS[p][2]]

    def block_parts(p):
        cols = pl.ds(PARTS[p][1], PARTS[p][2])
        return tuple((lambda ref, k, i=i: ref.at[k, pl.ds(i, 2), :, cols]) for i in (0, 2))

    def far_ring(p, h):
        m = PARTS[p][0]
        return raws[h].at[m], x_recv.at[m, h], block_parts(p), far[h][1], far[h][3]

    def far_start(p):
        m, start, width = PARTS[p]
        cols = slice(start, start + width)

        def away(k):
            for h in range(2):
                for j, slot in ((2, 0), (1, 1), (3, 2)):
                    raws[h][m, slot, k, :, cols] = grad_rows(p, h, j, k).astype(BF)

        def mine(k):
            for h in range(2):
                grad_own[m, h, k, :, cols] = grad_rows(p, h, 0, k)

        each(4, away)
        out = [ring_start(*far_ring(p, h)) for h in range(2)]
        each(4, mine)
        return out

    def far_add(p, d):
        for h in range(2):
            ring_add(*far_ring(p, h), add_blocks, d[h])

    def near_start(p, d):
        m, start, width = PARTS[p]
        cols = slice(start, start + width)
        out = []
        for h in range(2):
            ring_wait(d[h])

            def total(k):
                return (
                    grad_own[m, h, k, :, cols]
                    + x_recv[m, h, 1, k, :, cols].astype(F32)
                    + x_recv[m, h, 2, k, :, cols].astype(F32)
                )

            def away(k):
                b_send[m, h, k, :, cols] = total(k + 1).astype(BF)

            each(3, away)
            send, recv = b_send.at[m, h], b_recv.at[m, h]
            part = pl.ds(start, width)
            out += [
                push(send.at[k, :, part], recv.at[k, :, part], near[h][k + 1]) for k in (1, 0, 2)
            ]
            grad_own[m, h, 0, :, cols] = total(0)
        return out

    def out_cols(owner, start, width):
        return pl.ds(pl.multiple_of(owner * SLICE + start, 128), width)

    def update(p, d):
        m, start, width = PARTS[p]
        for copy in d:
            copy.wait_recv()

        def columns(n, h):
            cols = pl.ds(pl.multiple_of(start + n * 128, 128), 128)
            rows = slice(0, 80) if h == 0 else slice(80, BLOCK)
            high = 80 if h == 0 else 72
            grads = (
                grad_own[m, h, 0, 0:high, cols]
                + b_recv[m, h, 0, 0:high, cols].astype(F32)
                + b_recv[m, h, 1, 0:high, cols].astype(F32)
                + b_recv[m, h, 2, 0:high, cols].astype(F32)
            )
            weights = par[m, rows, cols]
            new_first = beta_one * m1[m, rows, cols] + (1.0 - beta_one) * grads
            new_second = beta_two * m2[m, rows, cols] + (1.0 - beta_two) * grads * grads
            first_hat = new_first / (1.0 - beta_one**adam_count)
            second_hat = new_second / (1.0 - beta_two**adam_count)
            step = first_hat / (jnp.sqrt(second_hat) + adam_eps) + weight_decay * weights
            new_weights = weights - learn_rate * step
            m1[m, rows, cols] = new_first
            m2[m, rows, cols] = new_second
            par[m, rows, cols] = new_weights
            land[m, 0, rows, cols] = new_weights.astype(BF)

        for h in range(2):
            each(width // 128, functools.partial(columns, h=h))
        mine = land.at[m, 0, :, pl.ds(start, width)]

        def slot(j, k):
            return land.at[m, 2 * j + k, :, pl.ds(start, width)]

        d = {
            "left": push(mine, slot(3, 0), y_plus),
            "right": push(mine, slot(1, 0), y_minus),
            "sib0": push(mine, slot(0, 1), sibling),
        }
        if p == 3:
            d["across"] = push(mine, slot(2, 0), y_ring[2])
        out_store(p, 0, 0)
        if p in (1, 3):
            move(m1.at[m], o_m1.at[m])
            move(m2.at[m], o_m2.at[m])
            move(par.at[m], o_par.at[m])
        return d

    def out_store(p, j, k):
        m, start, width = PARTS[p]
        owner = turn(y, j) * 2 + (c if k == 0 else 1 - c)
        block = land.at[m, 2 * j + k, :, pl.ds(start, width)]
        move(block, o_roll.at[m, :, out_cols(owner, start, width)])

    def out_on(p, d):
        m, start, width = PARTS[p]
        half = 128 * ((width // 128 + 1) // 2)
        for key, j, to, at_, wide in (
            ("left", 3, y_plus, start, half),
            ("right", 1, y_minus, start + half, width - half),
        ):
            d[key].wait_recv()
            cols = pl.ds(at_, wide)
            if p != 3:
                d[key, "across"] = push(land.at[m, 2 * j, :, cols], land.at[m, 4, :, cols], to)
            cols = pl.ds(start, width)
            d[key, "sib"] = push(
                land.at[m, 2 * j, :, cols], land.at[m, 2 * j + 1, :, cols], sibling
            )
            out_store(p, j, 0)

    def out_end(p, d):
        m, start, width = PARTS[p]
        for key in (("across",) if p == 3 else (("left", "across"), ("right", "across"))):
            d[key].wait_recv()
        cols = pl.ds(start, width)
        d["sib2"] = push(land.at[m, 4, :, cols], land.at[m, 5, :, cols], sibling)
        out_store(p, 2, 0)

    def out_sib(p, d):
        d["sib0"].wait_recv()
        out_store(p, 0, 1)
        d["left", "sib"].wait_recv()
        out_store(p, 3, 1)
        d["right", "sib"].wait_recv()
        out_store(p, 1, 1)
        d["sib2"].wait_recv()
        out_store(p, 2, 1)

    for copy in weights_sent:
        copy.wait()
    grad[pl.ds(D, 8), :] = jnp.zeros((8, SLICE), F32)

    def first_rows(at_, wide):
        grad[pl.ds(at_, wide), :] = grad_part(bk, 0, at_, wide, 0, SLICE)

    over_width(first_rows)
    gather_on(bk, 1, back1)
    back_pre(0)
    gather_near(bk, 1, back1)
    gather_end(bk, 1, back1)
    gather_sib(back1)

    def down_part(p):
        start, width = PARTS[p][1:]

        def body(at_, wide):
            cols = slice(start, start + width)
            grad[pl.ds(at_, wide), cols] += grad_part(bk, 1, at_, wide, start, width)

        over_width(body)

    def up_part(p):
        start, width = PARTS[p][1:]

        def body(at_, wide):
            grad[pl.ds(at_, wide), start : start + width] = grad_part(
                hid, 0, at_, wide, start, width
            ) + grad_part(hid, 1, at_, wide, start, width)

        over_width(body)

    down_part(0)
    far0 = far_start(0)
    down_part(1)
    far1 = far_start(1)
    back_pre(1)
    far_add(0, far0)
    up_part(2)
    far_add(1, far1)
    far2 = far_start(2)
    up_part(3)
    m1_in.wait()
    m2_in.wait()
    near0 = near_start(0, far0)
    near1 = near_start(1, far1)
    far3 = far_start(3)
    far_add(2, far2)
    out0 = update(0, near0)
    out1 = update(1, near1)
    far_add(3, far3)
    near2 = near_start(2, far2)
    out_on(0, out0)
    out_on(1, out1)
    near3 = near_start(3, far3)
    out2 = update(2, near2)
    out_end(0, out0)
    out_end(1, out1)
    out3 = update(3, near3)
    out_on(2, out2)
    out_on(3, out3)
    out_end(2, out2)
    out_end(3, out3)
    for p, out in enumerate((out0, out1, out2, out3)):
        out_sib(p, out)
    assert fresh_id[0] <= N_RECV, fresh_id[0]
    for copy in moves + sends:
        copy.wait()


def settle(*refs):
    sources, targets, held, sem = refs[:4], refs[4:8], refs[8:12], refs[12]
    pieces = [(i, m) for i in (3, 0, 1, 2) for m in range(2)]
    reads, writes = [], []
    for n, (i, m) in enumerate(pieces):
        there, here = sources[i].at[m], held[i].at[m]
        reads.append(pltpu.make_async_copy(there, here, sem.at[n]))
        reads[-1].start()
    for n, (i, m) in enumerate(pieces):
        reads[n].wait()
        here, there = held[i].at[m], targets[i].at[m]
        writes.append(pltpu.make_async_copy(here, there, sem.at[len(pieces) + n]))
        writes[-1].start()
    for write in writes:
        write.wait()


def per_device(
    latents,
    stale_velocity,
    noise,
    modulation,
    step_ratio,
    rewards,
    group_ids,
    step_index,
    valid_steps,
    patch_mask,
    params,
    first_moment,
    second_moment,
):
    any_ = pl.BlockSpec(memory_space=pl.ANY)
    shard = jax.ShapeDtypeStruct(params.shape, F32)
    outs = pl.pallas_call(
        kernel,
        out_shape=(shard, shard, shard, jax.ShapeDtypeStruct((2, BLOCK, 8 * SLICE), BF)),
        in_specs=[any_] * 13,
        out_specs=(any_,) * 4,
        scratch_shapes=[
            pltpu.VMEM((2, 2, 4, PATCH, D), BF),
            pltpu.VMEM((2, 2, 4, PATCH, D), BF),
            pltpu.VMEM((2, 4, 4, 80, SLICE), BF),
            pltpu.VMEM((2, 4, 4, 80, SLICE), BF),
            pltpu.VMEM((2560, SLICE), BF),
            pltpu.VMEM((D, SLICE), BF),
            pltpu.VMEM((2, 2, 4 * PATCH, SLICE), F32),
            pltpu.VMEM((2, 2, 4 * PATCH, SLICE), BF),
            pltpu.VMEM((2, 4, 4 * PATCH, SLICE), BF),
            pltpu.VMEM((2, 3, PATCH, D), BF),
            pltpu.VMEM((2, 3, PATCH, D), BF),
            pltpu.VMEM((2, PATCH, D), F32),
            pltpu.VMEM((D + 8, SLICE), F32),
            pltpu.VMEM((2, 2, 3, 4, 80, SLICE), BF),
            pltpu.VMEM((2, 2, 4, 80, SLICE), F32),
            pltpu.VMEM((2, 2, 3, 80, SLICE), BF),
            pltpu.VMEM((2, 2, 3, 80, SLICE), BF),
            pltpu.VMEM((2, PATCH, D), BF),
            pltpu.VMEM((2, PATCH, D), BF),
            pltpu.VMEM((2, BLOCK, SLICE), F32),
            pltpu.VMEM((2, BLOCK, SLICE), F32),
            pltpu.VMEM((2, BLOCK, SLICE), F32),
            pltpu.VMEM((2, 8, BLOCK, SLICE), BF),
            pltpu.VMEM((2, PATCH, 128), F32),
            pltpu.VMEM((8, 128), F32),
            pltpu.VMEM((4, 4, 8, 128), F32),
            pltpu.SMEM((2,), F32),
            pltpu.SMEM((2,), jnp.int32),
            pltpu.SMEM((2,), jnp.int32),
            pltpu.SMEM((2,), jnp.int32),
            pltpu.SMEM((2,), F32),
            pltpu.VMEM((2, PATCH), jnp.int32),
            pltpu.VMEM((3, 2, D), F32),
            pltpu.SemaphoreType.DMA((N_SEND + N_PAIR,)),
            pltpu.SemaphoreType.DMA((N_RECV + N_PAIR,)),
            pltpu.SemaphoreType.DMA((N_LOCAL,)),
        ],
        compiler_params=pltpu.CompilerParams(
            collective_id=0, has_side_effects=True, vmem_limit_bytes=63 << 20
        ),
    )(
        rewards,
        group_ids,
        step_index,
        valid_steps,
        step_ratio,
        patch_mask,
        modulation.transpose(1, 0, 2),
        latents,
        stale_velocity,
        noise,
        params,
        first_moment,
        second_moment,
    )
    return tuple(
        pl.pallas_call(
            settle,
            out_shape=tuple(jax.ShapeDtypeStruct(o.shape, o.dtype) for o in outs),
            in_specs=[any_] * 4,
            out_specs=(any_,) * 4,
            scratch_shapes=[pltpu.VMEM(o.shape, o.dtype) for o in outs]
            + [pltpu.SemaphoreType.DMA((16,))],
        )(*outs)
    )


def solution(mesh):
    rows = ("roll", "fsdp")
    weights = P(None, "fsdp", "roll")
    return jax.shard_map(
        per_device,
        mesh=mesh,
        in_specs=(
            P(rows, None, None),
            P(rows, None, None),
            P(rows, None, None),
            P(rows, None, None),
            P(rows),
            P(rows),
            P(rows),
            P(rows),
            P(rows),
            P(rows, None),
            weights,
            weights,
            weights,
        ),
        out_specs=(weights, weights, weights, P(None, "fsdp", None)),
        check_vma=False,
    )
```

```python
import functools

import jax
import jax.numpy as jnp
from jax import lax
from jax.experimental import pallas as pl
from jax.experimental.pallas import tpu as pltpu
from jax.sharding import PartitionSpec as P

GROUPS = 12
D = 2432
BLOCK = 152
SLICE = 640
PATCH = 80
CHUNK = 16

eps_norm = 1e-06
clip_low = 0.8
clip_high = 1.2
spread_floor = 0.25
beta_one = 0.9
beta_two = 0.999
learn_rate = 0.001
weight_decay = 0.01
adam_eps = 1e-08
adam_count = 100.0

BF = jnp.bfloat16
F32 = jnp.float32
MESH = pl.DeviceIdType.MESH
COLS = (pl.ds(0, 1280), pl.ds(1280, 1152))
OUT_COLS = ((0, 384), (384, 256))
LAST = (((1,), (1,)), ((), ()))
FIRST = (((0,), (0,)), ((), ()))
N_SEND = 48
N_PAIR = 8
N_RECV = 167
N_LOCAL = 20


def gelu_parts(pre):
    root = 0.7978845608028654
    square = pre * pre
    t = jnp.tanh(root * (pre + 0.044715 * (square * pre)))
    cdf = 0.5 * (1.0 + t)
    slope = cdf + pre * (0.5 * (1.0 - t * t)) * (root * (1.0 + (3.0 * 0.044715) * square))
    return pre * cdf, slope


class Once:
    def __init__(self, wait):
        self.todo = wait

    def wait(self):
        if self.todo is not None:
            self.todo()
        self.todo = None


def kernel(
    rewards_h,
    group_ids_h,
    step_index_h,
    valid_steps_h,
    step_ratio_h,
    mask_h,
    mod_h,
    lat_h,
    stale_h,
    noise_h,
    par_h,
    m1_h,
    m2_h,
    o_par,
    o_m1,
    o_m2,
    o_roll,
    hid,
    bk,
    raw0,
    raw1,
    asm_up,
    asm_down,
    pre,
    act,
    sib_recv,
    y_send,
    y_recv,
    own,
    grad,
    x_recv,
    grad_own,
    b_send,
    b_recv,
    stale,
    noise,
    par,
    m1,
    m2,
    land,
    mask_col,
    stats,
    stats_recv,
    rewards,
    group_ids,
    step_index,
    valid_steps,
    step_ratio,
    mask_in,
    mod,
    send_sem,
    recv_sem,
    local_sem,
):
    roll = lax.axis_index("roll")
    fsdp = lax.axis_index("fsdp")
    y, c = roll // 2, lax.rem(roll, 2)
    x, z = fsdp // 4, lax.rem(fsdp, 4)

    def turn(a, by):
        return lax.rem(a + by, 4)

    def at(x_, y_, z_, c_):
        return (y_ * 2 + c_, x_ * 4 + z_)

    y_ring = [at(x, turn(y, j), z, c) for j in range(4)]
    x_ring = [at(turn(x, j), y, z, c) for j in range(4)]
    z_ring = [at(x, y, turn(z, j), c) for j in range(4)]
    sibling = at(x, y, z, 1 - c)
    y_plus, y_minus = y_ring[1], y_ring[3]

    barrier = pltpu.get_barrier_semaphore()
    partners = y_ring[1:] + x_ring[1:] + z_ring[1:] + [sibling]
    for partner in partners:
        pl.semaphore_signal(barrier, inc=1, device_id=partner, device_id_type=MESH)

    stage, fresh_id, spare, sends, moves = [0], [0], [], [], []

    def recv_id():
        if stage[0] == 2 and spare:
            return spare.pop(0)
        fresh_id[0] += 1
        if stage[0] == 0:
            spare.append(fresh_id[0] - 1)
        return fresh_id[0] - 1

    def push(src, dst, device, landed=None, log=None):
        i, n = recv_id(), len(sends)
        if n >= N_SEND:
            sends[n - N_SEND].wait()

        def describe(src, dst):
            return pltpu.make_async_remote_copy(
                src_ref=src,
                dst_ref=dst,
                send_sem=send_sem.at[n % N_SEND],
                recv_sem=recv_sem.at[i],
                device_id=device,
                device_id_type=MESH,
            )

        copy = describe(src, dst)
        copy.start()
        sends.append(Once(copy.wait_send))
        if log is not None:
            log.append(sends[-1])
        return copy if landed is None else describe(landed, landed)

    def move(src, dst):
        n = len(moves)
        if n >= N_LOCAL:
            moves[n - N_LOCAL].wait()
        copy = pltpu.make_async_copy(src, dst, local_sem.at[n % N_LOCAL])
        copy.start()
        moves.append(Once(copy.wait))
        return moves[-1]

    par_in = move(par_h, par)
    lat_in = [move(lat_h.at[s], y_send.at[s, 0]) for s in range(2)] + [move(mod_h, mod)]
    small_in = [
        move(rewards_h, rewards),
        move(group_ids_h, group_ids),
        move(step_index_h, step_index),
        move(valid_steps_h, valid_steps),
        move(step_ratio_h, step_ratio),
        move(mask_h, mask_in),
    ]

    raws = (raw0, raw1)
    near = (x_ring, z_ring)
    far = (z_ring, x_ring)
    near_at = (x, z)
    far_at = (z, x)

    par_in.wait()
    for m in range(2):
        raw0[m, z, x] = par[m, 0:80, :].astype(BF)
        raw1[m, x, z, 0:72, :] = par[m, 80:BLOCK, :].astype(BF)
        raw1[m, x, z, 64:80, :] = jnp.concatenate(
            [par[m, 144:BLOCK, :], jnp.zeros((8, SLICE), F32)], axis=0
        ).astype(BF)

    def each(n, body):
        def step(i, carry):
            body(i)
            return carry

        lax.fori_loop(0, n, step, 0)

    def modulated(s):
        shift = mod[0, s : s + 1, :]
        scaling = 1.0 + mod[1, s : s + 1, :]

        def body(i, carry):
            rows = pl.ds(pl.multiple_of(i * CHUNK, CHUNK), CHUNK)
            values = y_send[s, 0, rows, :].astype(F32)
            middle = jnp.sum(values, axis=-1, keepdims=True) / D
            centred = values - middle
            spread = jnp.sum(centred * centred, axis=-1, keepdims=True) / D
            normed = centred * lax.rsqrt(spread + eps_norm)
            hid[s, 0, 0, rows, :] = (normed * scaling + shift).astype(BF)
            return carry

        lax.fori_loop(0, PATCH // CHUNK, body, 0)

    pl.semaphore_wait(barrier, len(partners))

    first, second, weights_sent = {}, {}, []

    def near_own(m):
        for h in range(2):
            a, b = far_at[h], near_at[h]
            mine = raws[h].at[m, a, b]
            for k in (3, 1):
                first[m, h, k] = push(
                    mine, mine, near[h][4 - k], raws[h].at[m, a, turn(b, k)], log=weights_sent
                )

    def near_on(m):
        k = (3, 1)[m]
        for h in range(2):
            a, b = far_at[h], near_at[h]
            first[m, h, k].wait_recv()
            block = raws[h].at[m, a, turn(b, k)]
            first[m, h, 2] = push(
                block, block, near[h][4 - k], raws[h].at[m, a, turn(b, 2)], log=weights_sent
            )
        for h in range(2):
            first[m, h, 4 - k].wait_recv()

    def far_own(m, k):
        for h in range(2):
            a, b = far_at[h], turn(near_at[h], k)
            if k == 2:
                first[m, h, 2].wait_recv()
            block = raws[h].at[m, a, b]
            for side in (3, 1):
                second[m, h, k, side] = push(
                    block, block, far[h][4 - side], raws[h].at[m, turn(a, side), b], log=weights_sent
                )

    def far_on(m, k):
        side = 3 if k < 2 else 1
        for h in range(2):
            a, b = far_at[h], turn(near_at[h], k)
            second[m, h, k, side].wait_recv()
            block = raws[h].at[m, turn(a, side), b]
            second[m, h, k, 2] = push(
                block, block, far[h][4 - side], raws[h].at[m, turn(a, 2), b], log=weights_sent
            )

    near_own(0)
    stale_in = move(stale_h, stale)
    noise_in = move(noise_h, noise)
    m1_in = move(m1_h, m1)
    m2_in = move(m2_h, m2)
    for copy in lat_in:
        copy.wait()

    def gather_own(buf, s):
        mine = buf.at[s, 0, 0]
        left, right = buf.at[s, 0, 3], buf.at[s, 0, 1]
        lo, hi = COLS
        return {
            "left_lo": push(mine.at[:, lo], left.at[:, lo], y_plus),
            "right_hi": push(mine.at[:, hi], right.at[:, hi], y_minus),
            "left_hi": push(mine.at[:, hi], left.at[:, hi], y_plus),
            "right_lo": push(mine.at[:, lo], right.at[:, lo], y_minus),
            "sib0": push(mine, buf.at[s, 1, 0], sibling),
        }

    def gather_on(buf, s, d):
        left, right, across = buf.at[s, 0, 3], buf.at[s, 0, 1], buf.at[s, 0, 2]
        lo, hi = COLS
        d["left_lo"].wait_recv()
        d["across_lo"] = push(left.at[:, lo], across.at[:, lo], y_plus)
        d["right_hi"].wait_recv()
        d["across_hi"] = push(right.at[:, hi], across.at[:, hi], y_minus)

    def gather_near(buf, s, d):
        d["left_hi"].wait_recv()
        d["sib3"] = push(buf.at[s, 0, 3], buf.at[s, 1, 3], sibling)
        d["right_lo"].wait_recv()
        d["sib1"] = push(buf.at[s, 0, 1], buf.at[s, 1, 1], sibling)

    def gather_end(buf, s, d):
        d["across_lo"].wait_recv()
        d["across_hi"].wait_recv()
        d["sib2"] = push(buf.at[s, 0, 2], buf.at[s, 1, 2], sibling)

    def gather_sib(d):
        for j in range(4):
            d["sib%d" % j].wait_recv()

    def stats_send(step):
        ring = ([None, sibling], y_ring, x_ring, z_ring)[step]
        log = []
        return [
            push(stats, stats_recv.at[step, j], ring[j], log=log) for j in range(1, len(ring))
        ], log

    def stats_sum(step, copies):
        total = stats[...]
        for j, copy in enumerate(copies[0]):
            copy.wait_recv()
            total = total + stats_recv[step, j + 1]
        for copy in copies[1]:
            copy.wait()
        stats[...] = total

    def assemble(m, out):
        for h in range(2):
            for k in range(4):
                second[m, h, k, 1 if k < 2 else 3].wait_recv()
                second[m, h, k, 2].wait_recv()

        def body(i, carry):
            base = pl.multiple_of(i * (4 * BLOCK), CHUNK)
            parts = []
            for k in range(4):
                parts += [raw0[m, k, i], raw1[m, i, k, 0:72, :]]
            out[pl.ds(base, 4 * BLOCK), :] = jnp.concatenate(parts, axis=0)
            return carry

        lax.fori_loop(0, 4, body, 0)

    def forward(s, i):
        rows = hid[s, i].reshape(4 * PATCH, D)
        value = jnp.dot(rows, asm_up[0:D, :], preferred_element_type=F32)
        pre[s, i] = value
        act[s, i] = gelu_parts(value)[0].astype(BF)

    modulated(0)
    rows0 = gather_own(hid, 0)
    near_own(1)
    near_on(0)
    far_own(0, 1)
    far_own(0, 0)
    modulated(1)

    for copy in small_in:
        copy.wait()
    lane = lax.broadcasted_iota(jnp.int32, (1, 128), 1)
    valid = [jnp.where(step_index[s] < valid_steps[s], 1.0, 0.0).astype(F32) for s in range(2)]
    member = [jnp.where(lane == group_ids[s], 1.0, 0.0).astype(F32) for s in range(2)]
    stats[...] = jnp.zeros((8, 128), F32)
    stats[0:1, :] = member[0] * valid[0] + member[1] * valid[1]
    stats[1:2, :] = member[0] * (valid[0] * rewards[0]) + member[1] * (valid[1] * rewards[1])
    stats[2:3, :] = member[0] * (valid[0] * (rewards[0] * rewards[0])) + member[1] * (
        valid[1] * (rewards[1] * rewards[1])
    )
    stats[3:4, :] = jnp.zeros((1, 128), F32) + (valid[0] + valid[1])

    stats_copies = stats_send(0)
    gather_on(hid, 0, rows0)
    near_on(1)
    rows1 = gather_own(hid, 1)
    stats_sum(0, stats_copies)
    far_own(0, 3)
    far_own(0, 2)
    far_on(0, 1)
    far_own(1, 2)
    far_on(0, 2)
    far_on(0, 0)
    far_on(0, 3)
    far_own(1, 0)
    far_own(1, 3)
    gather_on(hid, 1, rows1)
    stats_copies = stats_send(1)
    gather_near(hid, 0, rows0)
    gather_end(hid, 0, rows0)
    far_on(1, 2)
    far_own(1, 1)
    assemble(0, asm_up)
    gather_sib(rows0)
    forward(0, 0)
    gather_near(hid, 1, rows1)
    far_on(1, 0)
    forward(0, 1)
    gather_end(hid, 1, rows1)
    far_on(1, 3)
    far_on(1, 1)
    gather_sib(rows1)
    each(2, lambda i: forward(1, i))
    assemble(1, asm_down)
    stage[0] = 1
    stats_sum(1, stats_copies)
    stats_copies = stats_send(2)

    def pair_copy(s, n):
        i = s * 4 + n
        return pltpu.make_async_remote_copy(
            src_ref=asm_up.at[pl.ds(pl.multiple_of((s * 4 + n) * 320, CHUNK), 320)],
            dst_ref=sib_recv.at[s, n],
            send_sem=send_sem.at[N_SEND + i],
            recv_sem=recv_sem.at[N_RECV + i],
            device_id=sibling,
            device_id_type=MESH,
        )

    def branch_tile(s, i, n):
        cols = pl.ds(pl.multiple_of(jnp.minimum(n * SLICE, D - SLICE), 128), SLICE)
        value = lax.dot_general(act[s, i], asm_down[cols, :], LAST, preferred_element_type=F32)
        return cols, value

    def branch_half(s, half):
        def away(q):
            n = 2 * half + q
            value = branch_tile(s, 1, n)[1]
            asm_up[pl.ds(pl.multiple_of((s * 4 + n) * 320, CHUNK), 320), :] = value.astype(BF)
            pair_copy(s, n).start()

        def mine(q):
            n = 2 * half + q
            cols, value = branch_tile(s, 0, n)
            pair_copy(s, n).wait()
            value = value + sib_recv[s, n].astype(F32)
            own[s, :, cols] = value[0:80]
            for j, k in ((2, 0), (1, 1), (3, 2)):
                y_send[s, k, :, cols] = value[j * 80 : j * 80 + 80].astype(BF)

        each(2, away)
        each(2, mine)

    def ring_start(send, recv, parts, plus, minus):
        lo, hi = parts
        return {
            "across_hi": push(hi(send, 0), hi(recv, 0), plus),
            "across_lo": push(lo(send, 0), lo(recv, 0), minus),
            "plus_lo": push(lo(send, 1), lo(recv, 1), plus),
            "minus_hi": push(hi(send, 2), hi(recv, 2), minus),
        }

    def ring_add(send, recv, parts, plus, minus, add, d):
        lo, hi = parts
        d["across_hi"].wait_recv()
        add(hi(send, 1), hi(recv, 0))
        d["plus_hi"] = push(hi(send, 1), hi(recv, 1), plus)
        d["across_lo"].wait_recv()
        add(lo(send, 2), lo(recv, 0))
        d["minus_lo"] = push(lo(send, 2), lo(recv, 2), minus)

    def ring_wait(d):
        for part in ("plus_lo", "minus_hi", "plus_hi", "minus_lo"):
            d[part].wait_recv()

    def add_rows(dst, src):
        def body(i, carry):
            rows = pl.ds(pl.multiple_of(i * CHUNK, CHUNK), CHUNK)
            dst[rows, :] = (dst[rows, :].astype(F32) + src[rows, :].astype(F32)).astype(BF)
            return carry

        lax.fori_loop(0, dst.shape[0] // CHUNK, body, 0)

    def add_blocks(dst, src):
        for k in range(2):
            dst[k] = (dst[k].astype(F32) + src[k].astype(F32)).astype(BF)

    col_parts = tuple((lambda ref, k, cols=cols: ref.at[k, :, cols]) for cols in COLS)

    def branch_push(s, half, d):
        lo, hi = col_parts
        send, recv = y_send.at[s], y_recv.at[s]
        if half == 1:
            d["across_hi"] = push(hi(send, 0), hi(recv, 0), y_plus)
            d["minus_hi"] = push(hi(send, 2), hi(recv, 2), y_minus)
        else:
            d["across_lo"] = push(lo(send, 0), lo(recv, 0), y_minus)
            d["plus_lo"] = push(lo(send, 1), lo(recv, 1), y_plus)

    def branch_add(s, half, d):
        part = col_parts[half]
        send, recv = y_send.at[s], y_recv.at[s]
        key, k, to = (("lo", 2, y_minus), ("hi", 1, y_plus))[half]
        d["across_" + key].wait_recv()
        add_rows(part(send, k), part(recv, 0))
        d[("minus_lo", "plus_hi")[half]] = push(part(send, k), part(recv, k), to)

    def back_rows(s, d):
        ring_wait(d)
        gate = 1.0 + mod[2, s : s + 1, :]
        factor = step_ratio[s]

        def err_body(i, total):
            rows = pl.ds(pl.multiple_of(i * CHUNK, CHUNK), CHUNK)
            branch = (
                own[s, rows, :] + y_recv[s, 1, rows, :].astype(F32) + y_recv[s, 2, rows, :].astype(F32)
            )
            velocity = gate * branch
            drawn = noise[s, rows, :].astype(F32)
            err = drawn + factor * (stale[s, rows, :].astype(F32) - velocity)
            own[s, rows, :] = err
            gap = jnp.sum(drawn * drawn - err * err, axis=1, keepdims=True)
            return total + mask_col[s, rows, 0:1] * gap

        gaps = lax.fori_loop(0, PATCH // CHUNK, err_body, jnp.zeros((CHUNK, 1), F32))
        logratio = jnp.sum(gaps, axis=0, keepdims=True) / (2.0 * npatch[s])
        safe = jnp.maximum(stats[0:1, :], 1.0)
        middle = stats[1:2, :] / safe
        variance = jnp.maximum(stats[2:3, :] / safe - middle * middle, 0.0)
        spread = jnp.maximum(jnp.sqrt(variance), spread_floor)
        own_mean = jnp.sum(member[s] * middle, axis=1, keepdims=True)
        own_spread = jnp.sum(member[s] * spread, axis=1, keepdims=True)
        advantage = (rewards[s] - own_mean) / own_spread
        ratio = jnp.exp(logratio)
        clipped = jnp.clip(ratio, clip_low, clip_high)
        active = jnp.where(ratio * advantage <= clipped * advantage, 1.0, 0.0).astype(F32)
        coef = -valid[s] * advantage * ratio * active / jnp.maximum(stats[3:4, 0:1], 1.0)
        per_patch = coef / npatch[s]

        def back_body(i, carry):
            rows = pl.ds(pl.multiple_of(i * CHUNK, CHUNK), CHUNK)
            scale = per_patch * mask_col[s, rows, 0:1] * factor
            bk[s, 0, 0, rows, :] = (gate * (scale * own[s, rows, :])).astype(BF)
            return carry

        lax.fori_loop(0, PATCH // CHUNK, back_body, 0)

    ring0, ring1 = {}, {}
    branch_half(0, 1)
    branch_push(0, 1, ring0)
    branch_half(0, 0)
    branch_push(0, 0, ring0)
    stats_sum(2, stats_copies)
    stats_copies = stats_send(3)

    diag = lax.broadcasted_iota(jnp.int32, (PATCH, PATCH), 0) == lax.broadcasted_iota(
        jnp.int32, (PATCH, PATCH), 1
    )
    npatch = []
    for s in range(2):
        row = jnp.broadcast_to(mask_in[s : s + 1, :].astype(F32), (PATCH, PATCH))
        column = jnp.sum(jnp.where(diag, row, 0.0), axis=1, keepdims=True)
        mask_col[s] = jnp.broadcast_to(column, (PATCH, 128))
        npatch.append(jnp.maximum(jnp.sum(column, axis=0, keepdims=True), 1.0))

    branch_half(1, 1)
    branch_push(1, 1, ring1)
    branch_add(0, 1, ring0)
    branch_half(1, 0)
    branch_push(1, 0, ring1)
    branch_add(0, 0, ring0)
    stats_sum(3, stats_copies)
    stale_in.wait()
    noise_in.wait()
    branch_add(1, 1, ring1)
    branch_add(1, 0, ring1)
    back_rows(0, ring0)
    stage[0] = 2
    back0 = gather_own(bk, 0)
    back_rows(1, ring1)
    gather_on(bk, 0, back0)
    back1 = gather_own(bk, 1)
    gather_near(bk, 0, back0)
    gather_end(bk, 0, back0)
    gather_sib(back0)

    def back_pre(s):
        def body(i, carry):
            rows = bk[s, i].reshape(4 * PATCH, D)
            value = jnp.dot(rows, asm_down[...], preferred_element_type=F32)
            act[s, i] = (value * gelu_parts(pre[s, i])[1]).astype(BF)
            return carry

        lax.fori_loop(0, 2, body, 0)

    PARTS = ((1, 0, 256), (1, 256, 384), (0, 0, 256), (0, 256, 256), (0, 512, 128))
    final = len(PARTS) - 1

    def over_width(body):
        each(3, lambda n: body(pl.multiple_of(n * SLICE, 128), SLICE))
        body(3 * SLICE, D - 3 * SLICE)

    def grad_part(rows, s, at_, wide, start, width):
        left = rows[s, :, :, :, pl.ds(at_, wide)].reshape(8 * PATCH, wide)
        right = act[s, :, :, start : start + width].reshape(8 * PATCH, width)
        return lax.dot_general(left, right, FIRST, preferred_element_type=F32)

    def grad_rows(p, h, j, k):
        a, b = turn(far_at[h], j), turn(near_at[h], k)
        block = (b * 4 + a) if h == 0 else (a * 4 + b)
        rows = pl.ds(pl.multiple_of(block * BLOCK + 80 * h, 8), 80)
        return grad[rows, PARTS[p][1] : PARTS[p][1] + PARTS[p][2]]

    def block_parts(p):
        cols = pl.ds(PARTS[p][1], PARTS[p][2])
        return tuple((lambda ref, k, i=i: ref.at[k, pl.ds(i, 2), :, cols]) for i in (0, 2))

    def far_ring(p, h):
        m = PARTS[p][0]
        return raws[h].at[m], x_recv.at[m, h], block_parts(p), far[h][1], far[h][3]

    def far_start(p):
        m, start, width = PARTS[p]
        cols = slice(start, start + width)

        def away(k):
            for h in range(2):
                for j, slot in ((2, 0), (1, 1), (3, 2)):
                    raws[h][m, slot, k, :, cols] = grad_rows(p, h, j, k).astype(BF)

        def mine(k):
            for h in range(2):
                grad_own[m, h, k, :, cols] = grad_rows(p, h, 0, k)

        each(4, away)
        out = [ring_start(*far_ring(p, h)) for h in range(2)]
        each(4, mine)
        return out

    def far_add(p, d):
        for h in range(2):
            ring_add(*far_ring(p, h), add_blocks, d[h])

    def near_start(p, d):
        m, start, width = PARTS[p]
        cols = slice(start, start + width)
        out = []
        for h in range(2):
            ring_wait(d[h])

            def total(k):
                return (
                    grad_own[m, h, k, :, cols]
                    + x_recv[m, h, 1, k, :, cols].astype(F32)
                    + x_recv[m, h, 2, k, :, cols].astype(F32)
                )

            def away(k):
                b_send[m, h, k, :, cols] = total(k + 1).astype(BF)

            each(3, away)
            send, recv = b_send.at[m, h], b_recv.at[m, h]
            part = pl.ds(start, width)
            out += [
                push(send.at[k, :, part], recv.at[k, :, part], near[h][k + 1]) for k in (1, 0, 2)
            ]
            grad_own[m, h, 0, :, cols] = total(0)
        return out

    def out_cols(owner, start, width):
        return pl.ds(pl.multiple_of(owner * SLICE + start, 128), width)

    def update(p, d):
        m, start, width = PARTS[p]
        for copy in d:
            copy.wait_recv()

        def columns(n, h):
            cols = pl.ds(pl.multiple_of(start + n * 128, 128), 128)
            rows = slice(0, 80) if h == 0 else slice(80, BLOCK)
            high = 80 if h == 0 else 72
            grads = (
                grad_own[m, h, 0, 0:high, cols]
                + b_recv[m, h, 0, 0:high, cols].astype(F32)
                + b_recv[m, h, 1, 0:high, cols].astype(F32)
                + b_recv[m, h, 2, 0:high, cols].astype(F32)
            )
            weights = par[m, rows, cols]
            new_first = beta_one * m1[m, rows, cols] + (1.0 - beta_one) * grads
            new_second = beta_two * m2[m, rows, cols] + (1.0 - beta_two) * grads * grads
            first_hat = new_first / (1.0 - beta_one**adam_count)
            second_hat = new_second / (1.0 - beta_two**adam_count)
            step = first_hat / (jnp.sqrt(second_hat) + adam_eps) + weight_decay * weights
            new_weights = weights - learn_rate * step
            m1[m, rows, cols] = new_first
            m2[m, rows, cols] = new_second
            par[m, rows, cols] = new_weights
            land[m, 0, rows, cols] = new_weights.astype(BF)

        for h in range(2):
            each(width // 128, functools.partial(columns, h=h))
        mine = land.at[m, 0, :, pl.ds(start, width)]

        def slot(j, k):
            return land.at[m, 2 * j + k, :, pl.ds(start, width)]

        d = {
            "left": push(mine, slot(3, 0), y_plus),
            "right": push(mine, slot(1, 0), y_minus),
            "sib0": push(mine, slot(0, 1), sibling),
        }
        if p == final:
            d["across"] = push(mine, slot(2, 0), y_ring[2])
        out_store(p, 0, 0)
        if p in (1, final):
            move(m1.at[m], o_m1.at[m])
            move(m2.at[m], o_m2.at[m])
            move(par.at[m], o_par.at[m])
        return d

    def out_store(p, j, k):
        m, start, width = PARTS[p]
        owner = turn(y, j) * 2 + (c if k == 0 else 1 - c)
        block = land.at[m, 2 * j + k, :, pl.ds(start, width)]
        move(block, o_roll.at[m, :, out_cols(owner, start, width)])

    def out_on(p, d):
        m, start, width = PARTS[p]
        half = 128 * ((width // 128 + 1) // 2)
        for key, j, to, at_, wide in (
            ("left", 3, y_plus, start, half),
            ("right", 1, y_minus, start + half, width - half),
        ):
            d[key].wait_recv()
            cols = pl.ds(at_, wide)
            if p != final:
                d[key, "across"] = push(land.at[m, 2 * j, :, cols], land.at[m, 4, :, cols], to)
            cols = pl.ds(start, width)
            d[key, "sib"] = push(
                land.at[m, 2 * j, :, cols], land.at[m, 2 * j + 1, :, cols], sibling
            )
            out_store(p, j, 0)

    def out_end(p, d):
        m, start, width = PARTS[p]
        for key in (("across",) if p == final else (("left", "across"), ("right", "across"))):
            d[key].wait_recv()
        cols = pl.ds(start, width)
        d["sib2"] = push(land.at[m, 4, :, cols], land.at[m, 5, :, cols], sibling)
        out_store(p, 2, 0)

    def out_sib(p, d):
        d["sib0"].wait_recv()
        out_store(p, 0, 1)
        d["left", "sib"].wait_recv()
        out_store(p, 3, 1)
        d["right", "sib"].wait_recv()
        out_store(p, 1, 1)
        d["sib2"].wait_recv()
        out_store(p, 2, 1)

    for copy in weights_sent:
        copy.wait()
    grad[pl.ds(D, 8), :] = jnp.zeros((8, SLICE), F32)

    def first_rows(at_, wide):
        grad[pl.ds(at_, wide), :] = grad_part(bk, 0, at_, wide, 0, SLICE)

    over_width(first_rows)
    gather_on(bk, 1, back1)
    back_pre(0)
    gather_near(bk, 1, back1)
    gather_end(bk, 1, back1)
    gather_sib(back1)

    def down_part(p):
        start, width = PARTS[p][1:]

        def body(at_, wide):
            cols = slice(start, start + width)
            grad[pl.ds(at_, wide), cols] += grad_part(bk, 1, at_, wide, start, width)

        over_width(body)

    def up_part(p):
        start, width = PARTS[p][1:]

        def body(at_, wide):
            grad[pl.ds(at_, wide), start : start + width] = grad_part(
                hid, 0, at_, wide, start, width
            ) + grad_part(hid, 1, at_, wide, start, width)

        over_width(body)

    down_part(0)
    far0 = far_start(0)
    down_part(1)
    far1 = far_start(1)
    back_pre(1)
    far_add(0, far0)
    up_part(2)
    far_add(1, far1)
    far2 = far_start(2)
    up_part(3)
    far3 = far_start(3)
    up_part(4)
    far4 = far_start(4)
    near0 = near_start(0, far0)
    near1 = near_start(1, far1)
    far_add(2, far2)
    m1_in.wait()
    m2_in.wait()
    far_add(3, far3)
    far_add(4, far4)
    out0 = update(0, near0)
    out1 = update(1, near1)
    near2 = near_start(2, far2)
    near3 = near_start(3, far3)
    out_on(0, out0)
    near4 = near_start(4, far4)
    out2 = update(2, near2)
    out_on(1, out1)
    out3 = update(3, near3)
    out_end(0, out0)
    out4 = update(4, near4)
    out_end(1, out1)
    out_on(2, out2)
    out_on(3, out3)
    out_end(2, out2)
    out_on(4, out4)
    out_end(3, out3)
    out_end(4, out4)
    for p, out in enumerate((out0, out1, out2, out3, out4)):
        out_sib(p, out)
    assert fresh_id[0] <= N_RECV, fresh_id[0]
    for copy in moves + sends:
        copy.wait()


def settle(*refs):
    sources, targets, held, sem = refs[:4], refs[4:8], refs[8:12], refs[12]
    pieces = [(i, m) for i in (3, 0, 1, 2) for m in range(2)]
    reads, writes = [], []
    for n, (i, m) in enumerate(pieces):
        there, here = sources[i].at[m], held[i].at[m]
        reads.append(pltpu.make_async_copy(there, here, sem.at[n]))
        reads[-1].start()
    for n, (i, m) in enumerate(pieces):
        reads[n].wait()
        here, there = held[i].at[m], targets[i].at[m]
        writes.append(pltpu.make_async_copy(here, there, sem.at[len(pieces) + n]))
        writes[-1].start()
    for write in writes:
        write.wait()


def per_device(
    latents,
    stale_velocity,
    noise,
    modulation,
    step_ratio,
    rewards,
    group_ids,
    step_index,
    valid_steps,
    patch_mask,
    params,
    first_moment,
    second_moment,
):
    any_ = pl.BlockSpec(memory_space=pl.ANY)
    shard = jax.ShapeDtypeStruct(params.shape, F32)
    outs = pl.pallas_call(
        kernel,
        out_shape=(shard, shard, shard, jax.ShapeDtypeStruct((2, BLOCK, 8 * SLICE), BF)),
        in_specs=[any_] * 13,
        out_specs=(any_,) * 4,
        scratch_shapes=[
            pltpu.VMEM((2, 2, 4, PATCH, D), BF),
            pltpu.VMEM((2, 2, 4, PATCH, D), BF),
            pltpu.VMEM((2, 4, 4, 80, SLICE), BF),
            pltpu.VMEM((2, 4, 4, 80, SLICE), BF),
            pltpu.VMEM((2560, SLICE), BF),
            pltpu.VMEM((D, SLICE), BF),
            pltpu.VMEM((2, 2, 4 * PATCH, SLICE), F32),
            pltpu.VMEM((2, 2, 4 * PATCH, SLICE), BF),
            pltpu.VMEM((2, 4, 4 * PATCH, SLICE), BF),
            pltpu.VMEM((2, 3, PATCH, D), BF),
            pltpu.VMEM((2, 3, PATCH, D), BF),
            pltpu.VMEM((2, PATCH, D), F32),
            pltpu.VMEM((D + 8, SLICE), F32),
            pltpu.VMEM((2, 2, 3, 4, 80, SLICE), BF),
            pltpu.VMEM((2, 2, 4, 80, SLICE), F32),
            pltpu.VMEM((2, 2, 3, 80, SLICE), BF),
            pltpu.VMEM((2, 2, 3, 80, SLICE), BF),
            pltpu.VMEM((2, PATCH, D), BF),
            pltpu.VMEM((2, PATCH, D), BF),
            pltpu.VMEM((2, BLOCK, SLICE), F32),
            pltpu.VMEM((2, BLOCK, SLICE), F32),
            pltpu.VMEM((2, BLOCK, SLICE), F32),
            pltpu.VMEM((2, 8, BLOCK, SLICE), BF),
            pltpu.VMEM((2, PATCH, 128), F32),
            pltpu.VMEM((8, 128), F32),
            pltpu.VMEM((4, 4, 8, 128), F32),
            pltpu.SMEM((2,), F32),
            pltpu.SMEM((2,), jnp.int32),
            pltpu.SMEM((2,), jnp.int32),
            pltpu.SMEM((2,), jnp.int32),
            pltpu.SMEM((2,), F32),
            pltpu.VMEM((2, PATCH), jnp.int32),
            pltpu.VMEM((3, 2, D), F32),
            pltpu.SemaphoreType.DMA((N_SEND + N_PAIR,)),
            pltpu.SemaphoreType.DMA((N_RECV + N_PAIR,)),
            pltpu.SemaphoreType.DMA((N_LOCAL,)),
        ],
        compiler_params=pltpu.CompilerParams(
            collective_id=0, has_side_effects=True, vmem_limit_bytes=63 << 20
        ),
    )(
        rewards,
        group_ids,
        step_index,
        valid_steps,
        step_ratio,
        patch_mask,
        modulation.transpose(1, 0, 2),
        latents,
        stale_velocity,
        noise,
        params,
        first_moment,
        second_moment,
    )
    return tuple(
        pl.pallas_call(
            settle,
            out_shape=tuple(jax.ShapeDtypeStruct(o.shape, o.dtype) for o in outs),
            in_specs=[any_] * 4,
            out_specs=(any_,) * 4,
            scratch_shapes=[pltpu.VMEM(o.shape, o.dtype) for o in outs]
            + [pltpu.SemaphoreType.DMA((16,))],
        )(*outs)
    )


def solution(mesh):
    rows = ("roll", "fsdp")
    weights = P(None, "fsdp", "roll")
    return jax.shard_map(
        per_device,
        mesh=mesh,
        in_specs=(
            P(rows, None, None),
            P(rows, None, None),
            P(rows, None, None),
            P(rows, None, None),
            P(rows),
            P(rows),
            P(rows),
            P(rows),
            P(rows),
            P(rows, None),
            weights,
            weights,
            weights,
        ),
        out_specs=(weights, weights, weights, P(None, "fsdp", None)),
        check_vma=False,
    )
```

```python
import functools

import jax
import jax.numpy as jnp
from jax import lax
from jax.experimental import pallas as pl
from jax.experimental.pallas import tpu as pltpu
from jax.sharding import PartitionSpec as P

GROUPS = 12
D = 2432
BLOCK = 152
SLICE = 640
PATCH = 80
CHUNK = 16

eps_norm = 1e-06
clip_low = 0.8
clip_high = 1.2
spread_floor = 0.25
beta_one = 0.9
beta_two = 0.999
learn_rate = 0.001
weight_decay = 0.01
adam_eps = 1e-08
adam_count = 100.0

BF = jnp.bfloat16
F32 = jnp.float32
MESH = pl.DeviceIdType.MESH
COLS = (pl.ds(0, 1280), pl.ds(1280, 1152))
OUT_COLS = ((0, 384), (384, 256))
LAST = (((1,), (1,)), ((), ()))
FIRST = (((0,), (0,)), ((), ()))
N_SEND = 48
N_PAIR = 8
N_RECV = 167
N_LOCAL = 20


def gelu_parts(pre):
    root = 0.7978845608028654
    square = pre * pre
    t = jnp.tanh(root * (pre + 0.044715 * (square * pre)))
    cdf = 0.5 * (1.0 + t)
    slope = cdf + pre * (0.5 * (1.0 - t * t)) * (root * (1.0 + (3.0 * 0.044715) * square))
    return pre * cdf, slope


class Once:
    def __init__(self, wait):
        self.todo = wait

    def wait(self):
        if self.todo is not None:
            self.todo()
        self.todo = None


def kernel(
    rewards_h,
    group_ids_h,
    step_index_h,
    valid_steps_h,
    step_ratio_h,
    mask_h,
    mod_h,
    lat_h,
    stale_h,
    noise_h,
    par_h,
    m1_h,
    m2_h,
    o_par,
    o_m1,
    o_m2,
    o_roll,
    hid,
    bk,
    raw0,
    raw1,
    asm_up,
    asm_down,
    pre,
    act,
    sib_recv,
    y_send,
    y_recv,
    own,
    grad,
    x_recv,
    grad_own,
    b_send,
    b_recv,
    stale,
    noise,
    par,
    m1,
    m2,
    land,
    mask_col,
    stats,
    stats_recv,
    rewards,
    group_ids,
    step_index,
    valid_steps,
    step_ratio,
    mask_in,
    mod,
    send_sem,
    recv_sem,
    local_sem,
):
    roll = lax.axis_index("roll")
    fsdp = lax.axis_index("fsdp")
    y, c = roll // 2, lax.rem(roll, 2)
    x, z = fsdp // 4, lax.rem(fsdp, 4)

    def turn(a, by):
        return lax.rem(a + by, 4)

    def at(x_, y_, z_, c_):
        return (y_ * 2 + c_, x_ * 4 + z_)

    y_ring = [at(x, turn(y, j), z, c) for j in range(4)]
    x_ring = [at(turn(x, j), y, z, c) for j in range(4)]
    z_ring = [at(x, y, turn(z, j), c) for j in range(4)]
    sibling = at(x, y, z, 1 - c)
    y_plus, y_minus = y_ring[1], y_ring[3]

    barrier = pltpu.get_barrier_semaphore()
    partners = y_ring[1:] + x_ring[1:] + z_ring[1:] + [sibling]
    for partner in partners:
        pl.semaphore_signal(barrier, inc=1, device_id=partner, device_id_type=MESH)

    stage, fresh_id, spare, sends, moves = [0], [0], [], [], []

    def recv_id():
        if stage[0] == 2 and spare:
            return spare.pop(0)
        fresh_id[0] += 1
        if stage[0] == 0:
            spare.append(fresh_id[0] - 1)
        return fresh_id[0] - 1

    def push(src, dst, device, landed=None, log=None):
        i, n = recv_id(), len(sends)
        if n >= N_SEND:
            sends[n - N_SEND].wait()

        def describe(src, dst):
            return pltpu.make_async_remote_copy(
                src_ref=src,
                dst_ref=dst,
                send_sem=send_sem.at[n % N_SEND],
                recv_sem=recv_sem.at[i],
                device_id=device,
                device_id_type=MESH,
            )

        copy = describe(src, dst)
        copy.start()
        sends.append(Once(copy.wait_send))
        if log is not None:
            log.append(sends[-1])
        return copy if landed is None else describe(landed, landed)

    def move(src, dst):
        n = len(moves)
        if n >= N_LOCAL:
            moves[n - N_LOCAL].wait()
        copy = pltpu.make_async_copy(src, dst, local_sem.at[n % N_LOCAL])
        copy.start()
        moves.append(Once(copy.wait))
        return moves[-1]

    par_in = move(par_h, par)
    lat_in = [move(lat_h.at[s], y_send.at[s, 0]) for s in range(2)] + [move(mod_h, mod)]
    small_in = [
        move(rewards_h, rewards),
        move(group_ids_h, group_ids),
        move(step_index_h, step_index),
        move(valid_steps_h, valid_steps),
        move(step_ratio_h, step_ratio),
        move(mask_h, mask_in),
    ]

    raws = (raw0, raw1)
    near = (x_ring, z_ring)
    far = (z_ring, x_ring)
    near_at = (x, z)
    far_at = (z, x)

    par_in.wait()
    for m in range(2):
        raw0[m, z, x] = par[m, 0:80, :].astype(BF)
        raw1[m, x, z, 0:72, :] = par[m, 80:BLOCK, :].astype(BF)
        raw1[m, x, z, 64:80, :] = jnp.concatenate(
            [par[m, 144:BLOCK, :], jnp.zeros((8, SLICE), F32)], axis=0
        ).astype(BF)

    def each(n, body):
        def step(i, carry):
            body(i)
            return carry

        lax.fori_loop(0, n, step, 0)

    def modulated(s):
        shift = mod[0, s : s + 1, :]
        scaling = 1.0 + mod[1, s : s + 1, :]

        def body(i, carry):
            rows = pl.ds(pl.multiple_of(i * CHUNK, CHUNK), CHUNK)
            values = y_send[s, 0, rows, :].astype(F32)
            middle = jnp.sum(values, axis=-1, keepdims=True) / D
            centred = values - middle
            spread = jnp.sum(centred * centred, axis=-1, keepdims=True) / D
            normed = centred * lax.rsqrt(spread + eps_norm)
            hid[s, 0, 0, rows, :] = (normed * scaling + shift).astype(BF)
            return carry

        lax.fori_loop(0, PATCH // CHUNK, body, 0)

    pl.semaphore_wait(barrier, len(partners))

    first, second, weights_sent = {}, {}, []

    def near_own(m):
        for h in range(2):
            a, b = far_at[h], near_at[h]
            mine = raws[h].at[m, a, b]
            for k in (3, 1):
                first[m, h, k] = push(
                    mine, mine, near[h][4 - k], raws[h].at[m, a, turn(b, k)], log=weights_sent
                )

    def near_on(m):
        k = (3, 1)[m]
        for h in range(2):
            a, b = far_at[h], near_at[h]
            first[m, h, k].wait_recv()
            block = raws[h].at[m, a, turn(b, k)]
            first[m, h, 2] = push(
                block, block, near[h][4 - k], raws[h].at[m, a, turn(b, 2)], log=weights_sent
            )
        for h in range(2):
            first[m, h, 4 - k].wait_recv()

    def far_own(m, k):
        for h in range(2):
            a, b = far_at[h], turn(near_at[h], k)
            if k == 2:
                first[m, h, 2].wait_recv()
            block = raws[h].at[m, a, b]
            for side in (3, 1):
                second[m, h, k, side] = push(
                    block, block, far[h][4 - side], raws[h].at[m, turn(a, side), b], log=weights_sent
                )

    def far_on(m, k):
        side = 3 if k < 2 else 1
        for h in range(2):
            a, b = far_at[h], turn(near_at[h], k)
            second[m, h, k, side].wait_recv()
            block = raws[h].at[m, turn(a, side), b]
            second[m, h, k, 2] = push(
                block, block, far[h][4 - side], raws[h].at[m, turn(a, 2), b], log=weights_sent
            )

    near_own(0)
    stale_in = move(stale_h, stale)
    noise_in = move(noise_h, noise)
    m1_in = move(m1_h, m1)
    m2_in = move(m2_h, m2)
    for copy in lat_in:
        copy.wait()

    def gather_own(buf, s):
        mine = buf.at[s, 0, 0]
        left, right = buf.at[s, 0, 3], buf.at[s, 0, 1]
        lo, hi = COLS
        return {
            "left_lo": push(mine.at[:, lo], left.at[:, lo], y_plus),
            "right_hi": push(mine.at[:, hi], right.at[:, hi], y_minus),
            "left_hi": push(mine.at[:, hi], left.at[:, hi], y_plus),
            "right_lo": push(mine.at[:, lo], right.at[:, lo], y_minus),
            "sib0": push(mine, buf.at[s, 1, 0], sibling),
        }

    def gather_on(buf, s, d):
        left, right, across = buf.at[s, 0, 3], buf.at[s, 0, 1], buf.at[s, 0, 2]
        lo, hi = COLS
        d["left_lo"].wait_recv()
        d["across_lo"] = push(left.at[:, lo], across.at[:, lo], y_plus)
        d["right_hi"].wait_recv()
        d["across_hi"] = push(right.at[:, hi], across.at[:, hi], y_minus)

    def gather_near(buf, s, d):
        d["left_hi"].wait_recv()
        d["sib3"] = push(buf.at[s, 0, 3], buf.at[s, 1, 3], sibling)
        d["right_lo"].wait_recv()
        d["sib1"] = push(buf.at[s, 0, 1], buf.at[s, 1, 1], sibling)

    def gather_end(buf, s, d):
        d["across_lo"].wait_recv()
        d["across_hi"].wait_recv()
        d["sib2"] = push(buf.at[s, 0, 2], buf.at[s, 1, 2], sibling)

    def gather_sib(d):
        for j in range(4):
            d["sib%d" % j].wait_recv()

    def stats_send(step):
        ring = ([None, sibling], y_ring, x_ring, z_ring)[step]
        log = []
        return [
            push(stats, stats_recv.at[step, j], ring[j], log=log) for j in range(1, len(ring))
        ], log

    def stats_sum(step, copies):
        total = stats[...]
        for j, copy in enumerate(copies[0]):
            copy.wait_recv()
            total = total + stats_recv[step, j + 1]
        for copy in copies[1]:
            copy.wait()
        stats[...] = total

    def assemble(m, out):
        for h in range(2):
            for k in range(4):
                second[m, h, k, 1 if k < 2 else 3].wait_recv()
                second[m, h, k, 2].wait_recv()

        def body(i, carry):
            base = pl.multiple_of(i * (4 * BLOCK), CHUNK)
            parts = []
            for k in range(4):
                parts += [raw0[m, k, i], raw1[m, i, k, 0:72, :]]
            out[pl.ds(base, 4 * BLOCK), :] = jnp.concatenate(parts, axis=0)
            return carry

        lax.fori_loop(0, 4, body, 0)

    def forward(s, i):
        rows = hid[s, i].reshape(4 * PATCH, D)
        value = jnp.dot(rows, asm_up[0:D, :], preferred_element_type=F32)
        pre[s, i] = value
        act[s, i] = gelu_parts(value)[0].astype(BF)

    modulated(0)
    rows0 = gather_own(hid, 0)
    near_own(1)
    near_on(0)
    far_own(0, 1)
    far_own(0, 0)
    modulated(1)

    for copy in small_in:
        copy.wait()
    lane = lax.broadcasted_iota(jnp.int32, (1, 128), 1)
    valid = [jnp.where(step_index[s] < valid_steps[s], 1.0, 0.0).astype(F32) for s in range(2)]
    member = [jnp.where(lane == group_ids[s], 1.0, 0.0).astype(F32) for s in range(2)]
    stats[...] = jnp.zeros((8, 128), F32)
    stats[0:1, :] = member[0] * valid[0] + member[1] * valid[1]
    stats[1:2, :] = member[0] * (valid[0] * rewards[0]) + member[1] * (valid[1] * rewards[1])
    stats[2:3, :] = member[0] * (valid[0] * (rewards[0] * rewards[0])) + member[1] * (
        valid[1] * (rewards[1] * rewards[1])
    )
    stats[3:4, :] = jnp.zeros((1, 128), F32) + (valid[0] + valid[1])

    stats_copies = stats_send(0)
    gather_on(hid, 0, rows0)
    near_on(1)
    rows1 = gather_own(hid, 1)
    stats_sum(0, stats_copies)
    far_own(0, 3)
    far_own(0, 2)
    far_on(0, 1)
    far_own(1, 2)
    far_on(0, 2)
    far_on(0, 0)
    far_on(0, 3)
    far_own(1, 0)
    far_own(1, 3)
    gather_on(hid, 1, rows1)
    stats_copies = stats_send(1)
    gather_near(hid, 0, rows0)
    gather_end(hid, 0, rows0)
    far_on(1, 2)
    far_own(1, 1)
    assemble(0, asm_up)
    gather_sib(rows0)
    forward(0, 0)
    gather_near(hid, 1, rows1)
    far_on(1, 0)
    forward(0, 1)
    gather_end(hid, 1, rows1)
    far_on(1, 3)
    far_on(1, 1)
    gather_sib(rows1)
    each(2, lambda i: forward(1, i))
    assemble(1, asm_down)
    stage[0] = 1
    stats_sum(1, stats_copies)
    stats_copies = stats_send(2)

    def pair_copy(s, n):
        i = s * 4 + n
        return pltpu.make_async_remote_copy(
            src_ref=asm_up.at[pl.ds(pl.multiple_of((s * 4 + n) * 320, CHUNK), 320)],
            dst_ref=sib_recv.at[s, n],
            send_sem=send_sem.at[N_SEND + i],
            recv_sem=recv_sem.at[N_RECV + i],
            device_id=sibling,
            device_id_type=MESH,
        )

    def branch_tile(s, i, n):
        cols = pl.ds(pl.multiple_of(jnp.minimum(n * SLICE, D - SLICE), 128), SLICE)
        value = lax.dot_general(act[s, i], asm_down[cols, :], LAST, preferred_element_type=F32)
        return cols, value

    def branch_half(s, half):
        def away(q):
            n = 2 * half + q
            value = branch_tile(s, 1, n)[1]
            asm_up[pl.ds(pl.multiple_of((s * 4 + n) * 320, CHUNK), 320), :] = value.astype(BF)
            pair_copy(s, n).start()

        def mine(q):
            n = 2 * half + q
            cols, value = branch_tile(s, 0, n)
            pair_copy(s, n).wait()
            value = value + sib_recv[s, n].astype(F32)
            own[s, :, cols] = value[0:80]
            for j, k in ((2, 0), (1, 1), (3, 2)):
                y_send[s, k, :, cols] = value[j * 80 : j * 80 + 80].astype(BF)

        each(2, away)
        each(2, mine)

    def ring_start(send, recv, parts, plus, minus):
        lo, hi = parts
        return {
            "across_hi": push(hi(send, 0), hi(recv, 0), plus),
            "across_lo": push(lo(send, 0), lo(recv, 0), minus),
            "plus_lo": push(lo(send, 1), lo(recv, 1), plus),
            "minus_hi": push(hi(send, 2), hi(recv, 2), minus),
        }

    def ring_add(send, recv, parts, plus, minus, add, d):
        lo, hi = parts
        d["across_hi"].wait_recv()
        add(hi(send, 1), hi(recv, 0))
        d["plus_hi"] = push(hi(send, 1), hi(recv, 1), plus)
        d["across_lo"].wait_recv()
        add(lo(send, 2), lo(recv, 0))
        d["minus_lo"] = push(lo(send, 2), lo(recv, 2), minus)

    def ring_wait(d):
        for part in ("plus_lo", "minus_hi", "plus_hi", "minus_lo"):
            d[part].wait_recv()

    def add_rows(dst, src):
        def body(i, carry):
            rows = pl.ds(pl.multiple_of(i * CHUNK, CHUNK), CHUNK)
            dst[rows, :] = (dst[rows, :].astype(F32) + src[rows, :].astype(F32)).astype(BF)
            return carry

        lax.fori_loop(0, dst.shape[0] // CHUNK, body, 0)

    def add_blocks(dst, src):
        for k in range(2):
            dst[k] = (dst[k].astype(F32) + src[k].astype(F32)).astype(BF)

    col_parts = tuple((lambda ref, k, cols=cols: ref.at[k, :, cols]) for cols in COLS)

    def branch_push(s, half, d):
        lo, hi = col_parts
        send, recv = y_send.at[s], y_recv.at[s]
        if half == 1:
            d["across_hi"] = push(hi(send, 0), hi(recv, 0), y_plus)
            d["minus_hi"] = push(hi(send, 2), hi(recv, 2), y_minus)
        else:
            d["across_lo"] = push(lo(send, 0), lo(recv, 0), y_minus)
            d["plus_lo"] = push(lo(send, 1), lo(recv, 1), y_plus)

    def branch_add(s, half, d):
        part = col_parts[half]
        send, recv = y_send.at[s], y_recv.at[s]
        key, k, to = (("lo", 2, y_minus), ("hi", 1, y_plus))[half]
        d["across_" + key].wait_recv()
        add_rows(part(send, k), part(recv, 0))
        d[("minus_lo", "plus_hi")[half]] = push(part(send, k), part(recv, k), to)

    def back_rows(s, d):
        ring_wait(d)
        gate = 1.0 + mod[2, s : s + 1, :]
        factor = step_ratio[s]

        def err_body(i, total):
            rows = pl.ds(pl.multiple_of(i * CHUNK, CHUNK), CHUNK)
            branch = (
                own[s, rows, :] + y_recv[s, 1, rows, :].astype(F32) + y_recv[s, 2, rows, :].astype(F32)
            )
            velocity = gate * branch
            drawn = noise[s, rows, :].astype(F32)
            err = drawn + factor * (stale[s, rows, :].astype(F32) - velocity)
            own[s, rows, :] = err
            gap = jnp.sum(drawn * drawn - err * err, axis=1, keepdims=True)
            return total + mask_col[s, rows, 0:1] * gap

        gaps = lax.fori_loop(0, PATCH // CHUNK, err_body, jnp.zeros((CHUNK, 1), F32))
        logratio = jnp.sum(gaps, axis=0, keepdims=True) / (2.0 * npatch[s])
        safe = jnp.maximum(stats[0:1, :], 1.0)
        middle = stats[1:2, :] / safe
        variance = jnp.maximum(stats[2:3, :] / safe - middle * middle, 0.0)
        spread = jnp.maximum(jnp.sqrt(variance), spread_floor)
        own_mean = jnp.sum(member[s] * middle, axis=1, keepdims=True)
        own_spread = jnp.sum(member[s] * spread, axis=1, keepdims=True)
        advantage = (rewards[s] - own_mean) / own_spread
        ratio = jnp.exp(logratio)
        clipped = jnp.clip(ratio, clip_low, clip_high)
        active = jnp.where(ratio * advantage <= clipped * advantage, 1.0, 0.0).astype(F32)
        coef = -valid[s] * advantage * ratio * active / jnp.maximum(stats[3:4, 0:1], 1.0)
        per_patch = coef / npatch[s]

        def back_body(i, carry):
            rows = pl.ds(pl.multiple_of(i * CHUNK, CHUNK), CHUNK)
            scale = per_patch * mask_col[s, rows, 0:1] * factor
            bk[s, 0, 0, rows, :] = (gate * (scale * own[s, rows, :])).astype(BF)
            return carry

        lax.fori_loop(0, PATCH // CHUNK, back_body, 0)

    ring0, ring1 = {}, {}
    branch_half(0, 1)
    branch_push(0, 1, ring0)
    branch_half(0, 0)
    branch_push(0, 0, ring0)
    stats_sum(2, stats_copies)
    stats_copies = stats_send(3)

    diag = lax.broadcasted_iota(jnp.int32, (PATCH, PATCH), 0) == lax.broadcasted_iota(
        jnp.int32, (PATCH, PATCH), 1
    )
    npatch = []
    for s in range(2):
        row = jnp.broadcast_to(mask_in[s : s + 1, :].astype(F32), (PATCH, PATCH))
        column = jnp.sum(jnp.where(diag, row, 0.0), axis=1, keepdims=True)
        mask_col[s] = jnp.broadcast_to(column, (PATCH, 128))
        npatch.append(jnp.maximum(jnp.sum(column, axis=0, keepdims=True), 1.0))

    branch_half(1, 1)
    branch_push(1, 1, ring1)
    branch_add(0, 1, ring0)
    branch_half(1, 0)
    branch_push(1, 0, ring1)
    branch_add(0, 0, ring0)
    stats_sum(3, stats_copies)
    stale_in.wait()
    noise_in.wait()
    branch_add(1, 1, ring1)
    branch_add(1, 0, ring1)
    back_rows(0, ring0)
    stage[0] = 2
    back0 = gather_own(bk, 0)
    back_rows(1, ring1)
    gather_on(bk, 0, back0)
    back1 = gather_own(bk, 1)
    gather_near(bk, 0, back0)
    gather_end(bk, 0, back0)
    gather_sib(back0)

    def back_pre(s):
        def body(i, carry):
            rows = bk[s, i].reshape(4 * PATCH, D)
            value = jnp.dot(rows, asm_down[...], preferred_element_type=F32)
            act[s, i] = (value * gelu_parts(pre[s, i])[1]).astype(BF)
            return carry

        lax.fori_loop(0, 2, body, 0)

    PARTS = ((1, 0, 256), (1, 256, 384), (0, 0, 256), (0, 256, 256), (0, 512, 128))
    final = len(PARTS) - 1

    def over_width(body):
        each(3, lambda n: body(pl.multiple_of(n * SLICE, 128), SLICE))
        body(3 * SLICE, D - 3 * SLICE)

    def grad_part(rows, s, at_, wide, start, width):
        left = rows[s, :, :, :, pl.ds(at_, wide)].reshape(8 * PATCH, wide)
        right = act[s, :, :, start : start + width].reshape(8 * PATCH, width)
        return lax.dot_general(left, right, FIRST, preferred_element_type=F32)

    def grad_rows(p, h, j, k):
        a, b = turn(far_at[h], j), turn(near_at[h], k)
        block = (b * 4 + a) if h == 0 else (a * 4 + b)
        rows = pl.ds(pl.multiple_of(block * BLOCK + 80 * h, 8), 80)
        return grad[rows, PARTS[p][1] : PARTS[p][1] + PARTS[p][2]]

    def block_parts(p):
        cols = pl.ds(PARTS[p][1], PARTS[p][2])
        return tuple((lambda ref, k, i=i: ref.at[k, pl.ds(i, 2), :, cols]) for i in (0, 2))

    def far_ring(p, h):
        m = PARTS[p][0]
        return raws[h].at[m], x_recv.at[m, h], block_parts(p), far[h][1], far[h][3]

    def far_start(p):
        m, start, width = PARTS[p]
        cols = slice(start, start + width)

        def away(k):
            for h in range(2):
                for j, slot in ((2, 0), (1, 1), (3, 2)):
                    raws[h][m, slot, k, :, cols] = grad_rows(p, h, j, k).astype(BF)

        def mine(k):
            for h in range(2):
                grad_own[m, h, k, :, cols] = grad_rows(p, h, 0, k)

        each(4, away)
        out = [ring_start(*far_ring(p, h)) for h in range(2)]
        each(4, mine)
        return out

    def far_add(p, d):
        for h in range(2):
            ring_add(*far_ring(p, h), add_blocks, d[h])

    def near_start(p, d):
        m, start, width = PARTS[p]
        cols = slice(start, start + width)
        out = []
        for h in range(2):
            ring_wait(d[h])

            def total(k):
                return (
                    grad_own[m, h, k, :, cols]
                    + x_recv[m, h, 1, k, :, cols].astype(F32)
                    + x_recv[m, h, 2, k, :, cols].astype(F32)
                )

            def away(k):
                b_send[m, h, k, :, cols] = total(k + 1).astype(BF)

            each(3, away)
            send, recv = b_send.at[m, h], b_recv.at[m, h]
            part = pl.ds(start, width)
            out += [
                push(send.at[k, :, part], recv.at[k, :, part], near[h][k + 1]) for k in (1, 0, 2)
            ]
            grad_own[m, h, 0, :, cols] = total(0)
        return out

    def out_cols(owner, start, width):
        return pl.ds(pl.multiple_of(owner * SLICE + start, 128), width)

    def update(p, d):
        m, start, width = PARTS[p]
        for copy in d:
            copy.wait_recv()

        def columns(n, h):
            cols = pl.ds(pl.multiple_of(start + n * 128, 128), 128)
            rows = slice(0, 80) if h == 0 else slice(80, BLOCK)
            high = 80 if h == 0 else 72
            grads = (
                grad_own[m, h, 0, 0:high, cols]
                + b_recv[m, h, 0, 0:high, cols].astype(F32)
                + b_recv[m, h, 1, 0:high, cols].astype(F32)
                + b_recv[m, h, 2, 0:high, cols].astype(F32)
            )
            weights = par[m, rows, cols]
            new_first = beta_one * m1[m, rows, cols] + (1.0 - beta_one) * grads
            new_second = beta_two * m2[m, rows, cols] + (1.0 - beta_two) * grads * grads
            first_hat = new_first / (1.0 - beta_one**adam_count)
            second_hat = new_second / (1.0 - beta_two**adam_count)
            step = first_hat / (jnp.sqrt(second_hat) + adam_eps) + weight_decay * weights
            new_weights = weights - learn_rate * step
            m1[m, rows, cols] = new_first
            m2[m, rows, cols] = new_second
            par[m, rows, cols] = new_weights
            land[m, 0, rows, cols] = new_weights.astype(BF)

        for h in range(2):
            each(width // 128, functools.partial(columns, h=h))
        mine = land.at[m, 0, :, pl.ds(start, width)]

        def slot(j, k):
            return land.at[m, 2 * j + k, :, pl.ds(start, width)]

        d = {
            "left": push(mine, slot(3, 0), y_plus),
            "right": push(mine, slot(1, 0), y_minus),
            "sib0": push(mine, slot(0, 1), sibling),
        }
        if p == final:
            d["across"] = push(mine, slot(2, 0), y_ring[2])
        out_store(p, 0, 0)
        return d

    def state_store(m):
        move(m1.at[m], o_m1.at[m])
        move(m2.at[m], o_m2.at[m])
        move(par.at[m], o_par.at[m])

    def out_store(p, j, k):
        m, start, width = PARTS[p]
        owner = turn(y, j) * 2 + (c if k == 0 else 1 - c)
        block = land.at[m, 2 * j + k, :, pl.ds(start, width)]
        move(block, o_roll.at[m, :, out_cols(owner, start, width)])

    def out_on(p, d):
        m, start, width = PARTS[p]
        half = 128 * ((width // 128 + 1) // 2)
        for key, j, to, at_, wide in (
            ("left", 3, y_plus, start, half),
            ("right", 1, y_minus, start + half, width - half),
        ):
            d[key].wait_recv()
            cols = pl.ds(at_, wide)
            if p != final:
                d[key, "across"] = push(land.at[m, 2 * j, :, cols], land.at[m, 4, :, cols], to)
            cols = pl.ds(start, width)
            d[key, "sib"] = push(
                land.at[m, 2 * j, :, cols], land.at[m, 2 * j + 1, :, cols], sibling
            )
            out_store(p, j, 0)

    def out_end(p, d):
        m, start, width = PARTS[p]
        for key in (("across",) if p == final else (("left", "across"), ("right", "across"))):
            d[key].wait_recv()
        cols = pl.ds(start, width)
        d["sib2"] = push(land.at[m, 4, :, cols], land.at[m, 5, :, cols], sibling)
        out_store(p, 2, 0)

    def out_sib(p, d):
        d["sib0"].wait_recv()
        out_store(p, 0, 1)
        d["left", "sib"].wait_recv()
        out_store(p, 3, 1)
        d["right", "sib"].wait_recv()
        out_store(p, 1, 1)
        d["sib2"].wait_recv()
        out_store(p, 2, 1)

    for copy in weights_sent:
        copy.wait()
    grad[pl.ds(D, 8), :] = jnp.zeros((8, SLICE), F32)

    def first_rows(at_, wide):
        grad[pl.ds(at_, wide), :] = grad_part(bk, 0, at_, wide, 0, SLICE)

    over_width(first_rows)
    gather_on(bk, 1, back1)
    back_pre(0)
    gather_near(bk, 1, back1)
    for j in (0, 1, 3):
        back1["sib%d" % j].wait_recv()

    def grad_blocks(at_, wide, blocks, start, width):
        left = bk[1, :, blocks, :, pl.ds(at_, wide)]
        n = left.shape[1] * PATCH
        first_row = blocks.start * PATCH
        right = act[1, :, first_row : first_row + n, start : start + width].reshape(2 * n, width)
        return lax.dot_general(
            left.reshape(2 * n, wide), right, FIRST, preferred_element_type=F32
        )

    def early_rows(at_, wide):
        grad[pl.ds(at_, wide), :] += grad_blocks(at_, wide, slice(0, 2), 0, SLICE) + grad_blocks(
            at_, wide, slice(3, 4), 0, SLICE
        )

    over_width(early_rows)
    gather_end(bk, 1, back1)
    back1["sib2"].wait_recv()

    def down_part(p):
        start, width = PARTS[p][1:]

        def body(at_, wide):
            cols = slice(start, start + width)
            grad[pl.ds(at_, wide), cols] += grad_blocks(at_, wide, slice(2, 3), start, width)

        over_width(body)

    def up_part(p):
        start, width = PARTS[p][1:]

        def body(at_, wide):
            grad[pl.ds(at_, wide), start : start + width] = grad_part(
                hid, 0, at_, wide, start, width
            ) + grad_part(hid, 1, at_, wide, start, width)

        over_width(body)

    down_part(0)
    far0 = far_start(0)
    down_part(1)
    far1 = far_start(1)
    back_pre(1)
    far_add(1, far1)
    far_add(0, far0)
    up_part(2)
    far2 = far_start(2)
    near1 = near_start(1, far1)
    up_part(3)
    far_add(2, far2)
    far3 = far_start(3)
    near0 = near_start(0, far0)
    m1_in.wait()
    m2_in.wait()
    out1 = update(1, near1)
    far_add(3, far3)
    up_part(4)
    near2 = near_start(2, far2)
    far4 = far_start(4)
    out0 = update(0, near0)
    state_store(1)
    out_on(1, out1)
    near3 = near_start(3, far3)
    far_add(4, far4)
    out2 = update(2, near2)
    out3 = update(3, near3)
    near4 = near_start(4, far4)
    out_on(2, out2)
    out_on(0, out0)
    out_on(3, out3)
    out4 = update(4, near4)
    state_store(0)
    out_end(0, out0)
    out_end(3, out3)
    out_end(1, out1)
    out_on(4, out4)
    out_end(2, out2)
    out_end(4, out4)
    for p, out in enumerate((out0, out1, out2, out3, out4)):
        out_sib(p, out)
    assert fresh_id[0] <= N_RECV, fresh_id[0]
    for copy in moves + sends:
        copy.wait()


def settle(*refs):
    sources, targets, held, sem = refs[:4], refs[4:8], refs[8:12], refs[12]
    pieces = [(i, m) for i in (3, 0, 1, 2) for m in range(2)]
    reads, writes = [], []
    for n, (i, m) in enumerate(pieces):
        there, here = sources[i].at[m], held[i].at[m]
        reads.append(pltpu.make_async_copy(there, here, sem.at[n]))
        reads[-1].start()
    for n, (i, m) in enumerate(pieces):
        reads[n].wait()
        here, there = held[i].at[m], targets[i].at[m]
        writes.append(pltpu.make_async_copy(here, there, sem.at[len(pieces) + n]))
        writes[-1].start()
    for write in writes:
        write.wait()


def per_device(
    latents,
    stale_velocity,
    noise,
    modulation,
    step_ratio,
    rewards,
    group_ids,
    step_index,
    valid_steps,
    patch_mask,
    params,
    first_moment,
    second_moment,
):
    any_ = pl.BlockSpec(memory_space=pl.ANY)
    shard = jax.ShapeDtypeStruct(params.shape, F32)
    outs = pl.pallas_call(
        kernel,
        out_shape=(shard, shard, shard, jax.ShapeDtypeStruct((2, BLOCK, 8 * SLICE), BF)),
        in_specs=[any_] * 13,
        out_specs=(any_,) * 4,
        scratch_shapes=[
            pltpu.VMEM((2, 2, 4, PATCH, D), BF),
            pltpu.VMEM((2, 2, 4, PATCH, D), BF),
            pltpu.VMEM((2, 4, 4, 80, SLICE), BF),
            pltpu.VMEM((2, 4, 4, 80, SLICE), BF),
            pltpu.VMEM((2560, SLICE), BF),
            pltpu.VMEM((D, SLICE), BF),
            pltpu.VMEM((2, 2, 4 * PATCH, SLICE), F32),
            pltpu.VMEM((2, 2, 4 * PATCH, SLICE), BF),
            pltpu.VMEM((2, 4, 4 * PATCH, SLICE), BF),
            pltpu.VMEM((2, 3, PATCH, D), BF),
            pltpu.VMEM((2, 3, PATCH, D), BF),
            pltpu.VMEM((2, PATCH, D), F32),
            pltpu.VMEM((D + 8, SLICE), F32),
            pltpu.VMEM((2, 2, 3, 4, 80, SLICE), BF),
            pltpu.VMEM((2, 2, 4, 80, SLICE), F32),
            pltpu.VMEM((2, 2, 3, 80, SLICE), BF),
            pltpu.VMEM((2, 2, 3, 80, SLICE), BF),
            pltpu.VMEM((2, PATCH, D), BF),
            pltpu.VMEM((2, PATCH, D), BF),
            pltpu.VMEM((2, BLOCK, SLICE), F32),
            pltpu.VMEM((2, BLOCK, SLICE), F32),
            pltpu.VMEM((2, BLOCK, SLICE), F32),
            pltpu.VMEM((2, 8, BLOCK, SLICE), BF),
            pltpu.VMEM((2, PATCH, 128), F32),
            pltpu.VMEM((8, 128), F32),
            pltpu.VMEM((4, 4, 8, 128), F32),
            pltpu.SMEM((2,), F32),
            pltpu.SMEM((2,), jnp.int32),
            pltpu.SMEM((2,), jnp.int32),
            pltpu.SMEM((2,), jnp.int32),
            pltpu.SMEM((2,), F32),
            pltpu.VMEM((2, PATCH), jnp.int32),
            pltpu.VMEM((3, 2, D), F32),
            pltpu.SemaphoreType.DMA((N_SEND + N_PAIR,)),
            pltpu.SemaphoreType.DMA((N_RECV + N_PAIR,)),
            pltpu.SemaphoreType.DMA((N_LOCAL,)),
        ],
        compiler_params=pltpu.CompilerParams(
            collective_id=0, has_side_effects=True, vmem_limit_bytes=63 << 20
        ),
    )(
        rewards,
        group_ids,
        step_index,
        valid_steps,
        step_ratio,
        patch_mask,
        modulation.transpose(1, 0, 2),
        latents,
        stale_velocity,
        noise,
        params,
        first_moment,
        second_moment,
    )
    return tuple(
        pl.pallas_call(
            settle,
            out_shape=tuple(jax.ShapeDtypeStruct(o.shape, o.dtype) for o in outs),
            in_specs=[any_] * 4,
            out_specs=(any_,) * 4,
            scratch_shapes=[pltpu.VMEM(o.shape, o.dtype) for o in outs]
            + [pltpu.SemaphoreType.DMA((16,))],
        )(*outs)
    )


def solution(mesh):
    rows = ("roll", "fsdp")
    weights = P(None, "fsdp", "roll")
    return jax.shard_map(
        per_device,
        mesh=mesh,
        in_specs=(
            P(rows, None, None),
            P(rows, None, None),
            P(rows, None, None),
            P(rows, None, None),
            P(rows),
            P(rows),
            P(rows),
            P(rows),
            P(rows),
            P(rows, None),
            weights,
            weights,
            weights,
        ),
        out_specs=(weights, weights, weights, P(None, "fsdp", None)),
        check_vma=False,
    )
```

```python
import functools

import jax
import jax.numpy as jnp
from jax import lax
from jax.experimental import pallas as pl
from jax.experimental.pallas import tpu as pltpu
from jax.sharding import PartitionSpec as P

GROUPS = 12
D = 2432
BLOCK = 152
SLICE = 640
PATCH = 80
CHUNK = 16

eps_norm = 1e-06
clip_low = 0.8
clip_high = 1.2
spread_floor = 0.25
beta_one = 0.9
beta_two = 0.999
learn_rate = 0.001
weight_decay = 0.01
adam_eps = 1e-08
adam_count = 100.0

BF = jnp.bfloat16
F32 = jnp.float32
MESH = pl.DeviceIdType.MESH
COLS = (pl.ds(0, 1280), pl.ds(1280, 1152))
OUT_COLS = ((0, 384), (384, 256))
LAST = (((1,), (1,)), ((), ()))
FIRST = (((0,), (0,)), ((), ()))
N_SEND = 40
N_PAIR = 8
N_RECV = 167
N_LOCAL = 16


def gelu_parts(pre):
    root = 0.7978845608028654
    square = pre * pre
    t = jnp.tanh(root * (pre + 0.044715 * (square * pre)))
    cdf = 0.5 * (1.0 + t)
    slope = cdf + pre * (0.5 * (1.0 - t * t)) * (root * (1.0 + (3.0 * 0.044715) * square))
    return pre * cdf, slope


class Once:
    def __init__(self, wait):
        self.todo = wait

    def wait(self):
        if self.todo is not None:
            self.todo()
        self.todo = None


def kernel(
    rewards_h,
    group_ids_h,
    step_index_h,
    valid_steps_h,
    step_ratio_h,
    mask_h,
    mod_h,
    lat_h,
    stale_h,
    noise_h,
    par_h,
    m1_h,
    m2_h,
    o_par,
    o_m1,
    o_m2,
    o_roll,
    hid,
    bk,
    raw0,
    raw1,
    asm_up,
    asm_down,
    pre,
    act,
    sib_recv,
    y_send,
    y_recv,
    own,
    grad,
    x_recv,
    grad_own,
    b_send,
    b_recv,
    stale,
    noise,
    par,
    m1,
    m2,
    land,
    mask_col,
    stats,
    stats_recv,
    rewards,
    group_ids,
    step_index,
    valid_steps,
    step_ratio,
    mask_in,
    mod,
    send_sem,
    recv_sem,
    local_sem,
):
    roll = lax.axis_index("roll")
    fsdp = lax.axis_index("fsdp")
    y, c = roll // 2, lax.rem(roll, 2)
    x, z = fsdp // 4, lax.rem(fsdp, 4)

    def turn(a, by):
        return lax.rem(a + by, 4)

    def at(x_, y_, z_, c_):
        return (y_ * 2 + c_, x_ * 4 + z_)

    y_ring = [at(x, turn(y, j), z, c) for j in range(4)]
    x_ring = [at(turn(x, j), y, z, c) for j in range(4)]
    z_ring = [at(x, y, turn(z, j), c) for j in range(4)]
    sibling = at(x, y, z, 1 - c)
    y_plus, y_minus = y_ring[1], y_ring[3]

    barrier = pltpu.get_barrier_semaphore()
    partners = y_ring[1:] + x_ring[1:] + z_ring[1:] + [sibling]
    for partner in partners:
        pl.semaphore_signal(barrier, inc=1, device_id=partner, device_id_type=MESH)

    stage, fresh_id, spare, sends, moves = [0], [0], [], [], []

    def recv_id():
        if stage[0] == 2 and spare:
            return spare.pop(0)
        fresh_id[0] += 1
        if stage[0] == 0:
            spare.append(fresh_id[0] - 1)
        return fresh_id[0] - 1

    def push(src, dst, device, landed=None, log=None):
        i, n = recv_id(), len(sends)
        if n >= N_SEND:
            sends[n - N_SEND].wait()

        def describe(src, dst):
            return pltpu.make_async_remote_copy(
                src_ref=src,
                dst_ref=dst,
                send_sem=send_sem.at[n % N_SEND],
                recv_sem=recv_sem.at[i],
                device_id=device,
                device_id_type=MESH,
            )

        copy = describe(src, dst)
        copy.start()
        sends.append(Once(copy.wait_send))
        if log is not None:
            log.append(sends[-1])
        return copy if landed is None else describe(landed, landed)

    def move(src, dst):
        n = len(moves)
        if n >= N_LOCAL:
            moves[n - N_LOCAL].wait()
        copy = pltpu.make_async_copy(src, dst, local_sem.at[n % N_LOCAL])
        copy.start()
        moves.append(Once(copy.wait))
        return moves[-1]

    par_in = move(par_h, par)
    lat_in = [move(lat_h.at[s], y_send.at[s, 0]) for s in range(2)] + [move(mod_h, mod)]
    small_in = [
        move(rewards_h, rewards),
        move(group_ids_h, group_ids),
        move(step_index_h, step_index),
        move(valid_steps_h, valid_steps),
        move(step_ratio_h, step_ratio),
        move(mask_h, mask_in),
    ]

    raws = (raw0, raw1)
    near = (x_ring, z_ring)
    far = (z_ring, x_ring)
    near_at = (x, z)
    far_at = (z, x)

    par_in.wait()
    for m in range(2):
        raw0[m, z, x] = par[m, 0:80, :].astype(BF)
        raw1[m, x, z, 0:72, :] = par[m, 80:BLOCK, :].astype(BF)
        raw1[m, x, z, 64:80, :] = jnp.concatenate(
            [par[m, 144:BLOCK, :], jnp.zeros((8, SLICE), F32)], axis=0
        ).astype(BF)

    def each(n, body):
        def step(i, carry):
            body(i)
            return carry

        lax.fori_loop(0, n, step, 0)

    def modulated(s):
        shift = mod[0, s : s + 1, :]
        scaling = 1.0 + mod[1, s : s + 1, :]

        def body(i, carry):
            rows = pl.ds(pl.multiple_of(i * CHUNK, CHUNK), CHUNK)
            values = y_send[s, 0, rows, :].astype(F32)
            middle = jnp.sum(values, axis=-1, keepdims=True) / D
            centred = values - middle
            spread = jnp.sum(centred * centred, axis=-1, keepdims=True) / D
            normed = centred * lax.rsqrt(spread + eps_norm)
            hid[s, 0, 0, rows, :] = (normed * scaling + shift).astype(BF)
            return carry

        lax.fori_loop(0, PATCH // CHUNK, body, 0)

    pl.semaphore_wait(barrier, len(partners))

    first, second, weights_sent = {}, {}, []

    def near_own(m):
        for h in range(2):
            a, b = far_at[h], near_at[h]
            mine = raws[h].at[m, a, b]
            for k in (3, 1):
                first[m, h, k] = push(
                    mine, mine, near[h][4 - k], raws[h].at[m, a, turn(b, k)], log=weights_sent
                )

    def near_on(m):
        k = (3, 1)[m]
        for h in range(2):
            a, b = far_at[h], near_at[h]
            first[m, h, k].wait_recv()
            block = raws[h].at[m, a, turn(b, k)]
            first[m, h, 2] = push(
                block, block, near[h][4 - k], raws[h].at[m, a, turn(b, 2)], log=weights_sent
            )
        for h in range(2):
            first[m, h, 4 - k].wait_recv()

    def far_own(m, k):
        for h in range(2):
            a, b = far_at[h], turn(near_at[h], k)
            if k == 2:
                first[m, h, 2].wait_recv()
            block = raws[h].at[m, a, b]
            for side in (3, 1):
                second[m, h, k, side] = push(
                    block, block, far[h][4 - side], raws[h].at[m, turn(a, side), b], log=weights_sent
                )

    def far_on(m, k):
        side = 3 if k < 2 else 1
        for h in range(2):
            a, b = far_at[h], turn(near_at[h], k)
            second[m, h, k, side].wait_recv()
            block = raws[h].at[m, turn(a, side), b]
            second[m, h, k, 2] = push(
                block, block, far[h][4 - side], raws[h].at[m, turn(a, 2), b], log=weights_sent
            )

    near_own(0)
    stale_in = move(stale_h, stale)
    noise_in = move(noise_h, noise)
    m1_in = move(m1_h, m1)
    m2_in = move(m2_h, m2)
    for copy in lat_in:
        copy.wait()

    def gather_own(buf, s):
        mine = buf.at[s, 0, 0]
        left, right = buf.at[s, 0, 3], buf.at[s, 0, 1]
        lo, hi = COLS
        return {
            "left_lo": push(mine.at[:, lo], left.at[:, lo], y_plus),
            "right_hi": push(mine.at[:, hi], right.at[:, hi], y_minus),
            "left_hi": push(mine.at[:, hi], left.at[:, hi], y_plus),
            "right_lo": push(mine.at[:, lo], right.at[:, lo], y_minus),
            "sib0": push(mine, buf.at[s, 1, 0], sibling),
        }

    def gather_on(buf, s, d):
        left, right, across = buf.at[s, 0, 3], buf.at[s, 0, 1], buf.at[s, 0, 2]
        lo, hi = COLS
        d["left_lo"].wait_recv()
        d["across_lo"] = push(left.at[:, lo], across.at[:, lo], y_plus)
        d["right_hi"].wait_recv()
        d["across_hi"] = push(right.at[:, hi], across.at[:, hi], y_minus)

    def gather_near(buf, s, d):
        d["left_hi"].wait_recv()
        d["sib3"] = push(buf.at[s, 0, 3], buf.at[s, 1, 3], sibling)
        d["right_lo"].wait_recv()
        d["sib1"] = push(buf.at[s, 0, 1], buf.at[s, 1, 1], sibling)

    def gather_end(buf, s, d):
        d["across_lo"].wait_recv()
        d["across_hi"].wait_recv()
        d["sib2"] = push(buf.at[s, 0, 2], buf.at[s, 1, 2], sibling)

    def gather_sib(d):
        for j in range(4):
            d["sib%d" % j].wait_recv()

    def stats_send(step):
        ring = ([None, sibling], y_ring, x_ring, z_ring)[step]
        log = []
        return [
            push(stats, stats_recv.at[step, j], ring[j], log=log) for j in range(1, len(ring))
        ], log

    def stats_sum(step, copies):
        total = stats[...]
        for j, copy in enumerate(copies[0]):
            copy.wait_recv()
            total = total + stats_recv[step, j + 1]
        for copy in copies[1]:
            copy.wait()
        stats[...] = total

    def assemble(m, out):
        for h in range(2):
            for k in range(4):
                second[m, h, k, 1 if k < 2 else 3].wait_recv()
                second[m, h, k, 2].wait_recv()

        def body(i, carry):
            base = pl.multiple_of(i * (4 * BLOCK), CHUNK)
            parts = []
            for k in range(4):
                parts += [raw0[m, k, i], raw1[m, i, k, 0:72, :]]
            out[pl.ds(base, 4 * BLOCK), :] = jnp.concatenate(parts, axis=0)
            return carry

        lax.fori_loop(0, 4, body, 0)

    def forward(s, i):
        rows = hid[s, i].reshape(4 * PATCH, D)
        value = jnp.dot(rows, asm_up[0:D, :], preferred_element_type=F32)
        pre[s, i] = value
        act[s, i] = gelu_parts(value)[0].astype(BF)

    modulated(0)
    rows0 = gather_own(hid, 0)
    near_own(1)
    near_on(0)
    far_own(0, 1)
    far_own(0, 0)
    modulated(1)

    for copy in small_in:
        copy.wait()
    lane = lax.broadcasted_iota(jnp.int32, (1, 128), 1)
    valid = [jnp.where(step_index[s] < valid_steps[s], 1.0, 0.0).astype(F32) for s in range(2)]
    member = [jnp.where(lane == group_ids[s], 1.0, 0.0).astype(F32) for s in range(2)]
    stats[...] = jnp.zeros((8, 128), F32)
    stats[0:1, :] = member[0] * valid[0] + member[1] * valid[1]
    stats[1:2, :] = member[0] * (valid[0] * rewards[0]) + member[1] * (valid[1] * rewards[1])
    stats[2:3, :] = member[0] * (valid[0] * (rewards[0] * rewards[0])) + member[1] * (
        valid[1] * (rewards[1] * rewards[1])
    )
    stats[3:4, :] = jnp.zeros((1, 128), F32) + (valid[0] + valid[1])

    stats_copies = stats_send(0)
    gather_on(hid, 0, rows0)
    near_on(1)
    rows1 = gather_own(hid, 1)
    stats_sum(0, stats_copies)
    far_own(0, 3)
    far_own(0, 2)
    far_on(0, 1)
    far_own(1, 2)
    far_on(0, 2)
    far_on(0, 0)
    far_on(0, 3)
    far_own(1, 0)
    far_own(1, 3)
    gather_on(hid, 1, rows1)
    stats_copies = stats_send(1)
    gather_near(hid, 0, rows0)
    gather_end(hid, 0, rows0)
    far_on(1, 2)
    far_own(1, 1)
    assemble(0, asm_up)
    gather_sib(rows0)
    forward(0, 0)
    gather_near(hid, 1, rows1)
    far_on(1, 0)
    forward(0, 1)
    gather_end(hid, 1, rows1)
    far_on(1, 3)
    far_on(1, 1)
    gather_sib(rows1)
    each(2, lambda i: forward(1, i))
    assemble(1, asm_down)
    stage[0] = 1
    stats_sum(1, stats_copies)
    stats_copies = stats_send(2)

    def pair_copy(s, n):
        i = s * 4 + n
        return pltpu.make_async_remote_copy(
            src_ref=asm_up.at[pl.ds(pl.multiple_of((s * 4 + n) * 320, CHUNK), 320)],
            dst_ref=sib_recv.at[s, n],
            send_sem=send_sem.at[N_SEND + i],
            recv_sem=recv_sem.at[N_RECV + i],
            device_id=sibling,
            device_id_type=MESH,
        )

    def branch_tile(s, i, n):
        cols = pl.ds(pl.multiple_of(jnp.minimum(n * SLICE, D - SLICE), 128), SLICE)
        value = lax.dot_general(act[s, i], asm_down[cols, :], LAST, preferred_element_type=F32)
        return cols, value

    def branch_half(s, half):
        def away(q):
            n = 2 * half + q
            value = branch_tile(s, 1, n)[1]
            asm_up[pl.ds(pl.multiple_of((s * 4 + n) * 320, CHUNK), 320), :] = value.astype(BF)
            pair_copy(s, n).start()

        def mine(q):
            n = 2 * half + q
            cols, value = branch_tile(s, 0, n)
            pair_copy(s, n).wait()
            value = value + sib_recv[s, n].astype(F32)
            own[s, :, cols] = value[0:80]
            for j, k in ((2, 0), (1, 1), (3, 2)):
                y_send[s, k, :, cols] = value[j * 80 : j * 80 + 80].astype(BF)

        each(2, away)
        each(2, mine)

    def ring_start(send, recv, parts, plus, minus):
        lo, hi = parts
        return {
            "across_hi": push(hi(send, 0), hi(recv, 0), plus),
            "across_lo": push(lo(send, 0), lo(recv, 0), minus),
            "plus_lo": push(lo(send, 1), lo(recv, 1), plus),
            "minus_hi": push(hi(send, 2), hi(recv, 2), minus),
        }

    def ring_add(send, recv, parts, plus, minus, add, d):
        lo, hi = parts
        d["across_hi"].wait_recv()
        add(hi(send, 1), hi(recv, 0))
        d["plus_hi"] = push(hi(send, 1), hi(recv, 1), plus)
        d["across_lo"].wait_recv()
        add(lo(send, 2), lo(recv, 0))
        d["minus_lo"] = push(lo(send, 2), lo(recv, 2), minus)

    def ring_wait(d):
        for part in ("plus_lo", "minus_hi", "plus_hi", "minus_lo"):
            d[part].wait_recv()

    def add_rows(dst, src):
        def body(i, carry):
            rows = pl.ds(pl.multiple_of(i * CHUNK, CHUNK), CHUNK)
            dst[rows, :] = (dst[rows, :].astype(F32) + src[rows, :].astype(F32)).astype(BF)
            return carry

        lax.fori_loop(0, dst.shape[0] // CHUNK, body, 0)

    def add_blocks(dst, src):
        for k in range(2):
            dst[k] = (dst[k].astype(F32) + src[k].astype(F32)).astype(BF)

    col_parts = tuple((lambda ref, k, cols=cols: ref.at[k, :, cols]) for cols in COLS)

    def branch_push(s, half, d):
        lo, hi = col_parts
        send, recv = y_send.at[s], y_recv.at[s]
        if half == 1:
            d["across_hi"] = push(hi(send, 0), hi(recv, 0), y_plus)
            d["minus_hi"] = push(hi(send, 2), hi(recv, 2), y_minus)
        else:
            d["across_lo"] = push(lo(send, 0), lo(recv, 0), y_minus)
            d["plus_lo"] = push(lo(send, 1), lo(recv, 1), y_plus)

    def branch_add(s, half, d):
        part = col_parts[half]
        send, recv = y_send.at[s], y_recv.at[s]
        key, k, to = (("lo", 2, y_minus), ("hi", 1, y_plus))[half]
        d["across_" + key].wait_recv()
        add_rows(part(send, k), part(recv, 0))
        d[("minus_lo", "plus_hi")[half]] = push(part(send, k), part(recv, k), to)

    def back_rows(s, d):
        ring_wait(d)
        gate = 1.0 + mod[2, s : s + 1, :]
        factor = step_ratio[s]

        def err_body(i, total):
            rows = pl.ds(pl.multiple_of(i * CHUNK, CHUNK), CHUNK)
            branch = (
                own[s, rows, :] + y_recv[s, 1, rows, :].astype(F32) + y_recv[s, 2, rows, :].astype(F32)
            )
            velocity = gate * branch
            drawn = noise[s, rows, :].astype(F32)
            err = drawn + factor * (stale[s, rows, :].astype(F32) - velocity)
            own[s, rows, :] = err
            gap = jnp.sum(drawn * drawn - err * err, axis=1, keepdims=True)
            return total + mask_col[s, rows, 0:1] * gap

        gaps = lax.fori_loop(0, PATCH // CHUNK, err_body, jnp.zeros((CHUNK, 1), F32))
        logratio = jnp.sum(gaps, axis=0, keepdims=True) / (2.0 * npatch[s])
        safe = jnp.maximum(stats[0:1, :], 1.0)
        middle = stats[1:2, :] / safe
        variance = jnp.maximum(stats[2:3, :] / safe - middle * middle, 0.0)
        spread = jnp.maximum(jnp.sqrt(variance), spread_floor)
        own_mean = jnp.sum(member[s] * middle, axis=1, keepdims=True)
        own_spread = jnp.sum(member[s] * spread, axis=1, keepdims=True)
        advantage = (rewards[s] - own_mean) / own_spread
        ratio = jnp.exp(logratio)
        clipped = jnp.clip(ratio, clip_low, clip_high)
        active = jnp.where(ratio * advantage <= clipped * advantage, 1.0, 0.0).astype(F32)
        coef = -valid[s] * advantage * ratio * active / jnp.maximum(stats[3:4, 0:1], 1.0)
        per_patch = coef / npatch[s]

        def back_body(i, carry):
            rows = pl.ds(pl.multiple_of(i * CHUNK, CHUNK), CHUNK)
            scale = per_patch * mask_col[s, rows, 0:1] * factor
            bk[s, 0, 0, rows, :] = (gate * (scale * own[s, rows, :])).astype(BF)
            return carry

        lax.fori_loop(0, PATCH // CHUNK, back_body, 0)

    ring0, ring1 = {}, {}
    branch_half(0, 1)
    branch_push(0, 1, ring0)
    branch_half(0, 0)
    branch_push(0, 0, ring0)
    stats_sum(2, stats_copies)
    stats_copies = stats_send(3)

    diag = lax.broadcasted_iota(jnp.int32, (PATCH, PATCH), 0) == lax.broadcasted_iota(
        jnp.int32, (PATCH, PATCH), 1
    )
    npatch = []
    for s in range(2):
        row = jnp.broadcast_to(mask_in[s : s + 1, :].astype(F32), (PATCH, PATCH))
        column = jnp.sum(jnp.where(diag, row, 0.0), axis=1, keepdims=True)
        mask_col[s] = jnp.broadcast_to(column, (PATCH, 128))
        npatch.append(jnp.maximum(jnp.sum(column, axis=0, keepdims=True), 1.0))

    branch_half(1, 1)
    branch_push(1, 1, ring1)
    branch_add(0, 1, ring0)
    branch_half(1, 0)
    branch_push(1, 0, ring1)
    branch_add(0, 0, ring0)
    stats_sum(3, stats_copies)
    stale_in.wait()
    noise_in.wait()
    branch_add(1, 1, ring1)
    branch_add(1, 0, ring1)
    back_rows(0, ring0)
    stage[0] = 2
    back0 = gather_own(bk, 0)
    back_rows(1, ring1)
    gather_on(bk, 0, back0)
    back1 = gather_own(bk, 1)
    gather_near(bk, 0, back0)
    gather_end(bk, 0, back0)
    gather_sib(back0)

    def back_pre(s):
        def body(i, carry):
            rows = bk[s, i].reshape(4 * PATCH, D)
            value = jnp.dot(rows, asm_down[...], preferred_element_type=F32)
            act[s, i] = (value * gelu_parts(pre[s, i])[1]).astype(BF)
            return carry

        lax.fori_loop(0, 2, body, 0)

    PARTS = ((1, 0, 256), (1, 256, 384), (0, 0, 256), (0, 256, 256), (0, 512, 128))
    final = len(PARTS) - 1

    def over_width(body):
        each(3, lambda n: body(pl.multiple_of(n * SLICE, 128), SLICE))
        body(3 * SLICE, D - 3 * SLICE)

    def grad_part(rows, s, at_, wide, start, width):
        left = rows[s, :, :, :, pl.ds(at_, wide)].reshape(8 * PATCH, wide)
        right = act[s, :, :, start : start + width].reshape(8 * PATCH, width)
        return lax.dot_general(left, right, FIRST, preferred_element_type=F32)

    def grad_rows(p, h, j, k):
        a, b = turn(far_at[h], j), turn(near_at[h], k)
        block = (b * 4 + a) if h == 0 else (a * 4 + b)
        rows = pl.ds(pl.multiple_of(block * BLOCK + 80 * h, 8), 80)
        return grad[rows, PARTS[p][1] : PARTS[p][1] + PARTS[p][2]]

    def block_parts(p):
        cols = pl.ds(PARTS[p][1], PARTS[p][2])
        return tuple((lambda ref, k, i=i: ref.at[k, pl.ds(i, 2), :, cols]) for i in (0, 2))

    def far_ring(p, h):
        m = PARTS[p][0]
        return raws[h].at[m], x_recv.at[m, h], block_parts(p), far[h][1], far[h][3]

    def far_start(p):
        m, start, width = PARTS[p]
        cols = slice(start, start + width)

        def away(k):
            for h in range(2):
                for j, slot in ((2, 0), (1, 1), (3, 2)):
                    raws[h][m, slot, k, :, cols] = grad_rows(p, h, j, k).astype(BF)

        def mine(k):
            for h in range(2):
                grad_own[m, h, k, :, cols] = grad_rows(p, h, 0, k)

        each(4, away)
        out = [ring_start(*far_ring(p, h)) for h in range(2)]
        each(4, mine)
        return out

    def far_add(p, d):
        for h in range(2):
            ring_add(*far_ring(p, h), add_blocks, d[h])

    def near_start(p, d):
        m, start, width = PARTS[p]
        cols = slice(start, start + width)
        out = []
        for h in range(2):
            ring_wait(d[h])

            def total(k):
                return (
                    grad_own[m, h, k, :, cols]
                    + x_recv[m, h, 1, k, :, cols].astype(F32)
                    + x_recv[m, h, 2, k, :, cols].astype(F32)
                )

            def away(k):
                b_send[m, h, k, :, cols] = total(k + 1).astype(BF)

            each(3, away)
            send, recv = b_send.at[m, h], b_recv.at[m, h]
            part = pl.ds(start, width)
            out += [
                push(send.at[k, :, part], recv.at[k, :, part], near[h][k + 1]) for k in (1, 0, 2)
            ]
            grad_own[m, h, 0, :, cols] = total(0)
        return out

    def out_cols(owner, start, width):
        return pl.ds(pl.multiple_of(owner * SLICE + start, 128), width)

    def update(p, d):
        m, start, width = PARTS[p]
        for copy in d:
            copy.wait_recv()

        def columns(n, h):
            cols = pl.ds(pl.multiple_of(start + n * 128, 128), 128)
            rows = slice(0, 80) if h == 0 else slice(80, BLOCK)
            high = 80 if h == 0 else 72
            grads = (
                grad_own[m, h, 0, 0:high, cols]
                + b_recv[m, h, 0, 0:high, cols].astype(F32)
                + b_recv[m, h, 1, 0:high, cols].astype(F32)
                + b_recv[m, h, 2, 0:high, cols].astype(F32)
            )
            weights = par[m, rows, cols]
            new_first = beta_one * m1[m, rows, cols] + (1.0 - beta_one) * grads
            new_second = beta_two * m2[m, rows, cols] + (1.0 - beta_two) * grads * grads
            first_hat = new_first / (1.0 - beta_one**adam_count)
            second_hat = new_second / (1.0 - beta_two**adam_count)
            step = first_hat / (jnp.sqrt(second_hat) + adam_eps) + weight_decay * weights
            new_weights = weights - learn_rate * step
            m1[m, rows, cols] = new_first
            m2[m, rows, cols] = new_second
            par[m, rows, cols] = new_weights
            land[m, 0, rows, cols] = new_weights.astype(BF)

        for h in range(2):
            each(width // 128, functools.partial(columns, h=h))
        mine = land.at[m, 0, :, pl.ds(start, width)]

        def slot(j):
            return land.at[m, j, :, pl.ds(start, width)]

        d = {"left": push(mine, slot(3), y_plus), "right": push(mine, slot(1), y_minus)}
        if p == final:
            d["across"] = push(mine, slot(2), y_ring[2])
        d["sib0"] = out_give(p, 0)
        for state, result in ((m1, o_m1), (m2, o_m2), (par, o_par)):
            part = pl.ds(start, width)
            move(state.at[m, :, part], result.at[m, :, part])
        return d

    def out_give(p, j):
        m, start, width = PARTS[p]
        block = land.at[m, j, :, pl.ds(start, width)]
        owner = turn(y, j) * 2
        place = o_roll.at[m, :, out_cols(owner + c, start, width)]
        copy = push(block, place, sibling, o_roll.at[m, :, out_cols(owner + 1 - c, start, width)])
        move(block, place)
        return copy

    def out_on(p, d):
        m, start, width = PARTS[p]
        half = 128 * ((width // 128 + 1) // 2)
        for key, j, to, at_, wide in (
            ("left", 3, y_plus, start, half),
            ("right", 1, y_minus, start + half, width - half),
        ):
            d[key].wait_recv()
            cols = pl.ds(at_, wide)
            if p != final:
                d[key, "across"] = push(land.at[m, j, :, cols], land.at[m, 2, :, cols], to)
            d[key, "sib"] = out_give(p, j)

    def out_end(p, d):
        for key in (("across",) if p == final else (("left", "across"), ("right", "across"))):
            d[key].wait_recv()
        d["sib2"] = out_give(p, 2)

    def out_sib(d):
        for key in ("sib0", ("left", "sib"), ("right", "sib"), "sib2"):
            d[key].wait_recv()

    for copy in weights_sent:
        copy.wait()
    grad[pl.ds(D, 8), :] = jnp.zeros((8, SLICE), F32)

    def first_rows(at_, wide):
        grad[pl.ds(at_, wide), :] = grad_part(bk, 0, at_, wide, 0, SLICE)

    over_width(first_rows)
    gather_on(bk, 1, back1)
    back_pre(0)
    gather_near(bk, 1, back1)
    for j in (0, 1, 3):
        back1["sib%d" % j].wait_recv()

    def grad_blocks(at_, wide, blocks, start, width):
        left = bk[1, :, blocks, :, pl.ds(at_, wide)]
        n = left.shape[1] * PATCH
        first_row = blocks.start * PATCH
        right = act[1, :, first_row : first_row + n, start : start + width].reshape(2 * n, width)
        return lax.dot_general(
            left.reshape(2 * n, wide), right, FIRST, preferred_element_type=F32
        )

    def early_rows(at_, wide):
        grad[pl.ds(at_, wide), :] += grad_blocks(at_, wide, slice(0, 2), 0, SLICE) + grad_blocks(
            at_, wide, slice(3, 4), 0, SLICE
        )

    over_width(early_rows)
    gather_end(bk, 1, back1)
    back1["sib2"].wait_recv()

    def down_part(p):
        start, width = PARTS[p][1:]

        def body(at_, wide):
            cols = slice(start, start + width)
            grad[pl.ds(at_, wide), cols] += grad_blocks(at_, wide, slice(2, 3), start, width)

        over_width(body)

    def up_part(p):
        start, width = PARTS[p][1:]

        def body(at_, wide):
            grad[pl.ds(at_, wide), start : start + width] = grad_part(
                hid, 0, at_, wide, start, width
            ) + grad_part(hid, 1, at_, wide, start, width)

        over_width(body)

    down_part(0)
    far0 = far_start(0)
    down_part(1)
    far1 = far_start(1)
    back_pre(1)
    far_add(1, far1)
    far_add(0, far0)
    up_part(2)
    far2 = far_start(2)
    near1 = near_start(1, far1)
    up_part(3)
    far_add(2, far2)
    far3 = far_start(3)
    near0 = near_start(0, far0)
    m1_in.wait()
    m2_in.wait()
    out1 = update(1, near1)
    far_add(3, far3)
    up_part(4)
    near2 = near_start(2, far2)
    far4 = far_start(4)
    out0 = update(0, near0)
    out_on(1, out1)
    near3 = near_start(3, far3)
    far_add(4, far4)
    out2 = update(2, near2)
    out3 = update(3, near3)
    near4 = near_start(4, far4)
    out_on(2, out2)
    out_on(0, out0)
    out_on(3, out3)
    out4 = update(4, near4)
    out_end(0, out0)
    out_end(3, out3)
    out_end(1, out1)
    out_on(4, out4)
    out_end(2, out2)
    out_end(4, out4)
    for out in (out0, out1, out2, out3, out4):
        out_sib(out)
    assert fresh_id[0] <= N_RECV, fresh_id[0]
    for copy in moves + sends:
        copy.wait()


def settle(*refs):
    sources, targets, held, sem = refs[:4], refs[4:8], refs[8:12], refs[12]
    pieces = [(i, m) for i in (3, 0, 1, 2) for m in range(2)]
    reads, writes = [], []
    for n, (i, m) in enumerate(pieces):
        there, here = sources[i].at[m], held[i].at[m]
        reads.append(pltpu.make_async_copy(there, here, sem.at[n]))
        reads[-1].start()
    for n, (i, m) in enumerate(pieces):
        reads[n].wait()
        here, there = held[i].at[m], targets[i].at[m]
        writes.append(pltpu.make_async_copy(here, there, sem.at[len(pieces) + n]))
        writes[-1].start()
    for write in writes:
        write.wait()


def per_device(
    latents,
    stale_velocity,
    noise,
    modulation,
    step_ratio,
    rewards,
    group_ids,
    step_index,
    valid_steps,
    patch_mask,
    params,
    first_moment,
    second_moment,
):
    any_ = pl.BlockSpec(memory_space=pl.ANY)
    shard = jax.ShapeDtypeStruct(params.shape, F32)
    outs = pl.pallas_call(
        kernel,
        out_shape=(shard, shard, shard, jax.ShapeDtypeStruct((2, BLOCK, 8 * SLICE), BF)),
        in_specs=[any_] * 13,
        out_specs=(any_,) * 4,
        scratch_shapes=[
            pltpu.VMEM((2, 2, 4, PATCH, D), BF),
            pltpu.VMEM((2, 2, 4, PATCH, D), BF),
            pltpu.VMEM((2, 4, 4, 80, SLICE), BF),
            pltpu.VMEM((2, 4, 4, 80, SLICE), BF),
            pltpu.VMEM((2560, SLICE), BF),
            pltpu.VMEM((D, SLICE), BF),
            pltpu.VMEM((2, 2, 4 * PATCH, SLICE), F32),
            pltpu.VMEM((2, 2, 4 * PATCH, SLICE), BF),
            pltpu.VMEM((2, 4, 4 * PATCH, SLICE), BF),
            pltpu.VMEM((2, 3, PATCH, D), BF),
            pltpu.VMEM((2, 3, PATCH, D), BF),
            pltpu.VMEM((2, PATCH, D), F32),
            pltpu.VMEM((D + 8, SLICE), F32),
            pltpu.VMEM((2, 2, 3, 4, 80, SLICE), BF),
            pltpu.VMEM((2, 2, 4, 80, SLICE), F32),
            pltpu.VMEM((2, 2, 3, 80, SLICE), BF),
            pltpu.VMEM((2, 2, 3, 80, SLICE), BF),
            pltpu.VMEM((2, PATCH, D), BF),
            pltpu.VMEM((2, PATCH, D), BF),
            pltpu.VMEM((2, BLOCK, SLICE), F32),
            pltpu.VMEM((2, BLOCK, SLICE), F32),
            pltpu.VMEM((2, BLOCK, SLICE), F32),
            pltpu.VMEM((2, 4, BLOCK, SLICE), BF),
            pltpu.VMEM((2, PATCH, 128), F32),
            pltpu.VMEM((8, 128), F32),
            pltpu.VMEM((4, 4, 8, 128), F32),
            pltpu.SMEM((2,), F32),
            pltpu.SMEM((2,), jnp.int32),
            pltpu.SMEM((2,), jnp.int32),
            pltpu.SMEM((2,), jnp.int32),
            pltpu.SMEM((2,), F32),
            pltpu.VMEM((2, PATCH), jnp.int32),
            pltpu.VMEM((3, 2, D), F32),
            pltpu.SemaphoreType.DMA((N_SEND + N_PAIR,)),
            pltpu.SemaphoreType.DMA((N_RECV + N_PAIR,)),
            pltpu.SemaphoreType.DMA((N_LOCAL,)),
        ],
        compiler_params=pltpu.CompilerParams(
            collective_id=0, has_side_effects=True, vmem_limit_bytes=63 << 20
        ),
    )(
        rewards,
        group_ids,
        step_index,
        valid_steps,
        step_ratio,
        patch_mask,
        modulation.transpose(1, 0, 2),
        latents,
        stale_velocity,
        noise,
        params,
        first_moment,
        second_moment,
    )
    return tuple(
        pl.pallas_call(
            settle,
            out_shape=tuple(jax.ShapeDtypeStruct(o.shape, o.dtype) for o in outs),
            in_specs=[any_] * 4,
            out_specs=(any_,) * 4,
            scratch_shapes=[pltpu.VMEM(o.shape, o.dtype) for o in outs]
            + [pltpu.SemaphoreType.DMA((16,))],
        )(*outs)
    )


def solution(mesh):
    rows = ("roll", "fsdp")
    weights = P(None, "fsdp", "roll")
    return jax.shard_map(
        per_device,
        mesh=mesh,
        in_specs=(
            P(rows, None, None),
            P(rows, None, None),
            P(rows, None, None),
            P(rows, None, None),
            P(rows),
            P(rows),
            P(rows),
            P(rows),
            P(rows),
            P(rows, None),
            weights,
            weights,
            weights,
        ),
        out_specs=(weights, weights, weights, P(None, "fsdp", None)),
        check_vma=False,
    )
```

```python
import functools

import jax
import jax.numpy as jnp
from jax import lax
from jax.experimental import pallas as pl
from jax.experimental.pallas import tpu as pltpu
from jax.sharding import PartitionSpec as P

GROUPS = 12
D = 2432
BLOCK = 152
SLICE = 640
PATCH = 80
CHUNK = 16

eps_norm = 1e-06
clip_low = 0.8
clip_high = 1.2
spread_floor = 0.25
beta_one = 0.9
beta_two = 0.999
learn_rate = 0.001
weight_decay = 0.01
adam_eps = 1e-08
adam_count = 100.0

BF = jnp.bfloat16
F32 = jnp.float32
MESH = pl.DeviceIdType.MESH
COLS = (pl.ds(0, 1280), pl.ds(1280, 1152))
OUT_COLS = ((0, 384), (384, 256))
LAST = (((1,), (1,)), ((), ()))
FIRST = (((0,), (0,)), ((), ()))
N_SEND = 40
N_PAIR = 8
N_RECV = 167
N_LOCAL = 16


def gelu_parts(pre):
    root = 0.7978845608028654
    square = pre * pre
    t = jnp.tanh(root * (pre + 0.044715 * (square * pre)))
    cdf = 0.5 * (1.0 + t)
    slope = cdf + pre * (0.5 * (1.0 - t * t)) * (root * (1.0 + (3.0 * 0.044715) * square))
    return pre * cdf, slope


class Once:
    def __init__(self, wait):
        self.todo = wait

    def wait(self):
        if self.todo is not None:
            self.todo()
        self.todo = None


def kernel(
    rewards_h,
    group_ids_h,
    step_index_h,
    valid_steps_h,
    step_ratio_h,
    mask_h,
    mod_h,
    lat_h,
    stale_h,
    noise_h,
    par_h,
    m1_h,
    m2_h,
    o_par,
    o_m1,
    o_m2,
    o_roll,
    hid,
    bk,
    raw0,
    raw1,
    asm_up,
    asm_down,
    pre,
    act,
    sib_recv,
    y_send,
    y_recv,
    own,
    grad,
    x_recv,
    grad_own,
    b_send,
    b_recv,
    stale,
    noise,
    par,
    m1,
    m2,
    land,
    mask_col,
    stats,
    stats_recv,
    rewards,
    group_ids,
    step_index,
    valid_steps,
    step_ratio,
    mask_in,
    mod,
    send_sem,
    recv_sem,
    local_sem,
):
    roll = lax.axis_index("roll")
    fsdp = lax.axis_index("fsdp")
    y, c = roll // 2, lax.rem(roll, 2)
    x, z = fsdp // 4, lax.rem(fsdp, 4)

    def turn(a, by):
        return lax.rem(a + by, 4)

    def at(x_, y_, z_, c_):
        return (y_ * 2 + c_, x_ * 4 + z_)

    y_ring = [at(x, turn(y, j), z, c) for j in range(4)]
    x_ring = [at(turn(x, j), y, z, c) for j in range(4)]
    z_ring = [at(x, y, turn(z, j), c) for j in range(4)]
    sibling = at(x, y, z, 1 - c)
    y_plus, y_minus = y_ring[1], y_ring[3]

    barrier = pltpu.get_barrier_semaphore()
    partners = y_ring[1:] + x_ring[1:] + z_ring[1:] + [sibling]
    for partner in partners:
        pl.semaphore_signal(barrier, inc=1, device_id=partner, device_id_type=MESH)

    stage, fresh_id, spare, sends, moves = [0], [0], [], [], []

    def recv_id():
        if stage[0] == 2 and spare:
            return spare.pop(0)
        fresh_id[0] += 1
        if stage[0] == 0:
            spare.append(fresh_id[0] - 1)
        return fresh_id[0] - 1

    def push(src, dst, device, landed=None, log=None):
        i, n = recv_id(), len(sends)
        if n >= N_SEND:
            sends[n - N_SEND].wait()

        def describe(src, dst):
            return pltpu.make_async_remote_copy(
                src_ref=src,
                dst_ref=dst,
                send_sem=send_sem.at[n % N_SEND],
                recv_sem=recv_sem.at[i],
                device_id=device,
                device_id_type=MESH,
            )

        copy = describe(src, dst)
        copy.start()
        sends.append(Once(copy.wait_send))
        if log is not None:
            log.append(sends[-1])
        return copy if landed is None else describe(landed, landed)

    def move(src, dst):
        n = len(moves)
        if n >= N_LOCAL:
            moves[n - N_LOCAL].wait()
        copy = pltpu.make_async_copy(src, dst, local_sem.at[n % N_LOCAL])
        copy.start()
        moves.append(Once(copy.wait))
        return moves[-1]

    par_in = move(par_h, par)
    lat_in = [move(lat_h.at[s], y_send.at[s, 0]) for s in range(2)] + [move(mod_h, mod)]
    small_in = [
        move(rewards_h, rewards),
        move(group_ids_h, group_ids),
        move(step_index_h, step_index),
        move(valid_steps_h, valid_steps),
        move(step_ratio_h, step_ratio),
        move(mask_h, mask_in),
    ]

    raws = (raw0, raw1)
    near = (x_ring, z_ring)
    far = (z_ring, x_ring)
    near_at = (x, z)
    far_at = (z, x)

    par_in.wait()
    for m in range(2):
        raw0[m, z, x] = par[m, 0:80, :].astype(BF)
        raw1[m, x, z, 0:72, :] = par[m, 80:BLOCK, :].astype(BF)
        raw1[m, x, z, 64:80, :] = jnp.concatenate(
            [par[m, 144:BLOCK, :], jnp.zeros((8, SLICE), F32)], axis=0
        ).astype(BF)

    def each(n, body, unroll=1):
        def step(i, carry):
            body(i)
            return carry

        lax.fori_loop(0, n, step, 0, unroll=unroll)

    def modulated(s):
        shift = mod[0, s : s + 1, :]
        scaling = 1.0 + mod[1, s : s + 1, :]

        def body(i, carry):
            rows = pl.ds(pl.multiple_of(i * CHUNK, CHUNK), CHUNK)
            values = y_send[s, 0, rows, :].astype(F32)
            middle = jnp.sum(values, axis=-1, keepdims=True) / D
            centred = values - middle
            spread = jnp.sum(centred * centred, axis=-1, keepdims=True) / D
            normed = centred * lax.rsqrt(spread + eps_norm)
            hid[s, 0, 0, rows, :] = (normed * scaling + shift).astype(BF)
            return carry

        lax.fori_loop(0, PATCH // CHUNK, body, 0)

    pl.semaphore_wait(barrier, len(partners))

    first, second, weights_sent = {}, {}, []

    def near_own(m):
        for h in range(2):
            a, b = far_at[h], near_at[h]
            mine = raws[h].at[m, a, b]
            for k in (3, 1):
                first[m, h, k] = push(
                    mine, mine, near[h][4 - k], raws[h].at[m, a, turn(b, k)], log=weights_sent
                )

    def near_on(m):
        k = (3, 1)[m]
        for h in range(2):
            a, b = far_at[h], near_at[h]
            first[m, h, k].wait_recv()
            block = raws[h].at[m, a, turn(b, k)]
            first[m, h, 2] = push(
                block, block, near[h][4 - k], raws[h].at[m, a, turn(b, 2)], log=weights_sent
            )
        for h in range(2):
            first[m, h, 4 - k].wait_recv()

    def far_own(m, k):
        for h in range(2):
            a, b = far_at[h], turn(near_at[h], k)
            if k == 2:
                first[m, h, 2].wait_recv()
            block = raws[h].at[m, a, b]
            for side in (3, 1):
                second[m, h, k, side] = push(
                    block, block, far[h][4 - side], raws[h].at[m, turn(a, side), b], log=weights_sent
                )

    def far_on(m, k):
        side = 3 if k < 2 else 1
        for h in range(2):
            a, b = far_at[h], turn(near_at[h], k)
            second[m, h, k, side].wait_recv()
            block = raws[h].at[m, turn(a, side), b]
            second[m, h, k, 2] = push(
                block, block, far[h][4 - side], raws[h].at[m, turn(a, 2), b], log=weights_sent
            )

    near_own(0)
    stale_in = move(stale_h, stale)
    noise_in = move(noise_h, noise)
    m1_in = move(m1_h, m1)
    m2_in = move(m2_h, m2)
    for copy in lat_in:
        copy.wait()

    def gather_own(buf, s):
        mine = buf.at[s, 0, 0]
        left, right = buf.at[s, 0, 3], buf.at[s, 0, 1]
        lo, hi = COLS
        return {
            "left_lo": push(mine.at[:, lo], left.at[:, lo], y_plus),
            "right_hi": push(mine.at[:, hi], right.at[:, hi], y_minus),
            "left_hi": push(mine.at[:, hi], left.at[:, hi], y_plus),
            "right_lo": push(mine.at[:, lo], right.at[:, lo], y_minus),
            "sib0": push(mine, buf.at[s, 1, 0], sibling),
        }

    def gather_on(buf, s, d):
        left, right, across = buf.at[s, 0, 3], buf.at[s, 0, 1], buf.at[s, 0, 2]
        lo, hi = COLS
        d["left_lo"].wait_recv()
        d["across_lo"] = push(left.at[:, lo], across.at[:, lo], y_plus)
        d["right_hi"].wait_recv()
        d["across_hi"] = push(right.at[:, hi], across.at[:, hi], y_minus)

    def gather_near(buf, s, d):
        d["left_hi"].wait_recv()
        d["sib3"] = push(buf.at[s, 0, 3], buf.at[s, 1, 3], sibling)
        d["right_lo"].wait_recv()
        d["sib1"] = push(buf.at[s, 0, 1], buf.at[s, 1, 1], sibling)

    def gather_end(buf, s, d):
        d["across_lo"].wait_recv()
        d["across_hi"].wait_recv()
        d["sib2"] = push(buf.at[s, 0, 2], buf.at[s, 1, 2], sibling)

    def gather_sib(d):
        for j in range(4):
            d["sib%d" % j].wait_recv()

    def stats_send(step):
        ring = ([None, sibling], y_ring, x_ring, z_ring)[step]
        log = []
        return [
            push(stats, stats_recv.at[step, j], ring[j], log=log) for j in range(1, len(ring))
        ], log

    def stats_sum(step, copies):
        total = stats[...]
        for j, copy in enumerate(copies[0]):
            copy.wait_recv()
            total = total + stats_recv[step, j + 1]
        for copy in copies[1]:
            copy.wait()
        stats[...] = total

    def assemble(m, out):
        for h in range(2):
            for k in range(4):
                second[m, h, k, 1 if k < 2 else 3].wait_recv()
                second[m, h, k, 2].wait_recv()

        def body(i, carry):
            base = pl.multiple_of(i * (4 * BLOCK), CHUNK)
            parts = []
            for k in range(4):
                parts += [raw0[m, k, i], raw1[m, i, k, 0:72, :]]
            out[pl.ds(base, 4 * BLOCK), :] = jnp.concatenate(parts, axis=0)
            return carry

        lax.fori_loop(0, 4, body, 0)

    def forward(s, i):
        rows = hid[s, i].reshape(4 * PATCH, D)
        value = jnp.dot(rows, asm_up[0:D, :], preferred_element_type=F32)
        pre[s, i] = value
        act[s, i] = gelu_parts(value)[0].astype(BF)

    modulated(0)
    rows0 = gather_own(hid, 0)
    near_own(1)
    near_on(0)
    far_own(0, 1)
    far_own(0, 0)
    modulated(1)

    for copy in small_in:
        copy.wait()
    lane = lax.broadcasted_iota(jnp.int32, (1, 128), 1)
    valid = [jnp.where(step_index[s] < valid_steps[s], 1.0, 0.0).astype(F32) for s in range(2)]
    member = [jnp.where(lane == group_ids[s], 1.0, 0.0).astype(F32) for s in range(2)]
    stats[...] = jnp.zeros((8, 128), F32)
    stats[0:1, :] = member[0] * valid[0] + member[1] * valid[1]
    stats[1:2, :] = member[0] * (valid[0] * rewards[0]) + member[1] * (valid[1] * rewards[1])
    stats[2:3, :] = member[0] * (valid[0] * (rewards[0] * rewards[0])) + member[1] * (
        valid[1] * (rewards[1] * rewards[1])
    )
    stats[3:4, :] = jnp.zeros((1, 128), F32) + (valid[0] + valid[1])

    stats_copies = stats_send(0)
    gather_on(hid, 0, rows0)
    near_on(1)
    rows1 = gather_own(hid, 1)
    stats_sum(0, stats_copies)
    far_own(0, 3)
    far_own(0, 2)
    far_on(0, 1)
    far_own(1, 2)
    far_on(0, 2)
    far_on(0, 0)
    far_on(0, 3)
    far_own(1, 0)
    far_own(1, 3)
    gather_on(hid, 1, rows1)
    stats_copies = stats_send(1)
    gather_near(hid, 0, rows0)
    gather_end(hid, 0, rows0)
    far_on(1, 2)
    far_own(1, 1)
    assemble(0, asm_up)
    gather_sib(rows0)
    forward(0, 0)
    gather_near(hid, 1, rows1)
    far_on(1, 0)
    forward(0, 1)
    gather_end(hid, 1, rows1)
    far_on(1, 3)
    far_on(1, 1)
    gather_sib(rows1)
    each(2, lambda i: forward(1, i))
    assemble(1, asm_down)
    stage[0] = 1
    stats_sum(1, stats_copies)
    stats_copies = stats_send(2)

    def pair_copy(s, n):
        i = s * 4 + n
        return pltpu.make_async_remote_copy(
            src_ref=asm_up.at[pl.ds(pl.multiple_of((s * 4 + n) * 320, CHUNK), 320)],
            dst_ref=sib_recv.at[s, n],
            send_sem=send_sem.at[N_SEND + i],
            recv_sem=recv_sem.at[N_RECV + i],
            device_id=sibling,
            device_id_type=MESH,
        )

    def branch_tile(s, i, n):
        cols = pl.ds(pl.multiple_of(jnp.minimum(n * SLICE, D - SLICE), 128), SLICE)
        value = lax.dot_general(act[s, i], asm_down[cols, :], LAST, preferred_element_type=F32)
        return cols, value

    def branch_half(s, half):
        def away(q):
            n = 2 * half + q
            value = branch_tile(s, 1, n)[1]
            asm_up[pl.ds(pl.multiple_of((s * 4 + n) * 320, CHUNK), 320), :] = value.astype(BF)
            pair_copy(s, n).start()

        def mine(q):
            n = 2 * half + q
            cols, value = branch_tile(s, 0, n)
            pair_copy(s, n).wait()
            value = value + sib_recv[s, n].astype(F32)
            own[s, :, cols] = value[0:80]
            for j, k in ((2, 0), (1, 1), (3, 2)):
                y_send[s, k, :, cols] = value[j * 80 : j * 80 + 80].astype(BF)

        each(2, away, unroll=2)
        each(2, mine, unroll=2)

    def ring_start(send, recv, parts, plus, minus):
        lo, hi = parts
        return {
            "across_hi": push(hi(send, 0), hi(recv, 0), plus),
            "across_lo": push(lo(send, 0), lo(recv, 0), minus),
            "plus_lo": push(lo(send, 1), lo(recv, 1), plus),
            "minus_hi": push(hi(send, 2), hi(recv, 2), minus),
        }

    def ring_add(send, recv, parts, plus, minus, add, d):
        lo, hi = parts
        d["across_hi"].wait_recv()
        add(hi(send, 1), hi(recv, 0))
        d["plus_hi"] = push(hi(send, 1), hi(recv, 1), plus)
        d["across_lo"].wait_recv()
        add(lo(send, 2), lo(recv, 0))
        d["minus_lo"] = push(lo(send, 2), lo(recv, 2), minus)

    def ring_wait(d):
        for part in ("plus_lo", "minus_hi", "plus_hi", "minus_lo"):
            d[part].wait_recv()

    def add_rows(dst, src):
        def body(i, carry):
            rows = pl.ds(pl.multiple_of(i * CHUNK, CHUNK), CHUNK)
            dst[rows, :] = (dst[rows, :].astype(F32) + src[rows, :].astype(F32)).astype(BF)
            return carry

        lax.fori_loop(0, dst.shape[0] // CHUNK, body, 0)

    def add_blocks(dst, src):
        for k in range(2):
            dst[k] = (dst[k].astype(F32) + src[k].astype(F32)).astype(BF)

    col_parts = tuple((lambda ref, k, cols=cols: ref.at[k, :, cols]) for cols in COLS)

    def branch_push(s, half, d):
        lo, hi = col_parts
        send, recv = y_send.at[s], y_recv.at[s]
        if half == 1:
            d["across_hi"] = push(hi(send, 0), hi(recv, 0), y_plus)
            d["minus_hi"] = push(hi(send, 2), hi(recv, 2), y_minus)
        else:
            d["across_lo"] = push(lo(send, 0), lo(recv, 0), y_minus)
            d["plus_lo"] = push(lo(send, 1), lo(recv, 1), y_plus)

    def branch_add(s, half, d):
        part = col_parts[half]
        send, recv = y_send.at[s], y_recv.at[s]
        key, k, to = (("lo", 2, y_minus), ("hi", 1, y_plus))[half]
        d["across_" + key].wait_recv()
        add_rows(part(send, k), part(recv, 0))
        d[("minus_lo", "plus_hi")[half]] = push(part(send, k), part(recv, k), to)

    def back_rows(s, d):
        ring_wait(d)
        gate = 1.0 + mod[2, s : s + 1, :]
        factor = step_ratio[s]

        def err_body(i, total):
            rows = pl.ds(pl.multiple_of(i * CHUNK, CHUNK), CHUNK)
            branch = (
                own[s, rows, :] + y_recv[s, 1, rows, :].astype(F32) + y_recv[s, 2, rows, :].astype(F32)
            )
            velocity = gate * branch
            drawn = noise[s, rows, :].astype(F32)
            err = drawn + factor * (stale[s, rows, :].astype(F32) - velocity)
            own[s, rows, :] = err
            gap = jnp.sum(drawn * drawn - err * err, axis=1, keepdims=True)
            return total + mask_col[s, rows, 0:1] * gap

        gaps = lax.fori_loop(0, PATCH // CHUNK, err_body, jnp.zeros((CHUNK, 1), F32))
        logratio = jnp.sum(gaps, axis=0, keepdims=True) / (2.0 * npatch[s])
        safe = jnp.maximum(stats[0:1, :], 1.0)
        middle = stats[1:2, :] / safe
        variance = jnp.maximum(stats[2:3, :] / safe - middle * middle, 0.0)
        spread = jnp.maximum(jnp.sqrt(variance), spread_floor)
        own_mean = jnp.sum(member[s] * middle, axis=1, keepdims=True)
        own_spread = jnp.sum(member[s] * spread, axis=1, keepdims=True)
        advantage = (rewards[s] - own_mean) / own_spread
        ratio = jnp.exp(logratio)
        clipped = jnp.clip(ratio, clip_low, clip_high)
        active = jnp.where(ratio * advantage <= clipped * advantage, 1.0, 0.0).astype(F32)
        coef = -valid[s] * advantage * ratio * active / jnp.maximum(stats[3:4, 0:1], 1.0)
        per_patch = coef / npatch[s]

        def back_body(i, carry):
            rows = pl.ds(pl.multiple_of(i * CHUNK, CHUNK), CHUNK)
            scale = per_patch * mask_col[s, rows, 0:1] * factor
            bk[s, 0, 0, rows, :] = (gate * (scale * own[s, rows, :])).astype(BF)
            return carry

        lax.fori_loop(0, PATCH // CHUNK, back_body, 0)

    ring0, ring1 = {}, {}
    branch_half(0, 1)
    branch_push(0, 1, ring0)
    branch_half(0, 0)
    branch_push(0, 0, ring0)
    stats_sum(2, stats_copies)
    stats_copies = stats_send(3)

    diag = lax.broadcasted_iota(jnp.int32, (PATCH, PATCH), 0) == lax.broadcasted_iota(
        jnp.int32, (PATCH, PATCH), 1
    )
    npatch = []
    for s in range(2):
        row = jnp.broadcast_to(mask_in[s : s + 1, :].astype(F32), (PATCH, PATCH))
        column = jnp.sum(jnp.where(diag, row, 0.0), axis=1, keepdims=True)
        mask_col[s] = jnp.broadcast_to(column, (PATCH, 128))
        npatch.append(jnp.maximum(jnp.sum(column, axis=0, keepdims=True), 1.0))

    branch_half(1, 1)
    branch_push(1, 1, ring1)
    branch_add(0, 1, ring0)
    branch_half(1, 0)
    branch_push(1, 0, ring1)
    branch_add(0, 0, ring0)
    stats_sum(3, stats_copies)
    stale_in.wait()
    noise_in.wait()
    branch_add(1, 1, ring1)
    branch_add(1, 0, ring1)
    back_rows(0, ring0)
    stage[0] = 2
    back0 = gather_own(bk, 0)
    back_rows(1, ring1)
    gather_on(bk, 0, back0)
    back1 = gather_own(bk, 1)
    gather_near(bk, 0, back0)
    gather_end(bk, 0, back0)
    gather_sib(back0)

    def back_pre(s):
        def body(i, carry):
            rows = bk[s, i].reshape(4 * PATCH, D)
            value = jnp.dot(rows, asm_down[...], preferred_element_type=F32)
            act[s, i] = (value * gelu_parts(pre[s, i])[1]).astype(BF)
            return carry

        lax.fori_loop(0, 2, body, 0)

    PARTS = ((1, 0, 256), (1, 256, 384), (0, 0, 256), (0, 256, 256), (0, 512, 128))
    DIRECT = (3, 4)

    def over_width(body):
        each(3, lambda n: body(pl.multiple_of(n * SLICE, 128), SLICE))
        body(3 * SLICE, D - 3 * SLICE)

    def grad_part(rows, s, at_, wide, start, width):
        left = rows[s, :, :, :, pl.ds(at_, wide)].reshape(8 * PATCH, wide)
        right = act[s, :, :, start : start + width].reshape(8 * PATCH, width)
        return lax.dot_general(left, right, FIRST, preferred_element_type=F32)

    def grad_rows(p, h, j, k):
        a, b = turn(far_at[h], j), turn(near_at[h], k)
        block = (b * 4 + a) if h == 0 else (a * 4 + b)
        rows = pl.ds(pl.multiple_of(block * BLOCK + 80 * h, 8), 80)
        return grad[rows, PARTS[p][1] : PARTS[p][1] + PARTS[p][2]]

    def block_parts(p):
        cols = pl.ds(PARTS[p][1], PARTS[p][2])
        return tuple((lambda ref, k, i=i: ref.at[k, pl.ds(i, 2), :, cols]) for i in (0, 2))

    def far_ring(p, h):
        m = PARTS[p][0]
        return raws[h].at[m], x_recv.at[m, h], block_parts(p), far[h][1], far[h][3]

    def far_start(p):
        m, start, width = PARTS[p]
        cols = slice(start, start + width)

        def away(k):
            for h in range(2):
                for j, slot in ((2, 0), (1, 1), (3, 2)):
                    raws[h][m, slot, k, :, cols] = grad_rows(p, h, j, k).astype(BF)

        def mine(k):
            for h in range(2):
                grad_own[m, h, k, :, cols] = grad_rows(p, h, 0, k)

        each(4, away)
        out = [ring_start(*far_ring(p, h)) for h in range(2)]
        each(4, mine)
        return out

    def far_add(p, d):
        for h in range(2):
            ring_add(*far_ring(p, h), add_blocks, d[h])

    def near_start(p, d):
        m, start, width = PARTS[p]
        cols = slice(start, start + width)
        out = []
        for h in range(2):
            ring_wait(d[h])

            def total(k):
                return (
                    grad_own[m, h, k, :, cols]
                    + x_recv[m, h, 1, k, :, cols].astype(F32)
                    + x_recv[m, h, 2, k, :, cols].astype(F32)
                )

            def away(k):
                b_send[m, h, k, :, cols] = total(k + 1).astype(BF)

            each(3, away)
            send, recv = b_send.at[m, h], b_recv.at[m, h]
            part = pl.ds(start, width)
            out += [
                push(send.at[k, :, part], recv.at[k, :, part], near[h][k + 1]) for k in (1, 0, 2)
            ]
            grad_own[m, h, 0, :, cols] = total(0)
        return out

    def out_cols(owner, start, width):
        return pl.ds(pl.multiple_of(owner * SLICE + start, 128), width)

    def update(p, d):
        m, start, width = PARTS[p]
        for copy in d:
            copy.wait_recv()

        def columns(n, h):
            cols = pl.ds(pl.multiple_of(start + n * 128, 128), 128)
            rows = slice(0, 80) if h == 0 else slice(80, BLOCK)
            high = 80 if h == 0 else 72
            grads = (
                grad_own[m, h, 0, 0:high, cols]
                + b_recv[m, h, 0, 0:high, cols].astype(F32)
                + b_recv[m, h, 1, 0:high, cols].astype(F32)
                + b_recv[m, h, 2, 0:high, cols].astype(F32)
            )
            weights = par[m, rows, cols]
            new_first = beta_one * m1[m, rows, cols] + (1.0 - beta_one) * grads
            new_second = beta_two * m2[m, rows, cols] + (1.0 - beta_two) * grads * grads
            first_hat = new_first / (1.0 - beta_one**adam_count)
            second_hat = new_second / (1.0 - beta_two**adam_count)
            step = first_hat / (jnp.sqrt(second_hat) + adam_eps) + weight_decay * weights
            new_weights = weights - learn_rate * step
            m1[m, rows, cols] = new_first
            m2[m, rows, cols] = new_second
            par[m, rows, cols] = new_weights
            land[m, 0, rows, cols] = new_weights.astype(BF)

        for h in range(2):
            each(width // 128, functools.partial(columns, h=h))
        mine = land.at[m, 0, :, pl.ds(start, width)]

        def slot(j):
            return land.at[m, j, :, pl.ds(start, width)]

        d = {"left": push(mine, slot(3), y_plus), "right": push(mine, slot(1), y_minus)}
        if p in DIRECT:
            d["across"] = push(mine, slot(2), y_ring[2])
        d["sib0"] = out_give(p, 0)
        for state, result in ((m1, o_m1), (m2, o_m2), (par, o_par)):
            part = pl.ds(start, width)
            move(state.at[m, :, part], result.at[m, :, part])
        return d

    def out_give(p, j):
        m, start, width = PARTS[p]
        block = land.at[m, j, :, pl.ds(start, width)]
        owner = turn(y, j) * 2
        place = o_roll.at[m, :, out_cols(owner + c, start, width)]
        copy = push(block, place, sibling, o_roll.at[m, :, out_cols(owner + 1 - c, start, width)])
        move(block, place)
        return copy

    def out_on(p, d):
        m, start, width = PARTS[p]
        half = 128 * ((width // 128 + 1) // 2)
        for key, j, to, at_, wide in (
            ("left", 3, y_plus, start, half),
            ("right", 1, y_minus, start + half, width - half),
        ):
            d[key].wait_recv()
            cols = pl.ds(at_, wide)
            if p not in DIRECT:
                d[key, "across"] = push(land.at[m, j, :, cols], land.at[m, 2, :, cols], to)
            d[key, "sib"] = out_give(p, j)

    def out_end(p, d):
        for key in (("across",) if p in DIRECT else (("left", "across"), ("right", "across"))):
            d[key].wait_recv()
        d["sib2"] = out_give(p, 2)

    def out_sib(d):
        for key in ("sib0", ("left", "sib"), ("right", "sib"), "sib2"):
            d[key].wait_recv()

    for copy in weights_sent:
        copy.wait()
    grad[pl.ds(D, 8), :] = jnp.zeros((8, SLICE), F32)

    def first_rows(at_, wide):
        grad[pl.ds(at_, wide), :] = grad_part(bk, 0, at_, wide, 0, SLICE)

    over_width(first_rows)
    gather_on(bk, 1, back1)
    back_pre(0)
    gather_near(bk, 1, back1)
    for j in (0, 1, 3):
        back1["sib%d" % j].wait_recv()

    def grad_blocks(at_, wide, blocks, start, width):
        left = bk[1, :, blocks, :, pl.ds(at_, wide)]
        n = left.shape[1] * PATCH
        first_row = blocks.start * PATCH
        right = act[1, :, first_row : first_row + n, start : start + width].reshape(2 * n, width)
        return lax.dot_general(
            left.reshape(2 * n, wide), right, FIRST, preferred_element_type=F32
        )

    def early_rows(at_, wide):
        grad[pl.ds(at_, wide), :] += grad_blocks(at_, wide, slice(0, 2), 0, SLICE) + grad_blocks(
            at_, wide, slice(3, 4), 0, SLICE
        )

    over_width(early_rows)
    gather_end(bk, 1, back1)
    back1["sib2"].wait_recv()

    def down_part(p):
        start, width = PARTS[p][1:]

        def body(at_, wide):
            cols = slice(start, start + width)
            grad[pl.ds(at_, wide), cols] += grad_blocks(at_, wide, slice(2, 3), start, width)

        over_width(body)

    def up_part(p):
        start, width = PARTS[p][1:]

        def body(at_, wide):
            grad[pl.ds(at_, wide), start : start + width] = grad_part(
                hid, 0, at_, wide, start, width
            ) + grad_part(hid, 1, at_, wide, start, width)

        over_width(body)

    down_part(0)
    far0 = far_start(0)
    down_part(1)
    far1 = far_start(1)
    back_pre(1)
    far_add(0, far0)
    up_part(2)
    far_add(1, far1)
    up_part(3)
    far2 = far_start(2)
    near1 = near_start(1, far1)
    far_add(2, far2)
    far3 = far_start(3)
    up_part(4)
    m1_in.wait()
    m2_in.wait()
    out1 = update(1, near1)
    near2 = near_start(2, far2)
    far_add(3, far3)
    near0 = near_start(0, far0)
    far4 = far_start(4)
    out_on(1, out1)
    out2 = update(2, near2)
    near3 = near_start(3, far3)
    far_add(4, far4)
    out0 = update(0, near0)
    out_on(2, out2)
    out_end(1, out1)
    out3 = update(3, near3)
    near4 = near_start(4, far4)
    out_on(0, out0)
    out4 = update(4, near4)
    out_on(3, out3)
    out_end(3, out3)
    out_on(4, out4)
    out_end(2, out2)
    out_end(0, out0)
    out_end(4, out4)
    for out in (out0, out1, out2, out3, out4):
        out_sib(out)
    assert fresh_id[0] <= N_RECV, fresh_id[0]
    for copy in moves + sends:
        copy.wait()


def settle(*refs):
    sources, targets, held, sem = refs[:4], refs[4:8], refs[8:12], refs[12]
    pieces = [(i, m) for i in (3, 0, 1, 2) for m in range(2)]
    reads, writes = [], []
    for n, (i, m) in enumerate(pieces):
        there, here = sources[i].at[m], held[i].at[m]
        reads.append(pltpu.make_async_copy(there, here, sem.at[n]))
        reads[-1].start()
    for n, (i, m) in enumerate(pieces):
        reads[n].wait()
        here, there = held[i].at[m], targets[i].at[m]
        writes.append(pltpu.make_async_copy(here, there, sem.at[len(pieces) + n]))
        writes[-1].start()
    for write in writes:
        write.wait()


def per_device(
    latents,
    stale_velocity,
    noise,
    modulation,
    step_ratio,
    rewards,
    group_ids,
    step_index,
    valid_steps,
    patch_mask,
    params,
    first_moment,
    second_moment,
):
    any_ = pl.BlockSpec(memory_space=pl.ANY)
    shard = jax.ShapeDtypeStruct(params.shape, F32)
    outs = pl.pallas_call(
        kernel,
        out_shape=(shard, shard, shard, jax.ShapeDtypeStruct((2, BLOCK, 8 * SLICE), BF)),
        in_specs=[any_] * 13,
        out_specs=(any_,) * 4,
        scratch_shapes=[
            pltpu.VMEM((2, 2, 4, PATCH, D), BF),
            pltpu.VMEM((2, 2, 4, PATCH, D), BF),
            pltpu.VMEM((2, 4, 4, 80, SLICE), BF),
            pltpu.VMEM((2, 4, 4, 80, SLICE), BF),
            pltpu.VMEM((2560, SLICE), BF),
            pltpu.VMEM((D, SLICE), BF),
            pltpu.VMEM((2, 2, 4 * PATCH, SLICE), F32),
            pltpu.VMEM((2, 2, 4 * PATCH, SLICE), BF),
            pltpu.VMEM((2, 4, 4 * PATCH, SLICE), BF),
            pltpu.VMEM((2, 3, PATCH, D), BF),
            pltpu.VMEM((2, 3, PATCH, D), BF),
            pltpu.VMEM((2, PATCH, D), F32),
            pltpu.VMEM((D + 8, SLICE), F32),
            pltpu.VMEM((2, 2, 3, 4, 80, SLICE), BF),
            pltpu.VMEM((2, 2, 4, 80, SLICE), F32),
            pltpu.VMEM((2, 2, 3, 80, SLICE), BF),
            pltpu.VMEM((2, 2, 3, 80, SLICE), BF),
            pltpu.VMEM((2, PATCH, D), BF),
            pltpu.VMEM((2, PATCH, D), BF),
            pltpu.VMEM((2, BLOCK, SLICE), F32),
            pltpu.VMEM((2, BLOCK, SLICE), F32),
            pltpu.VMEM((2, BLOCK, SLICE), F32),
            pltpu.VMEM((2, 4, BLOCK, SLICE), BF),
            pltpu.VMEM((2, PATCH, 128), F32),
            pltpu.VMEM((8, 128), F32),
            pltpu.VMEM((4, 4, 8, 128), F32),
            pltpu.SMEM((2,), F32),
            pltpu.SMEM((2,), jnp.int32),
            pltpu.SMEM((2,), jnp.int32),
            pltpu.SMEM((2,), jnp.int32),
            pltpu.SMEM((2,), F32),
            pltpu.VMEM((2, PATCH), jnp.int32),
            pltpu.VMEM((3, 2, D), F32),
            pltpu.SemaphoreType.DMA((N_SEND + N_PAIR,)),
            pltpu.SemaphoreType.DMA((N_RECV + N_PAIR,)),
            pltpu.SemaphoreType.DMA((N_LOCAL,)),
        ],
        compiler_params=pltpu.CompilerParams(
            collective_id=0, has_side_effects=True, vmem_limit_bytes=63 << 20
        ),
    )(
        rewards,
        group_ids,
        step_index,
        valid_steps,
        step_ratio,
        patch_mask,
        modulation.transpose(1, 0, 2),
        latents,
        stale_velocity,
        noise,
        params,
        first_moment,
        second_moment,
    )
    return tuple(
        pl.pallas_call(
            settle,
            out_shape=tuple(jax.ShapeDtypeStruct(o.shape, o.dtype) for o in outs),
            in_specs=[any_] * 4,
            out_specs=(any_,) * 4,
            scratch_shapes=[pltpu.VMEM(o.shape, o.dtype) for o in outs]
            + [pltpu.SemaphoreType.DMA((16,))],
        )(*outs)
    )


def solution(mesh):
    rows = ("roll", "fsdp")
    weights = P(None, "fsdp", "roll")
    return jax.shard_map(
        per_device,
        mesh=mesh,
        in_specs=(
            P(rows, None, None),
            P(rows, None, None),
            P(rows, None, None),
            P(rows, None, None),
            P(rows),
            P(rows),
            P(rows),
            P(rows),
            P(rows),
            P(rows, None),
            weights,
            weights,
            weights,
        ),
        out_specs=(weights, weights, weights, P(None, "fsdp", None)),
        check_vma=False,
    )
```
